32 devices in a mesh: seq: 16 (over z, y, x), head: 2 (over core).
Axes of the slice: x: 2, y: 2, z: 4, core: 2. Of those that a mesh axis runs over, the one named last changes fastest.
Arguments:
- queries: bfloat16 [4096, 384], P('seq', 'head'), may hold values from -15 to 15
- key_states: bfloat16 [4096, 384], P('seq', 'head'), may hold values from -15 to 15
- value_states: bfloat16 [4096, 384], P('seq', 'head'), may hold values from -6 to 6
- pool_weight: float32 [64], replicated, may hold values from -0.75 to 0.75
- out_grad: bfloat16 [4096, 384], P('seq', 'head'), may hold values from -12 to 12
Outputs:
- attended: bfloat16 [4096, 384], P('seq', 'head')
- query_grad: bfloat16 [4096, 384], P('seq', 'head')
- key_grad: bfloat16 [4096, 384], P('seq', 'head')
- value_grad: bfloat16 [4096, 384], P('seq', 'head')
- pool_grad: float32 [64], replicated
The draws below stay inside these ranges and needn't reach their ends.
All inputs are finite; a program needn't handle non-finite values.
Results may differ from the reference program's by a relative error of at most 0.0045.
The reference program's roundings to bfloat16 on the way count: a program that leaves them out, or rounds other values in their place, can miss the bound.
Values may be sent and summed in bfloat16 or wider, within the bound.
No kernel may reach another device: no remote copies, remote signals or barrier semaphores. Data moves between devices by JAX's collectives and lax.ppermute only.
A program may use at most 64 MiB of HBM per device.

```python
import jax
import jax.numpy as jnp
from jax import lax

HEADS = 6
HEAD_DIM = 64
WIDTH = 384
BLOCK = 64
SEG_LEN = 64
TOKENS = 4096


def shared_pair(key):
    base = jax.random.fold_in(key, 11)
    first_key, second_key = jax.random.split(base, 2)
    query_draw = jnp.clip(jax.random.normal(first_key, (TOKENS, WIDTH), jnp.float32), -4.5, 4.5)
    key_draw = jnp.clip(jax.random.normal(second_key, (TOKENS, WIDTH), jnp.float32), -4.5, 4.5)
    return (query_draw, key_draw)


def draw_queries(key, part):
    return shared_pair(key)[0].astype(jnp.bfloat16)


def draw_key_states(key, part):
    return shared_pair(key)[1].astype(jnp.bfloat16)


def draw_out_grad(key, part):
    base = jax.random.fold_in(key, 29)
    ramp = jnp.arange(TOKENS).astype(jnp.float32) / max(TOKENS - 1, 1)
    noise = jnp.clip(jax.random.normal(base, (TOKENS, WIDTH), jnp.float32), -4.0, 4.0)
    scaled = noise * (1.0 + 2.0 * ramp)[:, None]
    return scaled.astype(jnp.bfloat16)


def steps_of(own_key, extent, cuts, least, largest):
    loudness, own = 1.0, jax.random.fold_in(own_key, 6)
    for position, shards_of in cuts:
        steps = jnp.exp(jax.random.uniform(jax.random.fold_in(own, position), (shards_of,), jnp.float32, least / len(cuts), largest / len(cuts)))
        loudness = loudness * jnp.repeat(steps, extent[position] // shards_of).reshape([-1 if axis == position else 1 for axis in range(len(extent))])
    return loudness


def normal_values(rng, shape, scale, reach, cuts=(), held_as=jnp.bfloat16):
    level = steps_of(rng, shape, cuts, -0.22, 0.18) if cuts else 1.0
    entries = jax.random.normal(rng, shape, jnp.float32) * scale * level
    return jnp.minimum(jnp.maximum(entries, -reach), reach).astype(held_as)


def setup_inputs(seed: int = 0) -> dict:
    key_of = jax.random.split(jax.random.key(seed), 6)
    queries = draw_queries(jax.random.fold_in(key_of[5], 71), 0)
    key_states = draw_key_states(jax.random.fold_in(key_of[5], 71), 0)
    value_states = normal_values(key_of[2], (TOKENS, WIDTH), 1.0, 6.0, ((0, 16), (1, 2)))
    pool_weight = normal_values(key_of[3], (SEG_LEN,), SEG_LEN ** -0.5, 0.75, (), jnp.float32)
    out_grad = draw_out_grad(jax.random.fold_in(key_of[5], 71), 0)
    return dict(queries=queries, key_states=key_states, value_states=value_states, pool_weight=pool_weight, out_grad=out_grad)


def make_windows(padded, block_count):
    span = block_count * BLOCK
    return jnp.concatenate([padded[0:span].reshape(block_count, BLOCK, -1), padded[BLOCK:span + BLOCK].reshape(block_count, BLOCK, -1), padded[2 * BLOCK:span + 2 * BLOCK].reshape(block_count, BLOCK, -1)], axis=1)


def undo_windows(window, block_count):
    span = block_count * BLOCK
    first_part = jnp.pad(window[:, :BLOCK].reshape(span, -1), ((0, 2 * BLOCK), (0, 0)))
    middle_part = jnp.pad(window[:, BLOCK:2 * BLOCK].reshape(span, -1), ((BLOCK, BLOCK), (0, 0)))
    last_part = jnp.pad(window[:, 2 * BLOCK:].reshape(span, -1), ((2 * BLOCK, 0), (0, 0)))
    return first_part + middle_part + last_part


def head_pass(query_head, key_ext, value_ext, global_key, global_value, grad_head, mask_first, mask_last):
    scale = HEAD_DIM ** -0.5
    tok_rows = query_head.shape[0]
    block_count = tok_rows // BLOCK
    key_windows = make_windows(key_ext, block_count).astype(jnp.float32)
    value_windows = make_windows(value_ext, block_count).astype(jnp.float32)
    query_blocks = query_head.reshape(block_count, BLOCK, -1).astype(jnp.float32)
    grad_blocks = grad_head.reshape(block_count, BLOCK, -1).astype(jnp.float32)
    local_scores = jnp.einsum('nbd,nkd->nbk', query_blocks, key_windows) * scale
    global_scores = jnp.dot(query_head, global_key.T, preferred_element_type=jnp.float32) * scale
    block_ids = jnp.arange(block_count)[:, None, None]
    key_ids = jnp.arange(3 * BLOCK)[None, None, :]
    invalid = jnp.logical_or(jnp.logical_and(mask_first, jnp.logical_and(block_ids == 0, key_ids < BLOCK)), jnp.logical_and(mask_last, jnp.logical_and(block_ids == block_count - 1, key_ids >= 2 * BLOCK)))
    local_scores = jnp.where(invalid, -jnp.inf, local_scores)
    row_max = jnp.maximum(local_scores.max(-1).reshape(tok_rows), global_scores.max(-1))
    local_exp = jnp.exp(local_scores - row_max.reshape(block_count, BLOCK, 1))
    global_exp = jnp.exp(global_scores - row_max[:, None])
    totals = local_exp.sum(-1).reshape(tok_rows) + global_exp.sum(-1)
    local_weights = local_exp / totals.reshape(block_count, BLOCK, 1)
    global_weights = global_exp / totals[:, None]
    local_probs = lax.optimization_barrier(local_weights.astype(jnp.bfloat16))
    global_probs = lax.optimization_barrier(global_weights.astype(jnp.bfloat16))
    mixed = jnp.einsum('nbk,nkd->nbd', local_probs.astype(jnp.float32), value_windows).reshape(tok_rows, -1)
    mixed = mixed + jnp.dot(global_probs, global_value, preferred_element_type=jnp.float32)
    attended = lax.optimization_barrier(mixed.astype(jnp.bfloat16))
    delta = jnp.sum(grad_head.astype(jnp.float32) * attended.astype(jnp.float32), axis=-1)
    local_dprob = jnp.einsum('nbd,nkd->nbk', grad_blocks, value_windows)
    global_dprob = jnp.dot(grad_head, global_value.T, preferred_element_type=jnp.float32)
    local_dscore = lax.optimization_barrier((local_weights * (local_dprob - delta.reshape(block_count, BLOCK, 1)) * scale).astype(jnp.bfloat16))
    global_dscore = lax.optimization_barrier((global_weights * (global_dprob - delta[:, None]) * scale).astype(jnp.bfloat16))
    query_grad = jnp.einsum('nbk,nkd->nbd', local_dscore.astype(jnp.float32), key_windows).reshape(tok_rows, -1)
    query_grad = (query_grad + jnp.dot(global_dscore, global_key, preferred_element_type=jnp.float32)).astype(jnp.bfloat16)
    key_window_grad = jnp.einsum('nbk,nbd->nkd', local_dscore.astype(jnp.float32), query_blocks)
    value_window_grad = jnp.einsum('nbk,nbd->nkd', local_probs.astype(jnp.float32), grad_blocks)
    global_key_grad = jnp.dot(global_dscore.T, query_head, preferred_element_type=jnp.float32)
    global_value_grad = jnp.dot(global_probs.T, grad_head, preferred_element_type=jnp.float32)
    return attended, query_grad, undo_windows(key_window_grad, block_count), undo_windows(value_window_grad, block_count), global_key_grad, global_value_grad


def reference(queries, key_states, value_states, pool_weight, out_grad):
    total_rows = queries.shape[0]
    head_count = HEADS
    global_rows = total_rows // SEG_LEN
    key_segments = key_states.reshape(global_rows, SEG_LEN, -1).astype(jnp.float32)
    value_segments = value_states.reshape(global_rows, SEG_LEN, -1).astype(jnp.float32)
    global_key = jnp.einsum('gpc,p->gc', key_segments, pool_weight, precision=lax.Precision.HIGHEST).astype(jnp.bfloat16)
    global_value = jnp.einsum('gpc,p->gc', value_segments, pool_weight, precision=lax.Precision.HIGHEST).astype(jnp.bfloat16)

    def split_heads(array):
        return jnp.moveaxis(array.reshape(array.shape[0], head_count, HEAD_DIM), 1, 0)

    def merge_heads(array):
        return jnp.moveaxis(array, 0, 1).reshape(array.shape[1], head_count * HEAD_DIM)

    padding = ((BLOCK, BLOCK), (0, 0))
    key_ext = jnp.pad(key_states, padding)
    value_ext = jnp.pad(value_states, padding)

    def one_head(items):
        return head_pass(items[0], items[1], items[2], items[3], items[4], items[5], True, True)

    results = lax.map(one_head, (split_heads(queries), split_heads(key_ext), split_heads(value_ext), split_heads(global_key), split_heads(global_value), split_heads(out_grad)))
    attended = merge_heads(results[0])
    query_grad = merge_heads(results[1])
    key_local = merge_heads(results[2])[BLOCK:total_rows + BLOCK]
    value_local = merge_heads(results[3])[BLOCK:total_rows + BLOCK]
    global_key_grad = merge_heads(results[4])
    global_value_grad = merge_heads(results[5])
    key_pooled = (global_key_grad[:, None, :] * pool_weight[None, :, None]).reshape(total_rows, -1)
    value_pooled = (global_value_grad[:, None, :] * pool_weight[None, :, None]).reshape(total_rows, -1)
    key_grad = (key_local + key_pooled).astype(jnp.bfloat16)
    value_grad = (value_local + value_pooled).astype(jnp.bfloat16)
    pool_grad = jnp.einsum('gc,gpc->p', global_key_grad, key_segments, precision=lax.Precision.HIGHEST) + jnp.einsum('gc,gpc->p', global_value_grad, value_segments, precision=lax.Precision.HIGHEST)
    return attended, query_grad, key_grad, value_grad, pool_grad
```

```python
import jax
import jax.numpy as jnp
from jax import lax
from jax.sharding import PartitionSpec as P

HEAD_DIM = 64
BLOCK = 64
SUM_DEV = 4


def exchanged(x, axes):
    return lax.all_to_all(x, axes, split_axis=0, concat_axis=0)


def to_all(x, axes):
    return exchanged(jnp.broadcast_to(x[None], (lax.axis_size(axes),) + x.shape), axes)


def extended(x, sides, width):
    for axis, dim in sides:
        devices, length = (lax.axis_size(axis), x.shape[dim])
        up = [(i, (i + 1) % devices) for i in range(devices - 1)]
        down = [(j, i) for i, j in up]
        last = lax.slice_in_dim(x, length - width, length, axis=dim)
        leading = lax.slice_in_dim(x, 0, width, axis=dim)
        before = lax.ppermute(last, axis, up)
        after = lax.ppermute(leading, axis, down)
        x = jnp.concatenate([before, x, after], axis=dim)
    return x


def make_windows(padded, block_count):
    span = block_count * BLOCK
    return jnp.concatenate(
        [
            padded[0:span].reshape(block_count, BLOCK, -1),
            padded[BLOCK : span + BLOCK].reshape(block_count, BLOCK, -1),
            padded[2 * BLOCK : span + 2 * BLOCK].reshape(block_count, BLOCK, -1),
        ],
        axis=1,
    )


def undo_windows(window, block_count):
    span = block_count * BLOCK
    first_part = jnp.pad(window[:, :BLOCK].reshape(span, -1), ((0, 2 * BLOCK), (0, 0)))
    middle_part = jnp.pad(window[:, BLOCK : 2 * BLOCK].reshape(span, -1), ((BLOCK, BLOCK), (0, 0)))
    last_part = jnp.pad(window[:, 2 * BLOCK :].reshape(span, -1), ((2 * BLOCK, 0), (0, 0)))
    return first_part + middle_part + last_part


def head_pass(
    query_head, key_ext, value_ext, global_key, global_value, grad_head, mask_first, mask_last
):
    scale = HEAD_DIM ** (-0.5)
    tok_rows = query_head.shape[0]
    block_count = tok_rows // BLOCK
    key_windows = make_windows(key_ext, block_count)
    value_windows = make_windows(value_ext, block_count)
    query_blocks = query_head.reshape(block_count, BLOCK, -1)
    grad_blocks = grad_head.reshape(block_count, BLOCK, -1)
    local_scores = (
        jnp.einsum("nbd,nkd->nbk", query_blocks, key_windows, preferred_element_type=jnp.float32)
        * scale
    )
    global_scores = (
        jnp.einsum("td,gd->tg", query_head, global_key, preferred_element_type=jnp.float32) * scale
    )
    block_ids = jnp.arange(block_count)[:, None, None]
    key_ids = jnp.arange(3 * BLOCK)[None, None, :]
    invalid = jnp.logical_or(
        jnp.logical_and(mask_first, jnp.logical_and(block_ids == 0, key_ids < BLOCK)),
        jnp.logical_and(
            mask_last, jnp.logical_and(block_ids == block_count - 1, key_ids >= 2 * BLOCK)
        ),
    )
    local_scores = jnp.where(invalid, -jnp.inf, local_scores)
    row_max = jnp.maximum(local_scores.max(-1).reshape(tok_rows), global_scores.max(-1))
    local_exp = jnp.exp(local_scores - row_max.reshape(block_count, BLOCK, 1))
    global_exp = jnp.exp(global_scores - row_max[:, None])
    totals = local_exp.sum(-1).reshape(tok_rows) + global_exp.sum(-1)
    local_weights = local_exp / totals.reshape(block_count, BLOCK, 1)
    global_weights = global_exp / totals[:, None]
    local_probs = local_weights.astype(jnp.bfloat16)
    global_probs = global_weights.astype(jnp.bfloat16)
    mixed = jnp.einsum(
        "nbk,nkd->nbd", local_probs, value_windows, preferred_element_type=jnp.float32
    ).reshape(tok_rows, -1)
    mixed = mixed + jnp.dot(global_probs, global_value, preferred_element_type=jnp.float32)
    attended = lax.optimization_barrier(mixed.astype(jnp.bfloat16))
    delta = jnp.sum(grad_head.astype(jnp.float32) * attended.astype(jnp.float32), axis=-1)
    local_dprob = jnp.einsum(
        "nbd,nkd->nbk", grad_blocks, value_windows, preferred_element_type=jnp.float32
    )
    global_dprob = jnp.einsum(
        "td,gd->tg", grad_head, global_value, preferred_element_type=jnp.float32
    )
    local_dscore = (
        local_weights * (local_dprob - delta.reshape(block_count, BLOCK, 1)) * scale
    ).astype(jnp.bfloat16)
    global_dscore = (global_weights * (global_dprob - delta[:, None]) * scale).astype(jnp.bfloat16)
    query_grad = jnp.einsum(
        "nbk,nkd->nbd", local_dscore, key_windows, preferred_element_type=jnp.float32
    ).reshape(tok_rows, -1)
    query_grad = (
        query_grad + jnp.dot(global_dscore, global_key, preferred_element_type=jnp.float32)
    ).astype(jnp.bfloat16)
    key_window_grad = jnp.einsum(
        "nbk,nbd->nkd", local_dscore, query_blocks, preferred_element_type=jnp.float32
    )
    value_window_grad = jnp.einsum(
        "nbk,nbd->nkd", local_probs, grad_blocks, preferred_element_type=jnp.float32
    )
    global_key_grad = jnp.einsum(
        "tg,td->gd", global_dscore, query_head, preferred_element_type=jnp.float32
    )
    global_value_grad = jnp.einsum(
        "tg,td->gd", global_probs, grad_head, preferred_element_type=jnp.float32
    )
    return (
        attended,
        query_grad,
        undo_windows(key_window_grad, block_count),
        undo_windows(value_window_grad, block_count),
        global_key_grad,
        global_value_grad,
    )


def merge_heads(array):
    return jnp.transpose(array, (1, 0, 2)).reshape(array.shape[1], array.shape[0] * array.shape[2])


def local(queries, key_states, value_states, pool_weight, out_grad):
    tok_rows, local_width = queries.shape
    head_local = local_width // HEAD_DIM
    seg_rows = pool_weight.shape[0]
    group_index = lax.axis_index("seq")
    group_total = lax.axis_size("seq")
    key_segments = key_states.reshape(SUM_DEV, seg_rows, local_width).astype(jnp.float32)
    value_segments = value_states.reshape(SUM_DEV, seg_rows, local_width).astype(jnp.float32)
    pooled_key = jnp.einsum("spc,p->sc", key_segments, pool_weight, precision=lax.Precision.HIGHEST)
    pooled_value = jnp.einsum(
        "spc,p->sc", value_segments, pool_weight, precision=lax.Precision.HIGHEST
    )
    summary = jnp.concatenate([pooled_key, pooled_value], axis=1).astype(jnp.bfloat16)
    global_rows = to_all(summary, "seq").reshape(group_total * SUM_DEV, 2 * local_width)
    joined = jnp.concatenate([key_states, value_states], axis=1)
    joined_ext = extended(joined, (("seq", 0),), BLOCK)
    mask_first = group_index == 0
    mask_last = group_index == group_total - 1

    def one_head(head_index):
        start = head_index * HEAD_DIM
        query_head = lax.dynamic_slice_in_dim(queries, start, HEAD_DIM, 1)
        key_ext = lax.dynamic_slice_in_dim(joined_ext, start, HEAD_DIM, 1)
        value_ext = lax.dynamic_slice_in_dim(joined_ext, local_width + start, HEAD_DIM, 1)
        global_key = lax.dynamic_slice_in_dim(global_rows, start, HEAD_DIM, 1)
        global_value = lax.dynamic_slice_in_dim(global_rows, local_width + start, HEAD_DIM, 1)
        grad_head = lax.dynamic_slice_in_dim(out_grad, start, HEAD_DIM, 1)
        return head_pass(
            query_head,
            key_ext,
            value_ext,
            global_key,
            global_value,
            grad_head,
            mask_first,
            mask_last,
        )

    results = lax.map(one_head, jnp.arange(head_local))
    attended = merge_heads(results[0])
    query_grad = merge_heads(results[1])
    joined_grad = jnp.concatenate([merge_heads(results[2]), merge_heads(results[3])], axis=1)
    global_part = jnp.concatenate([merge_heads(results[4]), merge_heads(results[5])], axis=1)
    edges = jnp.concatenate([joined_grad[:BLOCK], joined_grad[tok_rows + BLOCK :]], axis=0)
    returned = extended(edges.astype(jnp.bfloat16), (("seq", 0),), BLOCK).astype(edges.dtype)
    local_grad = joined_grad[BLOCK : tok_rows + BLOCK]
    local_grad = local_grad + jnp.pad(returned[:BLOCK], ((0, tok_rows - BLOCK), (0, 0)))
    local_grad = local_grad + jnp.pad(returned[3 * BLOCK :], ((tok_rows - BLOCK, 0), (0, 0)))
    owned = exchanged(global_part.reshape(group_total, SUM_DEV, 2 * local_width), "seq").sum(0)
    owned_key = owned[:, :local_width]
    owned_value = owned[:, local_width:]
    key_pooled = (owned_key[:, None, :] * pool_weight[None, :, None]).reshape(tok_rows, local_width)
    value_pooled = (owned_value[:, None, :] * pool_weight[None, :, None]).reshape(
        tok_rows, local_width
    )
    key_grad = (local_grad[:, :local_width] + key_pooled).astype(jnp.bfloat16)
    value_grad = (local_grad[:, local_width:] + value_pooled).astype(jnp.bfloat16)
    pool_term = jnp.einsum(
        "sc,spc->p", owned_key, key_segments, precision=lax.Precision.HIGHEST
    ) + jnp.einsum("sc,spc->p", owned_value, value_segments, precision=lax.Precision.HIGHEST)
    pool_grad = to_all(pool_term, ("seq", "head")).sum(0)
    return (attended, query_grad, key_grad, value_grad, pool_grad)


def solution(mesh):
    return jax.shard_map(
        local,
        mesh=mesh,
        in_specs=(P("seq", "head"), P("seq", "head"), P("seq", "head"), P(), P("seq", "head")),
        out_specs=(P("seq", "head"), P("seq", "head"), P("seq", "head"), P("seq", "head"), P()),
        check_vma=False,
    )
```

```python
import functools

import jax
import jax.numpy as jnp
from jax import lax
from jax.experimental import pallas as pl
from jax.experimental.pallas import tpu as pltpu
from jax.sharding import PartitionSpec as P

HEAD_DIM = 64
BLOCK = 64
SUM_DEV = 4
PAIR = 2 * BLOCK
SCALE = HEAD_DIM ** (-0.5)
LOW = -1e30
VMEM = pl.BlockSpec(memory_space=pltpu.VMEM)
SMEM = pl.BlockSpec(memory_space=pltpu.SMEM)
PARAMS = pltpu.CompilerParams(vmem_limit_bytes=40 * 1024 * 1024)
F32 = jnp.float32
BF16 = jnp.bfloat16


def mm(a, b):
    return lax.dot_general(a, b, (((1,), (0,)), ((), ())), preferred_element_type=F32)


def mm_nt(a, b):
    return lax.dot_general(a, b, (((1,), (1,)), ((), ())), preferred_element_type=F32)


def mm_tn(a, b):
    return lax.dot_general(a, b, (((0,), (0,)), ((), ())), preferred_element_type=F32)


def pieces(x):
    high = x.astype(BF16)
    rest = x - high.astype(F32)
    middle = rest.astype(BF16)
    low = (rest - middle.astype(F32)).astype(BF16)
    return jnp.concatenate([high, middle, low], axis=0)


def segment_mask(first, rows, lanes, seg):
    row = lax.broadcasted_iota(jnp.int32, (rows, lanes), 0)
    lane = lax.broadcasted_iota(jnp.int32, (rows, lanes), 1)
    return row - first == lane // seg


def pool_kernel(q_ref, k_ref, v_ref, g_ref, w_ref, rows_ref, up_ref, down_ref):
    seg = w_ref.shape[1]
    w = jnp.concatenate([w_ref[...]] * SUM_DEV, axis=1)
    w = jnp.broadcast_to(w, (2 * SUM_DEV, w.shape[1]))
    pooled = jnp.zeros((2 * SUM_DEV, k_ref.shape[1]), F32)
    for first, ref in ((0, k_ref), (SUM_DEV, v_ref)):
        weights = jnp.where(segment_mask(first, w.shape[0], w.shape[1], seg), w, 0.0)
        parts = mm(pieces(weights), ref[...])
        n = 2 * SUM_DEV
        pooled += parts[:n] + parts[n : 2 * n] + parts[2 * n :]
    rows_ref[...] = jnp.broadcast_to(pooled.astype(BF16)[None], rows_ref.shape)
    tok = k_ref.shape[0]
    at = 0
    for ref, width in ((k_ref, PAIR), (v_ref, PAIR), (q_ref, BLOCK), (g_ref, BLOCK)):
        up_ref[at : at + width] = ref[tok - width :]
        down_ref[at : at + width] = ref[:width]
        at += width


def head_rows(x):
    feature = lax.broadcasted_iota(jnp.int32, (1, x.shape[1]), 1) // HEAD_DIM
    return jnp.concatenate(
        [x * jnp.where(feature == h, SCALE, 0.0).astype(BF16) for h in range(x.shape[1] // HEAD_DIM)],
        axis=0,
    )


def own_head(x):
    return jnp.concatenate(
        [
            x[h * HEAD_DIM : (h + 1) * HEAD_DIM, h * PAIR : (h + 1) * PAIR]
            for h in range(x.shape[0] // HEAD_DIM)
        ],
        axis=0,
    )


def head_sums(x):
    return jnp.concatenate(
        [
            jnp.sum(x[h * HEAD_DIM : (h + 1) * HEAD_DIM], axis=0, keepdims=True)
            for h in range(x.shape[0] // HEAD_DIM)
        ],
        axis=1,
    )


def softmax(local, glob):
    top = jnp.maximum(
        jnp.max(local, axis=0, keepdims=True), jnp.max(glob, axis=0, keepdims=True)
    )
    local = jnp.exp(local - top)
    glob = jnp.exp(glob - top)
    total = jnp.sum(local, axis=0, keepdims=True) + jnp.sum(glob, axis=0, keepdims=True)
    inverse = 1.0 / total
    return local * inverse, glob * inverse


def attention_kernel(
    edge_ref, q_ref, k_ref, v_ref, g_ref, before_ref, after_ref, rows_ref,
    att_ref, qg_ref, kg_ref, vg_ref, part_ref, kx, vx,
):
    tok, width = q_ref.shape
    heads = width // HEAD_DIM
    lanes = heads * PAIR
    is_first, is_last = edge_ref[0] == 1, edge_ref[1] == 1
    kx[:PAIR] = before_ref[:PAIR]
    vx[:PAIR] = before_ref[PAIR : 2 * PAIR]
    kx[PAIR : PAIR + tok] = k_ref[...]
    vx[PAIR : PAIR + tok] = v_ref[...]
    kx[PAIR + tok :] = after_ref[:PAIR]
    vx[PAIR + tok :] = after_ref[PAIR : 2 * PAIR]
    global_rows = rows_ref[...]
    count = global_rows.shape[0]
    second = lax.broadcasted_iota(jnp.int32, (1, lanes), 1) % PAIR >= BLOCK
    is_key = lax.broadcasted_iota(jnp.int32, (count, lanes), 0) % (2 * SUM_DEV) < SUM_DEV
    global_values = pltpu.roll(global_rows.astype(F32), count - SUM_DEV, 0).astype(BF16)

    kg = jnp.zeros((tok + PAIR, width), F32)
    vg = jnp.zeros((tok + PAIR, width), F32)
    part = jnp.zeros((count, width), F32)
    kg_rows = [jnp.zeros((BLOCK, width), F32) for _ in range(tok // BLOCK + 2)]
    vg_rows = [jnp.zeros((BLOCK, width), F32) for _ in range(tok // BLOCK + 2)]
    pairs = tok // PAIR
    for p in range(pairs):
        q = q_ref[p * PAIR : (p + 1) * PAIR]
        g = g_ref[p * PAIR : (p + 1) * PAIR]
        qm, gm = head_rows(q), head_rows(g)
        start = BLOCK + p * PAIR
        keys, values = kx[start : start + 2 * PAIR], vx[start : start + 2 * PAIR]
        s = mm_nt(keys, qm)
        hide_low = second
        hide_high = jnp.logical_not(second)
        if p == 0:
            hide_low = jnp.logical_or(hide_low, is_first)
        if p == pairs - 1:
            hide_high = jnp.logical_or(hide_high, is_last)
        s = jnp.concatenate(
            [
                s[:BLOCK] + jnp.where(hide_low, LOW, 0.0),
                s[BLOCK : 3 * BLOCK],
                s[3 * BLOCK :] + jnp.where(hide_high, LOW, 0.0),
            ],
            axis=0,
        )
        sg = jnp.where(is_key, mm_nt(global_rows, qm), LOW)
        w, wg = softmax(s, sg)
        pr, prg = w.astype(BF16), wg.astype(BF16)
        att = own_head(mm_tn(values, pr) + mm_tn(global_values, prg)).astype(BF16).astype(F32)
        att_ref[p * PAIR : (p + 1) * PAIR] = att.T.astype(BF16)
        delta = head_sums(g.astype(F32).T * att) * SCALE
        ds = (w * (mm_nt(values, gm) - delta)).astype(BF16)
        dsg = (wg * (mm_nt(global_values, gm) - delta)).astype(BF16)
        qg = own_head(mm_tn(keys, ds) + mm_tn(global_rows, dsg))
        qg_ref[p * PAIR : (p + 1) * PAIR] = qg.T.astype(BF16)
        kgp = mm(ds, qm)
        vgp = mm(pr, gm)
        for b in range(4):
            kg_rows[2 * p + b] += kgp[b * BLOCK : (b + 1) * BLOCK]
            vg_rows[2 * p + b] += vgp[b * BLOCK : (b + 1) * BLOCK]
        shifted = pltpu.roll(wg, SUM_DEV, 0).astype(BF16)
        part += mm(dsg, qm) + mm(shifted, gm)
    part_ref[...] = part * (1.0 / SCALE)

    q = jnp.concatenate([before_ref[2 * PAIR : 2 * PAIR + BLOCK], after_ref[2 * PAIR : 2 * PAIR + BLOCK]], axis=0)
    g = jnp.concatenate([before_ref[2 * PAIR + BLOCK :], after_ref[2 * PAIR + BLOCK :]], axis=0)
    qm, gm = head_rows(q), head_rows(g)
    low, high = slice(0, 3 * BLOCK), slice(tok + BLOCK, tok + 4 * BLOCK)
    s = jnp.where(second, mm_nt(kx[high], qm), mm_nt(kx[low], qm))
    sg = jnp.where(is_key, mm_nt(global_rows, qm), LOW)
    w, wg = softmax(s, sg)
    pr, prg = w.astype(BF16), wg.astype(BF16)
    att = jnp.where(second, mm_tn(vx[high], pr), mm_tn(vx[low], pr)) + mm_tn(global_values, prg)
    att = own_head(att).astype(BF16).astype(F32)
    delta = head_sums(g.astype(F32).T * att) * SCALE
    near_low, near_high = slice(PAIR, PAIR + BLOCK), slice(tok + BLOCK, tok + PAIR)
    dp = jnp.where(second, mm_nt(vx[near_high], gm), mm_nt(vx[near_low], gm))
    w = jnp.where(second, w[:BLOCK], w[2 * BLOCK :])
    ds = w * (dp - delta)
    ds = jnp.concatenate([jnp.where(second, 0.0, ds), jnp.where(second, ds, 0.0)], axis=0).astype(BF16)
    pr = jnp.concatenate([jnp.where(second, 0.0, w), jnp.where(second, w, 0.0)], axis=0).astype(BF16)
    kgp, vgp = mm(ds, qm), mm(pr, gm)
    kg_rows[1] += kgp[:BLOCK]
    vg_rows[1] += vgp[:BLOCK]
    kg_rows[-2] += kgp[BLOCK:]
    vg_rows[-2] += vgp[BLOCK:]
    kg_ref[...] = jnp.concatenate(kg_rows[1:-1], axis=0) * (1.0 / SCALE)
    vg_ref[...] = jnp.concatenate(vg_rows[1:-1], axis=0) * (1.0 / SCALE)


def owned_kernel(parts_ref, k_ref, v_ref, owned_ref, term_ref):
    owned = jnp.sum(parts_ref[...], axis=0)
    owned_ref[...] = owned
    split = pieces(owned)
    n = 2 * SUM_DEV
    seg = k_ref.shape[0] // SUM_DEV
    total = jnp.zeros((1, k_ref.shape[0]), F32)
    for first, ref in ((0, k_ref), (SUM_DEV, v_ref)):
        met = mm_nt(split, ref[...])
        met = met[:n] + met[n : 2 * n] + met[2 * n :]
        met = jnp.where(segment_mask(first, met.shape[0], met.shape[1], seg), met, 0.0)
        total += jnp.sum(met, axis=0, keepdims=True)
    term = total[:, :seg]
    for j in range(1, SUM_DEV):
        term += total[:, j * seg : (j + 1) * seg]
    term_ref[...] = jnp.broadcast_to(term, term_ref.shape)


def finish_kernel(owned_ref, kg_ref, vg_ref, w_ref, key_ref, value_ref):
    seg = w_ref.shape[1]
    same = lax.broadcasted_iota(jnp.int32, (seg, seg), 0) == lax.broadcasted_iota(
        jnp.int32, (seg, seg), 1
    )
    column = jnp.sum(jnp.where(same, w_ref[...], 0.0), axis=1, keepdims=True)
    for j in range(SUM_DEV):
        rows = slice(j * seg, (j + 1) * seg)
        key_ref[rows] = (kg_ref[rows] + column * owned_ref[j : j + 1]).astype(BF16)
        value_ref[rows] = (
            vg_ref[rows] + column * owned_ref[SUM_DEV + j : SUM_DEV + j + 1]
        ).astype(BF16)


def shaped(shape, dtype):
    return jax.ShapeDtypeStruct(shape, dtype)


def call(kernel, outs, count, scratch=(), first=VMEM):
    return pl.pallas_call(
        kernel,
        out_shape=outs,
        in_specs=[first] + [VMEM] * (count - 1),
        out_specs=[VMEM] * len(outs),
        scratch_shapes=list(scratch),
        compiler_params=PARAMS,
    )


def local(queries, key_states, value_states, pool_weight, out_grad):
    tok, width = queries.shape
    group_index = lax.axis_index("seq")
    groups = lax.axis_size("seq")
    everyone = groups * lax.axis_size("head")
    n = 2 * SUM_DEV
    seg = pool_weight.shape[0]
    weight_row = pool_weight.reshape(1, seg)
    halo = shaped((3 * PAIR, width), BF16)
    own = shaped((tok, width), BF16)
    grad = shaped((tok, width), F32)

    summary, up, down = call(pool_kernel, [shaped((groups, n, width), BF16), halo, halo], 5)(
        queries, key_states, value_states, out_grad, weight_row
    )
    forward = [(i, i + 1) for i in range(groups - 1)]
    backward = [(i + 1, i) for i in range(groups - 1)]
    before = lax.ppermute(up, "seq", forward)
    after = lax.ppermute(down, "seq", backward)
    rows = lax.all_to_all(summary, "seq", split_axis=0, concat_axis=0)

    edge = jnp.stack([group_index == 0, group_index == groups - 1]).astype(jnp.int32)
    ext = pltpu.VMEM((tok + 2 * PAIR, width), BF16)
    attended, query_grad, key_part, value_part, part = call(
        attention_kernel,
        [own, own, grad, grad, shaped((groups * n, width), F32)],
        8,
        [ext, ext],
        SMEM,
    )(edge, queries, key_states, value_states, out_grad, before, after, rows.reshape(groups * n, width))

    parts = lax.all_to_all(part.reshape(groups, n, width), "seq", split_axis=0, concat_axis=0)
    owned, term = call(owned_kernel, [shaped((n, width), F32), shaped((everyone, seg), F32)], 3)(
        parts, key_states, value_states
    )
    terms = lax.all_to_all(term, ("seq", "head"), split_axis=0, concat_axis=0)
    key_grad, value_grad = call(finish_kernel, [own, own], 4)(
        owned, key_part, value_part, weight_row
    )
    return (attended, query_grad, key_grad, value_grad, terms.sum(0))


def solution(mesh):
    return jax.shard_map(
        local,
        mesh=mesh,
        in_specs=(P("seq", "head"), P("seq", "head"), P("seq", "head"), P(), P("seq", "head")),
        out_specs=(P("seq", "head"), P("seq", "head"), P("seq", "head"), P("seq", "head"), P()),
        check_vma=False,
    )
```

```python
import functools

import jax
import jax.numpy as jnp
from jax import lax
from jax.experimental import pallas as pl
from jax.experimental.pallas import tpu as pltpu
from jax.sharding import PartitionSpec as P

HEAD_DIM = 64
BLOCK = 64
SUM_DEV = 4
PAIR = 2 * BLOCK
SCALE = HEAD_DIM ** (-0.5)
LOW = -1e30
VMEM = pl.BlockSpec(memory_space=pltpu.VMEM)
SMEM = pl.BlockSpec(memory_space=pltpu.SMEM)
PARAMS = pltpu.CompilerParams(vmem_limit_bytes=40 * 1024 * 1024)
F32 = jnp.float32
BF16 = jnp.bfloat16


def mm(a, b):
    return lax.dot_general(a, b, (((1,), (0,)), ((), ())), preferred_element_type=F32)


def mm_nt(a, b):
    return lax.dot_general(a, b, (((1,), (1,)), ((), ())), preferred_element_type=F32)


def mm_tn(a, b):
    return lax.dot_general(a, b, (((0,), (0,)), ((), ())), preferred_element_type=F32)


def pieces(x):
    high = x.astype(BF16)
    rest = x - high.astype(F32)
    middle = rest.astype(BF16)
    low = (rest - middle.astype(F32)).astype(BF16)
    return jnp.concatenate([high, middle, low], axis=0)


def segment_mask(first, rows, lanes, seg):
    row = lax.broadcasted_iota(jnp.int32, (rows, lanes), 0)
    lane = lax.broadcasted_iota(jnp.int32, (rows, lanes), 1)
    return row - first == lane // seg


def pool_kernel(q_ref, k_ref, v_ref, g_ref, w_ref, rows_ref, up_ref, down_ref):
    seg = w_ref.shape[1]
    n = 2 * SUM_DEV
    w = jnp.concatenate([w_ref[...]] * SUM_DEV, axis=1)
    w = jnp.broadcast_to(w, (n, w.shape[1]))
    pooled = jnp.zeros((n, k_ref.shape[0]), F32)
    for first, ref in ((0, k_ref), (SUM_DEV, v_ref)):
        weights = jnp.where(segment_mask(first, w.shape[0], w.shape[1], seg), w, 0.0)
        parts = mm_nt(pieces(weights), ref[...])
        pooled += parts[:n] + parts[n : 2 * n] + parts[2 * n :]
    rows_ref[...] = jnp.broadcast_to(pooled.astype(BF16)[None], rows_ref.shape)
    tok = k_ref.shape[1]
    up_ref[:, :PAIR] = k_ref[:, tok - PAIR :]
    up_ref[:, PAIR : 2 * PAIR] = v_ref[:, tok - PAIR :]
    up_ref[:, 2 * PAIR :] = jnp.concatenate(
        [q_ref[:, tok - BLOCK :], g_ref[:, tok - BLOCK :]], axis=1
    )
    down_ref[:, :PAIR] = k_ref[:, :PAIR]
    down_ref[:, PAIR : 2 * PAIR] = v_ref[:, :PAIR]
    down_ref[:, 2 * PAIR :] = jnp.concatenate([q_ref[:, :BLOCK], g_ref[:, :BLOCK]], axis=1)


def by_head(x):
    width = x.shape[0]
    x = x * jnp.asarray(SCALE, BF16)
    columns = []
    for h in range(width // HEAD_DIM):
        rows = [x[h * HEAD_DIM : (h + 1) * HEAD_DIM]]
        if h:
            rows.insert(0, jnp.zeros((h * HEAD_DIM, x.shape[1]), BF16))
        if (h + 1) * HEAD_DIM < width:
            rows.append(jnp.zeros((width - (h + 1) * HEAD_DIM, x.shape[1]), BF16))
        columns.append(jnp.concatenate(rows, axis=0))
    return jnp.concatenate(columns, axis=1)


def own_head(x):
    return jnp.concatenate(
        [
            x[h * HEAD_DIM : (h + 1) * HEAD_DIM, h * PAIR : (h + 1) * PAIR]
            for h in range(x.shape[0] // HEAD_DIM)
        ],
        axis=0,
    )


def head_sums(x):
    return jnp.concatenate(
        [
            jnp.sum(x[h * HEAD_DIM : (h + 1) * HEAD_DIM], axis=0, keepdims=True)
            for h in range(x.shape[0] // HEAD_DIM)
        ],
        axis=1,
    )


def top_of(x):
    return jnp.max(x, axis=0, keepdims=True)


def total_of(x):
    return jnp.sum(x, axis=0, keepdims=True)


def second_half(lanes):
    return lax.broadcasted_iota(jnp.int32, (1, lanes), 1) % PAIR >= BLOCK


def global_scores(rows, qm):
    shape = (rows.shape[0], qm.shape[1])
    is_key = lax.broadcasted_iota(jnp.int32, shape, 0) % (2 * SUM_DEV) < SUM_DEV
    return jnp.where(is_key, mm(rows, qm), LOW)


def value_rows(rows):
    return pltpu.roll(rows.astype(F32), rows.shape[0] - SUM_DEV, 0).astype(BF16)


def local_kernel(edge_ref, q_ref, k_ref, v_ref, before_ref, after_ref, exp_ref, top_ref, total_ref, kx_ref, vx_ref):
    width, tok = q_ref.shape
    lanes = width // HEAD_DIM * PAIR
    pairs = tok // PAIR
    for at, x_ref, own_ref in ((0, kx_ref, k_ref), (PAIR, vx_ref, v_ref)):
        x_ref[:PAIR] = before_ref[:, at : at + PAIR].T
        x_ref[PAIR : PAIR + tok] = own_ref[...].T
        x_ref[PAIR + tok :] = after_ref[:, at : at + PAIR].T
    second = second_half(lanes)
    for p in range(pairs):
        qm = by_head(q_ref[:, p * PAIR : (p + 1) * PAIR])
        start = BLOCK + p * PAIR
        s = mm(kx_ref[start : start + 2 * PAIR], qm)
        hide_low = second
        hide_high = jnp.logical_not(second)
        if p == 0:
            hide_low = jnp.logical_or(hide_low, edge_ref[0] == 1)
        if p == pairs - 1:
            hide_high = jnp.logical_or(hide_high, edge_ref[1] == 1)
        s = jnp.concatenate(
            [
                s[:BLOCK] + jnp.where(hide_low, LOW, 0.0),
                s[BLOCK : 3 * BLOCK],
                s[3 * BLOCK :] + jnp.where(hide_high, LOW, 0.0),
            ],
            axis=0,
        )
        top = top_of(s)
        s = jnp.exp(s - top)
        exp_ref[p] = s
        top_ref[p] = top
        total_ref[p] = total_of(s)


def global_kernel(q_ref, g_ref, vx_ref, rows_ref, exp_ref, top_ref, total_ref, att_ref, part_ref, ds_ref, factor_ref, delta_ref):
    width, tok = q_ref.shape
    rows = rows_ref[...]
    values_g = value_rows(rows)
    part = jnp.zeros(part_ref.shape, F32)
    for p in range(tok // PAIR):
        own = slice(p * PAIR, (p + 1) * PAIR)
        start = BLOCK + p * PAIR
        g = g_ref[:, own]
        qm, gm = by_head(q_ref[:, own]), by_head(g)
        s = global_scores(rows, qm)
        local_top = top_ref[p]
        top = jnp.maximum(local_top, top_of(s))
        s = jnp.exp(s - top)
        factor = jnp.exp(local_top - top)
        inverse = 1.0 / (total_ref[p] * factor + total_of(s))
        factor = factor * inverse
        w = s * inverse
        probs = (exp_ref[p] * factor).astype(BF16)
        att = mm_tn(vx_ref[start : start + 2 * PAIR], probs) + mm_tn(values_g, w.astype(BF16))
        att = own_head(att).astype(BF16)
        att_ref[:, own] = att
        delta = head_sums(g.astype(F32) * att.astype(F32)) * SCALE
        ds = (w * (mm(values_g, gm) - delta)).astype(BF16)
        part += mm_nt(ds, qm) + mm_nt(pltpu.roll(w, SUM_DEV, 0).astype(BF16), gm)
        ds_ref[p] = ds
        factor_ref[p] = factor
        delta_ref[p] = delta
    part_ref[...] = part * (1.0 / SCALE)


def gradient_kernel(q_ref, g_ref, kx_ref, vx_ref, rows_ref, exp_ref, before_ref, after_ref, ds_ref, factor_ref, delta_ref, qg_ref, kg_ref, vg_ref):
    width, tok = q_ref.shape
    lanes = width // HEAD_DIM * PAIR
    rows = rows_ref[...]
    kg = [jnp.zeros((width, PAIR), F32) for _ in range(tok // PAIR + 1)]
    vg = [jnp.zeros((width, PAIR), F32) for _ in range(tok // PAIR + 1)]
    for p in range(tok // PAIR):
        own = slice(p * PAIR, (p + 1) * PAIR)
        start = BLOCK + p * PAIR
        near = slice(start, start + 2 * PAIR)
        qm, gm = by_head(q_ref[:, own]), by_head(g_ref[:, own])
        w = exp_ref[p] * factor_ref[p]
        probs = w.astype(BF16)
        ds = (w * (mm(vx_ref[near], gm) - delta_ref[p])).astype(BF16)
        qg = own_head(mm_tn(kx_ref[near], ds) + mm_tn(rows, ds_ref[p]))
        qg_ref[:, own] = qg.astype(BF16)
        kgp, vgp = mm_nt(qm, ds), mm_nt(gm, probs)
        for b in range(2):
            kg[p + b] += kgp[:, b * PAIR : (b + 1) * PAIR]
            vg[p + b] += vgp[:, b * PAIR : (b + 1) * PAIR]

    second = second_half(lanes)
    edges = jnp.concatenate([before_ref[:, 2 * PAIR :], after_ref[:, 2 * PAIR :]], axis=1)
    q = jnp.concatenate([edges[:, :BLOCK], edges[:, PAIR : PAIR + BLOCK]], axis=1)
    g = jnp.concatenate([edges[:, BLOCK:PAIR], edges[:, PAIR + BLOCK :]], axis=1)
    qm, gm = by_head(q), by_head(g)
    low, high = slice(0, 3 * BLOCK), slice(tok + BLOCK, tok + 4 * BLOCK)
    values_g = value_rows(rows)
    s = jnp.where(second, mm(kx_ref[high], qm), mm(kx_ref[low], qm))
    sg = global_scores(rows, qm)
    top = jnp.maximum(top_of(s), top_of(sg))
    s, sg = jnp.exp(s - top), jnp.exp(sg - top)
    inverse = 1.0 / (total_of(s) + total_of(sg))
    s, sg = s * inverse, sg * inverse
    probs = s.astype(BF16)
    att = jnp.where(second, mm_tn(vx_ref[high], probs), mm_tn(vx_ref[low], probs))
    att = own_head(att + mm_tn(values_g, sg.astype(BF16))).astype(BF16)
    delta = head_sums(g.astype(F32) * att.astype(F32)) * SCALE
    near_low, near_high = slice(PAIR, PAIR + BLOCK), slice(tok + BLOCK, tok + PAIR)
    dp = jnp.where(second, mm(vx_ref[near_high], gm), mm(vx_ref[near_low], gm))
    w = jnp.where(second, s[:BLOCK], s[2 * BLOCK :])
    ds = w * (dp - delta)
    ds = jnp.concatenate([jnp.where(second, 0.0, ds), jnp.where(second, ds, 0.0)], axis=0)
    w = jnp.concatenate([jnp.where(second, 0.0, w), jnp.where(second, w, 0.0)], axis=0)
    kge, vge = mm_nt(qm, ds.astype(BF16)), mm_nt(gm, w.astype(BF16))
    for grads, edge, ref in ((kg, kge, kg_ref), (vg, vge, vg_ref)):
        whole = jnp.concatenate(grads, axis=1)[:, BLOCK : BLOCK + tok]
        ref[:, :BLOCK] = (whole[:, :BLOCK] + edge[:, :BLOCK]) * (1.0 / SCALE)
        ref[:, BLOCK : tok - BLOCK] = whole[:, BLOCK : tok - BLOCK] * (1.0 / SCALE)
        ref[:, tok - BLOCK :] = (whole[:, tok - BLOCK :] + edge[:, BLOCK:]) * (1.0 / SCALE)


def owned_kernel(parts_ref, k_ref, v_ref, owned_ref, term_ref):
    owned = jnp.sum(parts_ref[...], axis=0)
    owned_ref[...] = owned
    split = pieces(owned)
    n = 2 * SUM_DEV
    seg = k_ref.shape[1] // SUM_DEV
    total = jnp.zeros((1, k_ref.shape[1]), F32)
    for first, ref in ((0, k_ref), (SUM_DEV, v_ref)):
        met = mm(split, ref[...])
        met = met[:n] + met[n : 2 * n] + met[2 * n :]
        met = jnp.where(segment_mask(first, met.shape[0], met.shape[1], seg), met, 0.0)
        total += jnp.sum(met, axis=0, keepdims=True)
    term = total[:, :seg]
    for j in range(1, SUM_DEV):
        term += total[:, j * seg : (j + 1) * seg]
    term_ref[...] = jnp.broadcast_to(term, term_ref.shape)


def finish_kernel(owned_ref, kg_ref, vg_ref, w_ref, key_ref, value_ref):
    seg = w_ref.shape[1]
    columns = owned_ref[...].T
    w = w_ref[...]
    for first, grad_ref, out_ref in ((0, kg_ref, key_ref), (SUM_DEV, vg_ref, value_ref)):
        pooled = jnp.concatenate(
            [columns[:, first + j : first + j + 1] * w for j in range(SUM_DEV)], axis=1
        )
        out_ref[...] = (grad_ref[...] + pooled).astype(BF16)


def shaped(shape, dtype):
    return jax.ShapeDtypeStruct(shape, dtype)


def call(kernel, outs, count, first=VMEM):
    return pl.pallas_call(
        kernel,
        out_shape=outs,
        in_specs=[first] + [VMEM] * (count - 1),
        out_specs=[VMEM] * len(outs),
        compiler_params=PARAMS,
    )


def local(queries, key_states, value_states, pool_weight, out_grad):
    tok, width = queries.shape
    group_index = lax.axis_index("seq")
    groups = lax.axis_size("seq")
    everyone = groups * lax.axis_size("head")
    n = 2 * SUM_DEV
    seg = pool_weight.shape[0]
    pairs, lanes = tok // PAIR, width // HEAD_DIM * PAIR
    weight_row = pool_weight.reshape(1, seg)
    q, k, v, g = queries.T, key_states.T, value_states.T, out_grad.T
    halo = shaped((width, 3 * PAIR), BF16)
    own = shaped((width, tok), BF16)
    grad = shaped((width, tok), F32)
    ext = shaped((tok + 2 * PAIR, width), BF16)
    stat = shaped((pairs, 1, lanes), F32)

    summary, up, down = call(pool_kernel, [shaped((groups, n, width), BF16), halo, halo], 5)(
        q, k, v, g, weight_row
    )
    before = lax.ppermute(up, "seq", [(i, i + 1) for i in range(groups - 1)])
    after = lax.ppermute(down, "seq", [(i + 1, i) for i in range(groups - 1)])
    rows = lax.all_to_all(summary, "seq", split_axis=0, concat_axis=0)
    rows = rows.reshape(groups * n, width)
    edge = jnp.stack([group_index == 0, group_index == groups - 1]).astype(jnp.int32)
    exps, top, total, kx, vx = call(
        local_kernel, [shaped((pairs, 2 * PAIR, lanes), F32), stat, stat, ext, ext], 6, SMEM
    )(edge, q, k, v, before, after)

    attended, part, ds, factor, delta = call(
        global_kernel,
        [own, shaped((groups * n, width), F32), shaped((pairs, groups * n, lanes), BF16), stat, stat],
        7,
    )(q, g, vx, rows, exps, top, total)
    parts = lax.all_to_all(part.reshape(groups, n, width), "seq", split_axis=0, concat_axis=0)
    query_grad, key_part, value_part = call(gradient_kernel, [own, grad, grad], 11)(
        q, g, kx, vx, rows, exps, before, after, ds, factor, delta
    )
    owned, term = call(owned_kernel, [shaped((n, width), F32), shaped((everyone, seg), F32)], 3)(
        parts, k, v
    )
    terms = lax.all_to_all(term, ("seq", "head"), split_axis=0, concat_axis=0)
    key_grad, value_grad = call(finish_kernel, [own, own], 4)(
        owned, key_part, value_part, weight_row
    )
    return (attended.T, query_grad.T, key_grad.T, value_grad.T, terms.sum(0))


def solution(mesh):
    return jax.shard_map(
        local,
        mesh=mesh,
        in_specs=(P("seq", "head"), P("seq", "head"), P("seq", "head"), P(), P("seq", "head")),
        out_specs=(P("seq", "head"), P("seq", "head"), P("seq", "head"), P("seq", "head"), P()),
        check_vma=False,
    )
```

```python
import functools

import jax
import jax.numpy as jnp
from jax import lax
from jax.experimental import pallas as pl
from jax.experimental.pallas import tpu as pltpu
from jax.sharding import PartitionSpec as P

HEAD_DIM = 64
BLOCK = 64
SUM_DEV = 4
PAIR = 2 * BLOCK
SCALE = HEAD_DIM ** (-0.5)
LOW = -1e30
VMEM = pl.BlockSpec(memory_space=pltpu.VMEM)
SMEM = pl.BlockSpec(memory_space=pltpu.SMEM)
PARAMS = pltpu.CompilerParams(vmem_limit_bytes=40 * 1024 * 1024)
F32 = jnp.float32
BF16 = jnp.bfloat16


def mm(a, b):
    return lax.dot_general(a, b, (((1,), (0,)), ((), ())), preferred_element_type=F32)


def mm_nt(a, b):
    return lax.dot_general(a, b, (((1,), (1,)), ((), ())), preferred_element_type=F32)


def mm_tn(a, b):
    return lax.dot_general(a, b, (((0,), (0,)), ((), ())), preferred_element_type=F32)


def pieces(x):
    high = x.astype(BF16)
    rest = x - high.astype(F32)
    middle = rest.astype(BF16)
    low = (rest - middle.astype(F32)).astype(BF16)
    return jnp.concatenate([high, middle, low], axis=0)


def segment_mask(first, rows, lanes, seg):
    row = lax.broadcasted_iota(jnp.int32, (rows, lanes), 0)
    lane = lax.broadcasted_iota(jnp.int32, (rows, lanes), 1)
    return row - first == lane // seg


def pool_kernel(*refs):
    sources, (rows_ref, up_ref, down_ref, *kept), sem = refs[:5], refs[5:13], refs[13]
    q_ref, k_ref, v_ref, g_ref, w_ref = kept
    copies = [
        pltpu.make_async_copy(source, target, sem.at[i])
        for i, (source, target) in enumerate(zip(sources, kept))
    ]
    for i in (4, 1, 2, 0, 3):
        copies[i].start()
    for i in (4, 1, 2):
        copies[i].wait()
    seg = w_ref.shape[1]
    n = 2 * SUM_DEV
    w = jnp.concatenate([w_ref[...]] * SUM_DEV, axis=1)
    w = jnp.broadcast_to(w, (n, w.shape[1]))
    pooled = jnp.zeros((n, k_ref.shape[0]), F32)
    for first, ref in ((0, k_ref), (SUM_DEV, v_ref)):
        weights = jnp.where(segment_mask(first, w.shape[0], w.shape[1], seg), w, 0.0)
        parts = mm_nt(pieces(weights), ref[...])
        pooled += parts[:n] + parts[n : 2 * n] + parts[2 * n :]
    rows_ref[...] = jnp.broadcast_to(pooled.astype(BF16)[None], rows_ref.shape)
    copies[0].wait()
    copies[3].wait()
    tok = k_ref.shape[1]
    up_ref[:, :PAIR] = k_ref[:, tok - PAIR :]
    up_ref[:, PAIR : 2 * PAIR] = v_ref[:, tok - PAIR :]
    up_ref[:, 2 * PAIR :] = jnp.concatenate(
        [q_ref[:, tok - BLOCK :], g_ref[:, tok - BLOCK :]], axis=1
    )
    down_ref[:, :PAIR] = k_ref[:, :PAIR]
    down_ref[:, PAIR : 2 * PAIR] = v_ref[:, :PAIR]
    down_ref[:, 2 * PAIR :] = jnp.concatenate([q_ref[:, :BLOCK], g_ref[:, :BLOCK]], axis=1)


def by_head(x):
    width = x.shape[0]
    x = x * jnp.asarray(SCALE, BF16)
    columns = []
    for h in range(width // HEAD_DIM):
        rows = [x[h * HEAD_DIM : (h + 1) * HEAD_DIM]]
        if h:
            rows.insert(0, jnp.zeros((h * HEAD_DIM, x.shape[1]), BF16))
        if (h + 1) * HEAD_DIM < width:
            rows.append(jnp.zeros((width - (h + 1) * HEAD_DIM, x.shape[1]), BF16))
        columns.append(jnp.concatenate(rows, axis=0))
    return jnp.concatenate(columns, axis=1)


def own_head(x):
    return jnp.concatenate(
        [
            x[h * HEAD_DIM : (h + 1) * HEAD_DIM, h * PAIR : (h + 1) * PAIR]
            for h in range(x.shape[0] // HEAD_DIM)
        ],
        axis=0,
    )


def head_sums(x):
    return jnp.concatenate(
        [
            jnp.sum(x[h * HEAD_DIM : (h + 1) * HEAD_DIM], axis=0, keepdims=True)
            for h in range(x.shape[0] // HEAD_DIM)
        ],
        axis=1,
    )


def top_of(x):
    return jnp.max(x, axis=0, keepdims=True)


def total_of(x):
    return jnp.sum(x, axis=0, keepdims=True)


def second_half(lanes):
    return lax.broadcasted_iota(jnp.int32, (1, lanes), 1) % PAIR >= BLOCK


def global_scores(rows, qm):
    shape = (rows.shape[0], qm.shape[1])
    is_key = lax.broadcasted_iota(jnp.int32, shape, 0) % (2 * SUM_DEV) < SUM_DEV
    return jnp.where(is_key, mm(rows, qm), LOW)


def value_rows(rows):
    return pltpu.roll(rows.astype(F32), rows.shape[0] - SUM_DEV, 0).astype(BF16)


def local_kernel(edge_ref, q_ref, k_ref, v_ref, before_ref, after_ref, exp_ref, top_ref, total_ref, kx_ref, vx_ref):
    width, tok = q_ref.shape
    lanes = width // HEAD_DIM * PAIR
    pairs = tok // PAIR
    for at, x_ref, own_ref in ((0, kx_ref, k_ref), (PAIR, vx_ref, v_ref)):
        x_ref[:PAIR] = before_ref[:, at : at + PAIR].T
        x_ref[PAIR : PAIR + tok] = own_ref[...].T
        x_ref[PAIR + tok :] = after_ref[:, at : at + PAIR].T
    second = second_half(lanes)
    for p in range(pairs):
        qm = by_head(q_ref[:, p * PAIR : (p + 1) * PAIR])
        start = BLOCK + p * PAIR
        s = mm(kx_ref[start : start + 2 * PAIR], qm)
        hide_low = second
        hide_high = jnp.logical_not(second)
        if p == 0:
            hide_low = jnp.logical_or(hide_low, edge_ref[0] == 1)
        if p == pairs - 1:
            hide_high = jnp.logical_or(hide_high, edge_ref[1] == 1)
        s = jnp.concatenate(
            [
                s[:BLOCK] + jnp.where(hide_low, LOW, 0.0),
                s[BLOCK : 3 * BLOCK],
                s[3 * BLOCK :] + jnp.where(hide_high, LOW, 0.0),
            ],
            axis=0,
        )
        top = top_of(s)
        s = jnp.exp(s - top)
        exp_ref[p] = s
        top_ref[p] = top
        total_ref[p] = total_of(s)


def global_kernel(q_ref, g_ref, vx_ref, rows_ref, exp_ref, top_ref, total_ref, att_ref, part_ref, ds_ref, factor_ref, delta_ref):
    width, tok = q_ref.shape
    rows = rows_ref[...]
    values_g = value_rows(rows)
    part = jnp.zeros(part_ref.shape, F32)
    for p in range(tok // PAIR):
        own = slice(p * PAIR, (p + 1) * PAIR)
        start = BLOCK + p * PAIR
        g = g_ref[:, own]
        qm, gm = by_head(q_ref[:, own]), by_head(g)
        s = global_scores(rows, qm)
        local_top = top_ref[p]
        top = jnp.maximum(local_top, top_of(s))
        s = jnp.exp(s - top)
        factor = jnp.exp(local_top - top)
        inverse = 1.0 / (total_ref[p] * factor + total_of(s))
        factor = factor * inverse
        w = s * inverse
        probs = (exp_ref[p] * factor).astype(BF16)
        att = mm_tn(vx_ref[start : start + 2 * PAIR], probs) + mm_tn(values_g, w.astype(BF16))
        att = own_head(att).astype(BF16)
        att_ref[:, own] = att
        delta = head_sums(g.astype(F32) * att.astype(F32)) * SCALE
        ds = (w * (mm(values_g, gm) - delta)).astype(BF16)
        part += mm_nt(ds, qm) + mm_nt(pltpu.roll(w, SUM_DEV, 0).astype(BF16), gm)
        ds_ref[p] = ds
        factor_ref[p] = factor
        delta_ref[p] = delta
    part_ref[...] = part * (1.0 / SCALE)


def gradient_kernel(q_ref, g_ref, kx_ref, vx_ref, rows_ref, exp_ref, before_ref, after_ref, ds_ref, factor_ref, delta_ref, qg_ref, kg_ref, vg_ref):
    width, tok = q_ref.shape
    lanes = width // HEAD_DIM * PAIR
    rows = rows_ref[...]
    kg = [jnp.zeros((width, PAIR), F32) for _ in range(tok // PAIR + 1)]
    vg = [jnp.zeros((width, PAIR), F32) for _ in range(tok // PAIR + 1)]
    for p in range(tok // PAIR):
        own = slice(p * PAIR, (p + 1) * PAIR)
        start = BLOCK + p * PAIR
        near = slice(start, start + 2 * PAIR)
        qm, gm = by_head(q_ref[:, own]), by_head(g_ref[:, own])
        w = exp_ref[p] * factor_ref[p]
        probs = w.astype(BF16)
        ds = (w * (mm(vx_ref[near], gm) - delta_ref[p])).astype(BF16)
        qg = own_head(mm_tn(kx_ref[near], ds) + mm_tn(rows, ds_ref[p]))
        qg_ref[:, own] = qg.astype(BF16)
        kgp, vgp = mm_nt(qm, ds), mm_nt(gm, probs)
        for b in range(2):
            kg[p + b] += kgp[:, b * PAIR : (b + 1) * PAIR]
            vg[p + b] += vgp[:, b * PAIR : (b + 1) * PAIR]

    second = second_half(lanes)
    edges = jnp.concatenate([before_ref[:, 2 * PAIR :], after_ref[:, 2 * PAIR :]], axis=1)
    q = jnp.concatenate([edges[:, :BLOCK], edges[:, PAIR : PAIR + BLOCK]], axis=1)
    g = jnp.concatenate([edges[:, BLOCK:PAIR], edges[:, PAIR + BLOCK :]], axis=1)
    qm, gm = by_head(q), by_head(g)
    low, high = slice(0, 3 * BLOCK), slice(tok + BLOCK, tok + 4 * BLOCK)
    values_g = value_rows(rows)
    s = jnp.where(second, mm(kx_ref[high], qm), mm(kx_ref[low], qm))
    sg = global_scores(rows, qm)
    top = jnp.maximum(top_of(s), top_of(sg))
    s, sg = jnp.exp(s - top), jnp.exp(sg - top)
    inverse = 1.0 / (total_of(s) + total_of(sg))
    s, sg = s * inverse, sg * inverse
    probs = s.astype(BF16)
    att = jnp.where(second, mm_tn(vx_ref[high], probs), mm_tn(vx_ref[low], probs))
    att = own_head(att + mm_tn(values_g, sg.astype(BF16))).astype(BF16)
    delta = head_sums(g.astype(F32) * att.astype(F32)) * SCALE
    near_low, near_high = slice(PAIR, PAIR + BLOCK), slice(tok + BLOCK, tok + PAIR)
    dp = jnp.where(second, mm(vx_ref[near_high], gm), mm(vx_ref[near_low], gm))
    w = jnp.where(second, s[:BLOCK], s[2 * BLOCK :])
    ds = w * (dp - delta)
    ds = jnp.concatenate([jnp.where(second, 0.0, ds), jnp.where(second, ds, 0.0)], axis=0)
    w = jnp.concatenate([jnp.where(second, 0.0, w), jnp.where(second, w, 0.0)], axis=0)
    kge, vge = mm_nt(qm, ds.astype(BF16)), mm_nt(gm, w.astype(BF16))
    for grads, edge, ref in ((kg, kge, kg_ref), (vg, vge, vg_ref)):
        whole = jnp.concatenate(grads, axis=1)[:, BLOCK : BLOCK + tok]
        ref[:, :BLOCK] = (whole[:, :BLOCK] + edge[:, :BLOCK]) * (1.0 / SCALE)
        ref[:, BLOCK : tok - BLOCK] = whole[:, BLOCK : tok - BLOCK] * (1.0 / SCALE)
        ref[:, tok - BLOCK :] = (whole[:, tok - BLOCK :] + edge[:, BLOCK:]) * (1.0 / SCALE)


def owned_kernel(parts_ref, k_ref, v_ref, owned_ref, term_ref):
    owned = jnp.sum(parts_ref[...], axis=0)
    owned_ref[...] = owned
    split = pieces(owned)
    n = 2 * SUM_DEV
    seg = k_ref.shape[1] // SUM_DEV
    total = jnp.zeros((1, k_ref.shape[1]), F32)
    for first, ref in ((0, k_ref), (SUM_DEV, v_ref)):
        met = mm(split, ref[...])
        met = met[:n] + met[n : 2 * n] + met[2 * n :]
        met = jnp.where(segment_mask(first, met.shape[0], met.shape[1], seg), met, 0.0)
        total += jnp.sum(met, axis=0, keepdims=True)
    term = total[:, :seg]
    for j in range(1, SUM_DEV):
        term += total[:, j * seg : (j + 1) * seg]
    term_ref[...] = jnp.broadcast_to(term, term_ref.shape)


def finish_kernel(owned_ref, kg_ref, vg_ref, w_ref, key_ref, value_ref):
    seg = w_ref.shape[1]
    columns = owned_ref[...].T
    w = w_ref[...]
    for first, grad_ref, out_ref in ((0, kg_ref, key_ref), (SUM_DEV, vg_ref, value_ref)):
        pooled = jnp.concatenate(
            [columns[:, first + j : first + j + 1] * w for j in range(SUM_DEV)], axis=1
        )
        out_ref[...] = (grad_ref[...] + pooled).astype(BF16)


def shaped(shape, dtype):
    return jax.ShapeDtypeStruct(shape, dtype)


def call(kernel, outs, count, first=VMEM):
    return pl.pallas_call(
        kernel,
        out_shape=outs,
        in_specs=[first] + [VMEM] * (count - 1),
        out_specs=[VMEM] * len(outs),
        compiler_params=PARAMS,
    )


def local(queries, key_states, value_states, pool_weight, out_grad):
    tok, width = queries.shape
    group_index = lax.axis_index("seq")
    groups = lax.axis_size("seq")
    everyone = groups * lax.axis_size("head")
    n = 2 * SUM_DEV
    seg = pool_weight.shape[0]
    pairs, lanes = tok // PAIR, width // HEAD_DIM * PAIR
    halo = shaped((width, 3 * PAIR), BF16)
    own = shaped((width, tok), BF16)
    grad = shaped((width, tok), F32)
    ext = shaped((tok + 2 * PAIR, width), BF16)
    stat = shaped((pairs, 1, lanes), F32)

    arguments = (queries.T, key_states.T, value_states.T, out_grad.T, pool_weight.reshape(1, seg))
    summary, up, down, q, k, v, g, weight_row = pl.pallas_call(
        pool_kernel,
        out_shape=[shaped((groups, n, width), BF16), halo, halo] + [own] * 4 + [shaped((1, seg), F32)],
        in_specs=[pl.BlockSpec(memory_space=pltpu.HBM)] * 5,
        out_specs=[VMEM] * 8,
        scratch_shapes=[pltpu.SemaphoreType.DMA((5,))],
        compiler_params=PARAMS,
    )(*[pltpu.with_memory_space_constraint(x, pltpu.HBM) for x in arguments])
    before = lax.ppermute(up, "seq", [(i, i + 1) for i in range(groups - 1)])
    after = lax.ppermute(down, "seq", [(i + 1, i) for i in range(groups - 1)])
    rows = lax.all_to_all(summary, "seq", split_axis=0, concat_axis=0)
    rows = rows.reshape(groups * n, width)
    edge = jnp.stack([group_index == 0, group_index == groups - 1]).astype(jnp.int32)
    exps, top, total, kx, vx = call(
        local_kernel, [shaped((pairs, 2 * PAIR, lanes), F32), stat, stat, ext, ext], 6, SMEM
    )(edge, q, k, v, before, after)

    attended, part, ds, factor, delta = call(
        global_kernel,
        [own, shaped((groups * n, width), F32), shaped((pairs, groups * n, lanes), BF16), stat, stat],
        7,
    )(q, g, vx, rows, exps, top, total)
    parts = lax.all_to_all(part.reshape(groups, n, width), "seq", split_axis=0, concat_axis=0)
    query_grad, key_part, value_part = call(gradient_kernel, [own, grad, grad], 11)(
        q, g, kx, vx, rows, exps, before, after, ds, factor, delta
    )
    owned, term = call(owned_kernel, [shaped((n, width), F32), shaped((everyone, seg), F32)], 3)(
        parts, k, v
    )
    terms = lax.all_to_all(term, ("seq", "head"), split_axis=0, concat_axis=0)
    key_grad, value_grad = call(finish_kernel, [own, own], 4)(
        owned, key_part, value_part, weight_row
    )
    return (attended.T, query_grad.T, key_grad.T, value_grad.T, terms.sum(0))


def solution(mesh):
    return jax.shard_map(
        local,
        mesh=mesh,
        in_specs=(P("seq", "head"), P("seq", "head"), P("seq", "head"), P(), P("seq", "head")),
        out_specs=(P("seq", "head"), P("seq", "head"), P("seq", "head"), P("seq", "head"), P()),
        check_vma=False,
    )
```

```python
import functools

import jax
import jax.numpy as jnp
from jax import lax
from jax.experimental import pallas as pl
from jax.experimental.pallas import tpu as pltpu
from jax.sharding import PartitionSpec as P

HEAD_DIM = 64
BLOCK = 64
SUM_DEV = 4
PAIR = 2 * BLOCK
SCALE = HEAD_DIM ** (-0.5)
LOW = -1e30
VMEM = pl.BlockSpec(memory_space=pltpu.VMEM)
SMEM = pl.BlockSpec(memory_space=pltpu.SMEM)
PARAMS = pltpu.CompilerParams(vmem_limit_bytes=40 * 1024 * 1024)
F32 = jnp.float32
BF16 = jnp.bfloat16


def mm(a, b):
    return lax.dot_general(a, b, (((1,), (0,)), ((), ())), preferred_element_type=F32)


def mm_nt(a, b):
    return lax.dot_general(a, b, (((1,), (1,)), ((), ())), preferred_element_type=F32)


def mm_tn(a, b):
    return lax.dot_general(a, b, (((0,), (0,)), ((), ())), preferred_element_type=F32)


def pieces(x):
    high = x.astype(BF16)
    rest = x - high.astype(F32)
    middle = rest.astype(BF16)
    low = (rest - middle.astype(F32)).astype(BF16)
    return jnp.concatenate([high, middle, low], axis=0)


def segment_mask(first, rows, lanes, seg):
    row = lax.broadcasted_iota(jnp.int32, (rows, lanes), 0)
    lane = lax.broadcasted_iota(jnp.int32, (rows, lanes), 1)
    return row - first == lane // seg


def pool_kernel(*refs):
    sources, (rows_ref, up_ref, down_ref, *kept), sem = refs[:5], refs[5:13], refs[13]
    q_ref, k_ref, v_ref, g_ref, w_ref = kept
    copies = [
        pltpu.make_async_copy(source, target, sem.at[i])
        for i, (source, target) in enumerate(zip(sources, kept))
    ]
    for i in (4, 1, 2, 0, 3):
        copies[i].start()
    for i in (4, 1, 2):
        copies[i].wait()
    seg = w_ref.shape[1]
    n = 2 * SUM_DEV
    w = jnp.concatenate([w_ref[...]] * SUM_DEV, axis=1)
    w = jnp.broadcast_to(w, (n, w.shape[1]))
    pooled = jnp.zeros((n, k_ref.shape[0]), F32)
    for first, ref in ((0, k_ref), (SUM_DEV, v_ref)):
        weights = jnp.where(segment_mask(first, w.shape[0], w.shape[1], seg), w, 0.0)
        parts = mm_nt(pieces(weights), ref[...])
        pooled += parts[:n] + parts[n : 2 * n] + parts[2 * n :]
    rows_ref[...] = jnp.broadcast_to(pooled.astype(BF16)[None], rows_ref.shape)
    copies[0].wait()
    copies[3].wait()
    tok = k_ref.shape[1]
    up_ref[:, :PAIR] = k_ref[:, tok - PAIR :]
    up_ref[:, PAIR : 2 * PAIR] = v_ref[:, tok - PAIR :]
    up_ref[:, 2 * PAIR :] = jnp.concatenate(
        [q_ref[:, tok - BLOCK :], g_ref[:, tok - BLOCK :]], axis=1
    )
    down_ref[:, :PAIR] = k_ref[:, :PAIR]
    down_ref[:, PAIR : 2 * PAIR] = v_ref[:, :PAIR]
    down_ref[:, 2 * PAIR :] = jnp.concatenate([q_ref[:, :BLOCK], g_ref[:, :BLOCK]], axis=1)


def by_head(x):
    width = x.shape[0]
    x = x * jnp.asarray(SCALE, BF16)
    columns = []
    for h in range(width // HEAD_DIM):
        rows = [x[h * HEAD_DIM : (h + 1) * HEAD_DIM]]
        if h:
            rows.insert(0, jnp.zeros((h * HEAD_DIM, x.shape[1]), BF16))
        if (h + 1) * HEAD_DIM < width:
            rows.append(jnp.zeros((width - (h + 1) * HEAD_DIM, x.shape[1]), BF16))
        columns.append(jnp.concatenate(rows, axis=0))
    return jnp.concatenate(columns, axis=1)


def own_head(x):
    return jnp.concatenate(
        [
            x[h * HEAD_DIM : (h + 1) * HEAD_DIM, h * PAIR : (h + 1) * PAIR]
            for h in range(x.shape[0] // HEAD_DIM)
        ],
        axis=0,
    )


def head_sums(x):
    return jnp.concatenate(
        [
            jnp.sum(x[h * HEAD_DIM : (h + 1) * HEAD_DIM], axis=0, keepdims=True)
            for h in range(x.shape[0] // HEAD_DIM)
        ],
        axis=1,
    )


def top_of(x):
    return jnp.max(x, axis=0, keepdims=True)


def total_of(x):
    return jnp.sum(x, axis=0, keepdims=True)


def second_half(lanes):
    return lax.broadcasted_iota(jnp.int32, (1, lanes), 1) % PAIR >= BLOCK


def global_scores(rows, qm):
    shape = (rows.shape[0], qm.shape[1])
    is_key = lax.broadcasted_iota(jnp.int32, shape, 0) % (2 * SUM_DEV) < SUM_DEV
    return jnp.where(is_key, mm(rows, qm), LOW)


def value_rows(rows):
    return pltpu.roll(rows.astype(F32), rows.shape[0] - SUM_DEV, 0).astype(BF16)


def local_kernel(edge_ref, q_ref, k_ref, v_ref, before_ref, after_ref, exp_ref, top_ref, total_ref, kx_ref, vx_ref):
    width, tok = q_ref.shape
    lanes = width // HEAD_DIM * PAIR
    pairs = tok // PAIR
    for at, x_ref, own_ref in ((0, kx_ref, k_ref), (PAIR, vx_ref, v_ref)):
        x_ref[:PAIR] = before_ref[:, at : at + PAIR].T
        x_ref[PAIR : PAIR + tok] = own_ref[...].T
        x_ref[PAIR + tok :] = after_ref[:, at : at + PAIR].T
    second = second_half(lanes)
    for p in range(pairs):
        qm = by_head(q_ref[:, p * PAIR : (p + 1) * PAIR])
        start = BLOCK + p * PAIR
        s = mm(kx_ref[start : start + 2 * PAIR], qm)
        hide_low = second
        hide_high = jnp.logical_not(second)
        if p == 0:
            hide_low = jnp.logical_or(hide_low, edge_ref[0] == 1)
        if p == pairs - 1:
            hide_high = jnp.logical_or(hide_high, edge_ref[1] == 1)
        s = jnp.concatenate(
            [
                s[:BLOCK] + jnp.where(hide_low, LOW, 0.0),
                s[BLOCK : 3 * BLOCK],
                s[3 * BLOCK :] + jnp.where(hide_high, LOW, 0.0),
            ],
            axis=0,
        )
        top = top_of(s)
        s = jnp.exp(s - top)
        exp_ref[p] = s
        top_ref[p] = top
        total_ref[p] = total_of(s)


def global_kernel(q_ref, g_ref, vx_ref, rows_ref, exp_ref, top_ref, total_ref, att_ref, part_ref, ds_ref, factor_ref, delta_ref):
    width, tok = q_ref.shape
    rows = rows_ref[...]
    values_g = value_rows(rows)
    part = jnp.zeros(part_ref.shape, F32)
    for p in range(tok // PAIR):
        own = slice(p * PAIR, (p + 1) * PAIR)
        start = BLOCK + p * PAIR
        g = g_ref[:, own]
        qm, gm = by_head(q_ref[:, own]), by_head(g)
        s = global_scores(rows, qm)
        local_top = top_ref[p]
        top = jnp.maximum(local_top, top_of(s))
        s = jnp.exp(s - top)
        factor = jnp.exp(local_top - top)
        inverse = 1.0 / (total_ref[p] * factor + total_of(s))
        factor = factor * inverse
        w = s * inverse
        probs = (exp_ref[p] * factor).astype(BF16)
        att = mm_tn(vx_ref[start : start + 2 * PAIR], probs) + mm_tn(values_g, w.astype(BF16))
        att = own_head(att).astype(BF16)
        att_ref[:, own] = att
        delta = head_sums(g.astype(F32) * att.astype(F32)) * SCALE
        ds = (w * (mm(values_g, gm) - delta)).astype(BF16)
        part += mm_nt(ds, qm) + mm_nt(pltpu.roll(w, SUM_DEV, 0).astype(BF16), gm)
        ds_ref[p] = ds
        factor_ref[p] = factor
        delta_ref[p] = delta
    part_ref[...] = part * (1.0 / SCALE)


def gradient_kernel(q_ref, g_ref, kx_ref, vx_ref, rows_ref, exp_ref, before_ref, after_ref, ds_ref, factor_ref, delta_ref, qg_ref, kg_ref, vg_ref):
    width, tok = q_ref.shape
    lanes = width // HEAD_DIM * PAIR
    rows = rows_ref[...]
    kg = [jnp.zeros((width, PAIR), F32) for _ in range(tok // PAIR + 1)]
    vg = [jnp.zeros((width, PAIR), F32) for _ in range(tok // PAIR + 1)]
    for p in range(tok // PAIR):
        own = slice(p * PAIR, (p + 1) * PAIR)
        start = BLOCK + p * PAIR
        near = slice(start, start + 2 * PAIR)
        qm, gm = by_head(q_ref[:, own]), by_head(g_ref[:, own])
        w = exp_ref[p] * factor_ref[p]
        probs = w.astype(BF16)
        ds = (w * (mm(vx_ref[near], gm) - delta_ref[p])).astype(BF16)
        qg = own_head(mm_tn(kx_ref[near], ds) + mm_tn(rows, ds_ref[p]))
        qg_ref[:, own] = qg.astype(BF16)
        kgp, vgp = mm_nt(qm, ds), mm_nt(gm, probs)
        for b in range(2):
            kg[p + b] += kgp[:, b * PAIR : (b + 1) * PAIR]
            vg[p + b] += vgp[:, b * PAIR : (b + 1) * PAIR]

    second = second_half(lanes)
    edges = jnp.concatenate([before_ref[:, 2 * PAIR :], after_ref[:, 2 * PAIR :]], axis=1)
    q = jnp.concatenate([edges[:, :BLOCK], edges[:, PAIR : PAIR + BLOCK]], axis=1)
    g = jnp.concatenate([edges[:, BLOCK:PAIR], edges[:, PAIR + BLOCK :]], axis=1)
    qm, gm = by_head(q), by_head(g)
    low, high = slice(0, 3 * BLOCK), slice(tok + BLOCK, tok + 4 * BLOCK)
    values_g = value_rows(rows)
    s = jnp.where(second, mm(kx_ref[high], qm), mm(kx_ref[low], qm))
    sg = global_scores(rows, qm)
    top = jnp.maximum(top_of(s), top_of(sg))
    s, sg = jnp.exp(s - top), jnp.exp(sg - top)
    inverse = 1.0 / (total_of(s) + total_of(sg))
    s, sg = s * inverse, sg * inverse
    probs = s.astype(BF16)
    att = jnp.where(second, mm_tn(vx_ref[high], probs), mm_tn(vx_ref[low], probs))
    att = own_head(att + mm_tn(values_g, sg.astype(BF16))).astype(BF16)
    delta = head_sums(g.astype(F32) * att.astype(F32)) * SCALE
    near_low, near_high = slice(PAIR, PAIR + BLOCK), slice(tok + BLOCK, tok + PAIR)
    dp = jnp.where(second, mm(vx_ref[near_high], gm), mm(vx_ref[near_low], gm))
    w = jnp.where(second, s[:BLOCK], s[2 * BLOCK :])
    ds = w * (dp - delta)
    ds = jnp.concatenate([jnp.where(second, 0.0, ds), jnp.where(second, ds, 0.0)], axis=0)
    w = jnp.concatenate([jnp.where(second, 0.0, w), jnp.where(second, w, 0.0)], axis=0)
    kge, vge = mm_nt(qm, ds.astype(BF16)), mm_nt(gm, w.astype(BF16))
    for grads, edge, ref in ((kg, kge, kg_ref), (vg, vge, vg_ref)):
        whole = jnp.concatenate(grads, axis=1)[:, BLOCK : BLOCK + tok]
        ref[:, :BLOCK] = (whole[:, :BLOCK] + edge[:, :BLOCK]) * (1.0 / SCALE)
        ref[:, BLOCK : tok - BLOCK] = whole[:, BLOCK : tok - BLOCK] * (1.0 / SCALE)
        ref[:, tok - BLOCK :] = (whole[:, tok - BLOCK :] + edge[:, BLOCK:]) * (1.0 / SCALE)


def owned_kernel(parts_ref, k_ref, v_ref, owned_ref, term_ref):
    owned = jnp.sum(parts_ref[...], axis=0)
    owned_ref[...] = owned
    split = pieces(owned)
    n = 2 * SUM_DEV
    seg = k_ref.shape[1] // SUM_DEV
    total = jnp.zeros((1, k_ref.shape[1]), F32)
    for first, ref in ((0, k_ref), (SUM_DEV, v_ref)):
        met = mm(split, ref[...])
        met = met[:n] + met[n : 2 * n] + met[2 * n :]
        met = jnp.where(segment_mask(first, met.shape[0], met.shape[1], seg), met, 0.0)
        total += jnp.sum(met, axis=0, keepdims=True)
    term = total[:, :seg]
    for j in range(1, SUM_DEV):
        term += total[:, j * seg : (j + 1) * seg]
    term_ref[...] = jnp.broadcast_to(term, term_ref.shape)


def finish_kernel(owned_ref, kg_ref, vg_ref, w_ref, key_ref, value_ref):
    seg = w_ref.shape[1]
    columns = owned_ref[...].T
    w = w_ref[...]
    for first, grad_ref, out_ref in ((0, kg_ref, key_ref), (SUM_DEV, vg_ref, value_ref)):
        pooled = jnp.concatenate(
            [columns[:, first + j : first + j + 1] * w for j in range(SUM_DEV)], axis=1
        )
        out_ref[...] = (grad_ref[...] + pooled).astype(BF16)


def shaped(shape, dtype):
    return jax.ShapeDtypeStruct(shape, dtype)


def call(kernel, outs, count, first=VMEM):
    return pl.pallas_call(
        kernel,
        out_shape=outs,
        in_specs=[first] + [VMEM] * (count - 1),
        out_specs=[VMEM] * len(outs),
        compiler_params=PARAMS,
    )


def local(queries, key_states, value_states, pool_weight, out_grad):
    tok, width = queries.shape
    group_index = lax.axis_index("seq")
    groups = lax.axis_size("seq")
    everyone = groups * lax.axis_size("head")
    n = 2 * SUM_DEV
    seg = pool_weight.shape[0]
    pairs, lanes = tok // PAIR, width // HEAD_DIM * PAIR
    halo = shaped((width, 3 * PAIR), BF16)
    own = shaped((width, tok), BF16)
    grad = shaped((width, tok), F32)
    ext = shaped((tok + 2 * PAIR, width), BF16)
    stat = shaped((pairs, 1, lanes), F32)

    arguments = (queries.T, key_states.T, value_states.T, out_grad.T, pool_weight.reshape(1, seg))
    summary, up, down, q, k, v, g, weight_row = pl.pallas_call(
        pool_kernel,
        out_shape=[shaped((groups, n, width), BF16), halo, halo] + [own] * 4 + [shaped((1, seg), F32)],
        in_specs=[pl.BlockSpec(memory_space=pltpu.HBM)] * 5,
        out_specs=[VMEM] * 8,
        scratch_shapes=[pltpu.SemaphoreType.DMA((5,))],
        compiler_params=PARAMS,
    )(*[pltpu.with_memory_space_constraint(x, pltpu.HBM) for x in arguments])
    before = lax.ppermute(up, "seq", [(i, i + 1) for i in range(groups - 1)])
    after = lax.ppermute(down, "seq", [(i + 1, i) for i in range(groups - 1)])
    reverse = [list(range(groups))[::-1]]
    rows = lax.all_to_all(
        summary, "seq", split_axis=0, concat_axis=0, axis_index_groups=reverse
    )
    rows = rows.reshape(groups * n, width)
    edge = jnp.stack([group_index == 0, group_index == groups - 1]).astype(jnp.int32)
    exps, top, total, kx, vx = call(
        local_kernel, [shaped((pairs, 2 * PAIR, lanes), F32), stat, stat, ext, ext], 6, SMEM
    )(edge, q, k, v, before, after)

    attended, part, ds, factor, delta = call(
        global_kernel,
        [own, shaped((groups * n, width), F32), shaped((pairs, groups * n, lanes), BF16), stat, stat],
        7,
    )(q, g, vx, rows, exps, top, total)
    parts = lax.all_to_all(
        part.reshape(groups, n, width), "seq", split_axis=0, concat_axis=0, axis_index_groups=reverse
    )
    query_grad, key_part, value_part = call(gradient_kernel, [own, grad, grad], 11)(
        q, g, kx, vx, rows, exps, before, after, ds, factor, delta
    )
    owned, term = call(owned_kernel, [shaped((n, width), F32), shaped((everyone, seg), F32)], 3)(
        parts, k, v
    )
    terms = lax.all_to_all(term, ("seq", "head"), split_axis=0, concat_axis=0)
    key_grad, value_grad = call(finish_kernel, [own, own], 4)(
        owned, key_part, value_part, weight_row
    )
    return (attended.T, query_grad.T, key_grad.T, value_grad.T, terms.sum(0))


def solution(mesh):
    return jax.shard_map(
        local,
        mesh=mesh,
        in_specs=(P("seq", "head"), P("seq", "head"), P("seq", "head"), P(), P("seq", "head")),
        out_specs=(P("seq", "head"), P("seq", "head"), P("seq", "head"), P("seq", "head"), P()),
        check_vma=False,
    )
```

```python
import functools

import jax
import jax.numpy as jnp
from jax import lax
from jax.experimental import pallas as pl
from jax.experimental.pallas import tpu as pltpu
from jax.sharding import PartitionSpec as P

HEAD_DIM = 64
BLOCK = 64
SUM_DEV = 4
PAIR = 2 * BLOCK
SCALE = HEAD_DIM ** (-0.5)
LOW = -1e30
VMEM = pl.BlockSpec(memory_space=pltpu.VMEM)
SMEM = pl.BlockSpec(memory_space=pltpu.SMEM)
PARAMS = pltpu.CompilerParams(vmem_limit_bytes=40 * 1024 * 1024)
F32 = jnp.float32
BF16 = jnp.bfloat16


def mm(a, b):
    return lax.dot_general(a, b, (((1,), (0,)), ((), ())), preferred_element_type=F32)


def mm_nt(a, b):
    return lax.dot_general(a, b, (((1,), (1,)), ((), ())), preferred_element_type=F32)


def mm_tn(a, b):
    return lax.dot_general(a, b, (((0,), (0,)), ((), ())), preferred_element_type=F32)


def pieces(x):
    high = x.astype(BF16)
    rest = x - high.astype(F32)
    middle = rest.astype(BF16)
    low = (rest - middle.astype(F32)).astype(BF16)
    return jnp.concatenate([high, middle, low], axis=0)


def segment_mask(first, rows, lanes, seg):
    row = lax.broadcasted_iota(jnp.int32, (rows, lanes), 0)
    lane = lax.broadcasted_iota(jnp.int32, (rows, lanes), 1)
    return row - first == lane // seg


def pool_kernel(*refs):
    sources, (rows_ref, up_ref, down_ref, *kept), sem = refs[:5], refs[5:13], refs[13]
    q_ref, k_ref, v_ref, g_ref, w_ref = kept
    copies = [
        pltpu.make_async_copy(source, target, sem.at[i])
        for i, (source, target) in enumerate(zip(sources, kept))
    ]
    for i in (4, 1, 2, 0, 3):
        copies[i].start()
    for i in (4, 1, 2):
        copies[i].wait()
    seg = w_ref.shape[1]
    n = 2 * SUM_DEV
    w = jnp.concatenate([w_ref[...]] * SUM_DEV, axis=1)
    w = jnp.broadcast_to(w, (n, w.shape[1]))
    pooled = jnp.zeros((n, k_ref.shape[0]), F32)
    for first, ref in ((0, k_ref), (SUM_DEV, v_ref)):
        weights = jnp.where(segment_mask(first, w.shape[0], w.shape[1], seg), w, 0.0)
        parts = mm_nt(pieces(weights), ref[...])
        pooled += parts[:n] + parts[n : 2 * n] + parts[2 * n :]
    rows_ref[...] = jnp.broadcast_to(pooled.astype(BF16)[None], rows_ref.shape)
    copies[0].wait()
    copies[3].wait()
    tok = k_ref.shape[1]
    up_ref[:, :PAIR] = k_ref[:, tok - PAIR :]
    up_ref[:, PAIR : 2 * PAIR] = v_ref[:, tok - PAIR :]
    up_ref[:, 2 * PAIR :] = jnp.concatenate(
        [q_ref[:, tok - BLOCK :], g_ref[:, tok - BLOCK :]], axis=1
    )
    down_ref[:, :PAIR] = k_ref[:, :PAIR]
    down_ref[:, PAIR : 2 * PAIR] = v_ref[:, :PAIR]
    down_ref[:, 2 * PAIR :] = jnp.concatenate([q_ref[:, :BLOCK], g_ref[:, :BLOCK]], axis=1)


def by_head(x):
    width = x.shape[0]
    x = x * jnp.asarray(SCALE, BF16)
    columns = []
    for h in range(width // HEAD_DIM):
        rows = [x[h * HEAD_DIM : (h + 1) * HEAD_DIM]]
        if h:
            rows.insert(0, jnp.zeros((h * HEAD_DIM, x.shape[1]), BF16))
        if (h + 1) * HEAD_DIM < width:
            rows.append(jnp.zeros((width - (h + 1) * HEAD_DIM, x.shape[1]), BF16))
        columns.append(jnp.concatenate(rows, axis=0))
    return jnp.concatenate(columns, axis=1)


def own_head(x):
    return jnp.concatenate(
        [
            x[h * HEAD_DIM : (h + 1) * HEAD_DIM, h * PAIR : (h + 1) * PAIR]
            for h in range(x.shape[0] // HEAD_DIM)
        ],
        axis=0,
    )


def head_sums(x):
    return jnp.concatenate(
        [
            jnp.sum(x[h * HEAD_DIM : (h + 1) * HEAD_DIM], axis=0, keepdims=True)
            for h in range(x.shape[0] // HEAD_DIM)
        ],
        axis=1,
    )


def top_of(x):
    return jnp.max(x, axis=0, keepdims=True)


def total_of(x):
    return jnp.sum(x, axis=0, keepdims=True)


def second_half(lanes):
    return lax.broadcasted_iota(jnp.int32, (1, lanes), 1) % PAIR >= BLOCK


def global_scores(rows, qm):
    shape = (rows.shape[0], qm.shape[1])
    is_key = lax.broadcasted_iota(jnp.int32, shape, 0) % (2 * SUM_DEV) < SUM_DEV
    return jnp.where(is_key, mm(rows, qm), LOW)


def value_rows(rows):
    return pltpu.roll(rows.astype(F32), rows.shape[0] - SUM_DEV, 0).astype(BF16)


def local_kernel(edge_ref, q_ref, k_ref, v_ref, before_ref, after_ref, exp_ref, top_ref, total_ref, kx_ref, vx_ref):
    width, tok = q_ref.shape
    lanes = width // HEAD_DIM * PAIR
    pairs = tok // PAIR
    for at, x_ref, own_ref in ((0, kx_ref, k_ref), (PAIR, vx_ref, v_ref)):
        x_ref[:PAIR] = before_ref[:, at : at + PAIR].T
        x_ref[PAIR : PAIR + tok] = own_ref[...].T
        x_ref[PAIR + tok :] = after_ref[:, at : at + PAIR].T
    second = second_half(lanes)
    for p in range(pairs):
        qm = by_head(q_ref[:, p * PAIR : (p + 1) * PAIR])
        start = BLOCK + p * PAIR
        s = mm(kx_ref[start : start + 2 * PAIR], qm)
        hide_low = second
        hide_high = jnp.logical_not(second)
        if p == 0:
            hide_low = jnp.logical_or(hide_low, edge_ref[0] == 1)
        if p == pairs - 1:
            hide_high = jnp.logical_or(hide_high, edge_ref[1] == 1)
        s = jnp.concatenate(
            [
                s[:BLOCK] + jnp.where(hide_low, LOW, 0.0),
                s[BLOCK : 3 * BLOCK],
                s[3 * BLOCK :] + jnp.where(hide_high, LOW, 0.0),
            ],
            axis=0,
        )
        top = top_of(s)
        s = jnp.exp(s - top)
        exp_ref[p] = s
        top_ref[p] = top
        total_ref[p] = total_of(s)


def global_kernel(q_ref, g_ref, vx_ref, rows_ref, exp_ref, top_ref, total_ref, att_ref, part_ref, ds_ref, factor_ref, delta_ref):
    width, tok = q_ref.shape
    rows = rows_ref[...]
    values_g = value_rows(rows)
    part = jnp.zeros(part_ref.shape, F32)
    for p in range(tok // PAIR):
        own = slice(p * PAIR, (p + 1) * PAIR)
        start = BLOCK + p * PAIR
        g = g_ref[:, own]
        qm, gm = by_head(q_ref[:, own]), by_head(g)
        s = global_scores(rows, qm)
        local_top = top_ref[p]
        top = jnp.maximum(local_top, top_of(s))
        s = jnp.exp(s - top)
        factor = jnp.exp(local_top - top)
        inverse = 1.0 / (total_ref[p] * factor + total_of(s))
        factor = factor * inverse
        w = s * inverse
        probs = (exp_ref[p] * factor).astype(BF16)
        att = mm_tn(vx_ref[start : start + 2 * PAIR], probs) + mm_tn(values_g, w.astype(BF16))
        att = own_head(att).astype(BF16)
        att_ref[:, own] = att
        delta = head_sums(g.astype(F32) * att.astype(F32)) * SCALE
        ds = (w * (mm(values_g, gm) - delta)).astype(BF16)
        part += mm_nt(ds, qm) + mm_nt(pltpu.roll(w, SUM_DEV, 0).astype(BF16), gm)
        ds_ref[p] = ds
        factor_ref[p] = factor
        delta_ref[p] = delta
    part_ref[...] = part * (1.0 / SCALE)


def gradient_kernel(q_ref, g_ref, kx_ref, vx_ref, rows_ref, exp_ref, before_ref, after_ref, ds_ref, factor_ref, delta_ref, qg_ref, kg_ref, vg_ref):
    width, tok = q_ref.shape
    lanes = width // HEAD_DIM * PAIR
    rows = rows_ref[...]
    kg = [jnp.zeros((width, PAIR), F32) for _ in range(tok // PAIR + 1)]
    vg = [jnp.zeros((width, PAIR), F32) for _ in range(tok // PAIR + 1)]
    for p in range(tok // PAIR):
        own = slice(p * PAIR, (p + 1) * PAIR)
        start = BLOCK + p * PAIR
        near = slice(start, start + 2 * PAIR)
        qm, gm = by_head(q_ref[:, own]), by_head(g_ref[:, own])
        w = exp_ref[p] * factor_ref[p]
        probs = w.astype(BF16)
        ds = (w * (mm(vx_ref[near], gm) - delta_ref[p])).astype(BF16)
        qg = own_head(mm_tn(kx_ref[near], ds) + mm_tn(rows, ds_ref[p]))
        qg_ref[:, own] = qg.astype(BF16)
        kgp, vgp = mm_nt(qm, ds), mm_nt(gm, probs)
        for b in range(2):
            kg[p + b] += kgp[:, b * PAIR : (b + 1) * PAIR]
            vg[p + b] += vgp[:, b * PAIR : (b + 1) * PAIR]

    second = second_half(lanes)
    edges = jnp.concatenate([before_ref[:, 2 * PAIR :], after_ref[:, 2 * PAIR :]], axis=1)
    q = jnp.concatenate([edges[:, :BLOCK], edges[:, PAIR : PAIR + BLOCK]], axis=1)
    g = jnp.concatenate([edges[:, BLOCK:PAIR], edges[:, PAIR + BLOCK :]], axis=1)
    qm, gm = by_head(q), by_head(g)
    low, high = slice(0, 3 * BLOCK), slice(tok + BLOCK, tok + 4 * BLOCK)
    values_g = value_rows(rows)
    s = jnp.where(second, mm(kx_ref[high], qm), mm(kx_ref[low], qm))
    sg = global_scores(rows, qm)
    top = jnp.maximum(top_of(s), top_of(sg))
    s, sg = jnp.exp(s - top), jnp.exp(sg - top)
    inverse = 1.0 / (total_of(s) + total_of(sg))
    s, sg = s * inverse, sg * inverse
    probs = s.astype(BF16)
    att = jnp.where(second, mm_tn(vx_ref[high], probs), mm_tn(vx_ref[low], probs))
    att = own_head(att + mm_tn(values_g, sg.astype(BF16))).astype(BF16)
    delta = head_sums(g.astype(F32) * att.astype(F32)) * SCALE
    near_low, near_high = slice(PAIR, PAIR + BLOCK), slice(tok + BLOCK, tok + PAIR)
    dp = jnp.where(second, mm(vx_ref[near_high], gm), mm(vx_ref[near_low], gm))
    w = jnp.where(second, s[:BLOCK], s[2 * BLOCK :])
    ds = w * (dp - delta)
    ds = jnp.concatenate([jnp.where(second, 0.0, ds), jnp.where(second, ds, 0.0)], axis=0)
    w = jnp.concatenate([jnp.where(second, 0.0, w), jnp.where(second, w, 0.0)], axis=0)
    kge, vge = mm_nt(qm, ds.astype(BF16)), mm_nt(gm, w.astype(BF16))
    for grads, edge, ref in ((kg, kge, kg_ref), (vg, vge, vg_ref)):
        whole = jnp.concatenate(grads, axis=1)[:, BLOCK : BLOCK + tok]
        ref[:, :BLOCK] = (whole[:, :BLOCK] + edge[:, :BLOCK]) * (1.0 / SCALE)
        ref[:, BLOCK : tok - BLOCK] = whole[:, BLOCK : tok - BLOCK] * (1.0 / SCALE)
        ref[:, tok - BLOCK :] = (whole[:, tok - BLOCK :] + edge[:, BLOCK:]) * (1.0 / SCALE)


def owned_kernel(parts_ref, k_ref, v_ref, owned_ref, term_ref):
    owned = jnp.sum(parts_ref[...], axis=0)
    owned_ref[...] = owned
    split = pieces(owned)
    n = 2 * SUM_DEV
    seg = k_ref.shape[1] // SUM_DEV
    total = jnp.zeros((1, k_ref.shape[1]), F32)
    for first, ref in ((0, k_ref), (SUM_DEV, v_ref)):
        met = mm(split, ref[...])
        met = met[:n] + met[n : 2 * n] + met[2 * n :]
        met = jnp.where(segment_mask(first, met.shape[0], met.shape[1], seg), met, 0.0)
        total += jnp.sum(met, axis=0, keepdims=True)
    term = total[:, :seg]
    for j in range(1, SUM_DEV):
        term += total[:, j * seg : (j + 1) * seg]
    term_ref[...] = jnp.broadcast_to(term, term_ref.shape)


def finish_kernel(owned_ref, kg_ref, vg_ref, w_ref, key_ref, value_ref):
    seg = w_ref.shape[1]
    columns = owned_ref[...].T
    w = w_ref[...]
    for first, grad_ref, out_ref in ((0, kg_ref, key_ref), (SUM_DEV, vg_ref, value_ref)):
        pooled = jnp.concatenate(
            [columns[:, first + j : first + j + 1] * w for j in range(SUM_DEV)], axis=1
        )
        out_ref[...] = (grad_ref[...] + pooled).astype(BF16)


def shaped(shape, dtype):
    return jax.ShapeDtypeStruct(shape, dtype)


def call(kernel, outs, count, first=VMEM):
    return pl.pallas_call(
        kernel,
        out_shape=outs,
        in_specs=[first] + [VMEM] * (count - 1),
        out_specs=[VMEM] * len(outs),
        compiler_params=PARAMS,
    )


def local(queries, key_states, value_states, pool_weight, out_grad):
    tok, width = queries.shape
    group_index = lax.axis_index("seq")
    groups = lax.axis_size("seq")
    everyone = groups * lax.axis_size("head")
    n = 2 * SUM_DEV
    seg = pool_weight.shape[0]
    pairs, lanes = tok // PAIR, width // HEAD_DIM * PAIR
    halo = shaped((width, 3 * PAIR), BF16)
    own = shaped((width, tok), BF16)
    grad = shaped((width, tok), F32)
    ext = shaped((tok + 2 * PAIR, width), BF16)
    stat = shaped((pairs, 1, lanes), F32)

    arguments = (queries.T, key_states.T, value_states.T, out_grad.T, pool_weight.reshape(1, seg))
    summary, up, down, q, k, v, g, weight_row = pl.pallas_call(
        pool_kernel,
        out_shape=[shaped((groups, n, width), BF16), halo, halo] + [own] * 4 + [shaped((1, seg), F32)],
        in_specs=[pl.BlockSpec(memory_space=pltpu.HBM)] * 5,
        out_specs=[VMEM] * 8,
        scratch_shapes=[pltpu.SemaphoreType.DMA((5,))],
        compiler_params=PARAMS,
    )(*[pltpu.with_memory_space_constraint(x, pltpu.HBM) for x in arguments])
    before = lax.ppermute(up, "seq", [(i, i + 1) for i in range(groups - 1)])
    after = lax.ppermute(down, "seq", [(i + 1, i) for i in range(groups - 1)])
    order = [[(i + groups // 2) % groups for i in range(groups)]]
    rows = lax.all_to_all(
        summary, "seq", split_axis=0, concat_axis=0, axis_index_groups=order
    )
    rows = rows.reshape(groups * n, width)
    edge = jnp.stack([group_index == 0, group_index == groups - 1]).astype(jnp.int32)
    exps, top, total, kx, vx = call(
        local_kernel, [shaped((pairs, 2 * PAIR, lanes), F32), stat, stat, ext, ext], 6, SMEM
    )(edge, q, k, v, before, after)

    attended, part, ds, factor, delta = call(
        global_kernel,
        [own, shaped((groups * n, width), F32), shaped((pairs, groups * n, lanes), BF16), stat, stat],
        7,
    )(q, g, vx, rows, exps, top, total)
    parts = lax.all_to_all(
        part.reshape(groups, n, width), "seq", split_axis=0, concat_axis=0, axis_index_groups=order
    )
    query_grad, key_part, value_part = call(gradient_kernel, [own, grad, grad], 11)(
        q, g, kx, vx, rows, exps, before, after, ds, factor, delta
    )
    owned, term = call(owned_kernel, [shaped((n, width), F32), shaped((everyone, seg), F32)], 3)(
        parts, k, v
    )
    terms = lax.all_to_all(term, ("seq", "head"), split_axis=0, concat_axis=0)
    key_grad, value_grad = call(finish_kernel, [own, own], 4)(
        owned, key_part, value_part, weight_row
    )
    return (attended.T, query_grad.T, key_grad.T, value_grad.T, terms.sum(0))


def solution(mesh):
    return jax.shard_map(
        local,
        mesh=mesh,
        in_specs=(P("seq", "head"), P("seq", "head"), P("seq", "head"), P(), P("seq", "head")),
        out_specs=(P("seq", "head"), P("seq", "head"), P("seq", "head"), P("seq", "head"), P()),
        check_vma=False,
    )
```

```python
import functools

import jax
import jax.numpy as jnp
from jax import lax
from jax.experimental import pallas as pl
from jax.experimental.pallas import tpu as pltpu
from jax.sharding import PartitionSpec as P

HEAD_DIM = 64
BLOCK = 64
SUM_DEV = 4
PAIR = 2 * BLOCK
SCALE = HEAD_DIM ** (-0.5)
LOW = -1e30
VMEM = pl.BlockSpec(memory_space=pltpu.VMEM)
SMEM = pl.BlockSpec(memory_space=pltpu.SMEM)
PARAMS = pltpu.CompilerParams(vmem_limit_bytes=40 * 1024 * 1024)
F32 = jnp.float32
BF16 = jnp.bfloat16


def mm(a, b):
    return lax.dot_general(a, b, (((1,), (0,)), ((), ())), preferred_element_type=F32)


def mm_nt(a, b):
    return lax.dot_general(a, b, (((1,), (1,)), ((), ())), preferred_element_type=F32)


def mm_tn(a, b):
    return lax.dot_general(a, b, (((0,), (0,)), ((), ())), preferred_element_type=F32)


def pieces(x):
    high = x.astype(BF16)
    rest = x - high.astype(F32)
    middle = rest.astype(BF16)
    low = (rest - middle.astype(F32)).astype(BF16)
    return jnp.concatenate([high, middle, low], axis=0)


def segment_mask(first, rows, lanes, seg):
    row = lax.broadcasted_iota(jnp.int32, (rows, lanes), 0)
    lane = lax.broadcasted_iota(jnp.int32, (rows, lanes), 1)
    return row - first == lane // seg


def pool_kernel(*refs):
    sources, (rows_ref, up_ref, *kept), sem = refs[:5], refs[5:12], refs[12]
    q_ref, k_ref, v_ref, g_ref, w_ref = kept
    copies = [
        pltpu.make_async_copy(source, target, sem.at[i])
        for i, (source, target) in enumerate(zip(sources, kept))
    ]
    for i in (4, 1, 2, 0, 3):
        copies[i].start()
    for i in (4, 1, 2):
        copies[i].wait()
    seg = w_ref.shape[1]
    n = 2 * SUM_DEV
    w = jnp.concatenate([w_ref[...]] * SUM_DEV, axis=1)
    w = jnp.broadcast_to(w, (n, w.shape[1]))
    pooled = jnp.zeros((n, k_ref.shape[0]), F32)
    for first, ref in ((0, k_ref), (SUM_DEV, v_ref)):
        weights = jnp.where(segment_mask(first, w.shape[0], w.shape[1], seg), w, 0.0)
        parts = mm_nt(pieces(weights), ref[...])
        pooled += parts[:n] + parts[n : 2 * n] + parts[2 * n :]
    rows_ref[...] = jnp.broadcast_to(pooled.astype(BF16)[None], rows_ref.shape)
    copies[0].wait()
    copies[3].wait()
    tok = k_ref.shape[1]
    up_ref[:, :PAIR] = k_ref[:, tok - PAIR :]
    up_ref[:, PAIR : 2 * PAIR] = v_ref[:, tok - PAIR :]
    up_ref[:, 2 * PAIR :] = jnp.concatenate(
        [q_ref[:, tok - BLOCK :], g_ref[:, tok - BLOCK :]], axis=1
    )


def by_head(x):
    width = x.shape[0]
    x = x * jnp.asarray(SCALE, BF16)
    columns = []
    for h in range(width // HEAD_DIM):
        rows = [x[h * HEAD_DIM : (h + 1) * HEAD_DIM]]
        if h:
            rows.insert(0, jnp.zeros((h * HEAD_DIM, x.shape[1]), BF16))
        if (h + 1) * HEAD_DIM < width:
            rows.append(jnp.zeros((width - (h + 1) * HEAD_DIM, x.shape[1]), BF16))
        columns.append(jnp.concatenate(rows, axis=0))
    return jnp.concatenate(columns, axis=1)


def own_head(x):
    return jnp.concatenate(
        [
            x[h * HEAD_DIM : (h + 1) * HEAD_DIM, h * PAIR : (h + 1) * PAIR]
            for h in range(x.shape[0] // HEAD_DIM)
        ],
        axis=0,
    )


def head_sums(x):
    return jnp.concatenate(
        [
            jnp.sum(x[h * HEAD_DIM : (h + 1) * HEAD_DIM], axis=0, keepdims=True)
            for h in range(x.shape[0] // HEAD_DIM)
        ],
        axis=1,
    )


def top_of(x):
    return jnp.max(x, axis=0, keepdims=True)


def total_of(x):
    return jnp.sum(x, axis=0, keepdims=True)


def second_half(lanes):
    return lax.broadcasted_iota(jnp.int32, (1, lanes), 1) % PAIR >= BLOCK


def global_scores(rows, qm):
    shape = (rows.shape[0], qm.shape[1])
    is_key = lax.broadcasted_iota(jnp.int32, shape, 0) % (2 * SUM_DEV) < SUM_DEV
    return jnp.where(is_key, mm(rows, qm), LOW)


def value_rows(rows):
    return pltpu.roll(rows.astype(F32), rows.shape[0] - SUM_DEV, 0).astype(BF16)


def local_kernel(
    edge_ref, q_ref, k_ref, v_ref, g_ref, before_ref,
    exp_ref, top_ref, total_ref, qx_ref, gx_ref, kx_ref, vx_ref, kt_ref, vt_ref,
):
    width, tok = q_ref.shape
    lanes = width // HEAD_DIM * PAIR
    pairs = tok // PAIR
    for at, t_ref, x_ref, own_ref in ((0, kt_ref, kx_ref, k_ref), (PAIR, vt_ref, vx_ref, v_ref)):
        t_ref[:, :PAIR] = before_ref[:, at : at + PAIR]
        t_ref[:, PAIR:] = own_ref[...]
        x_ref[:PAIR] = before_ref[:, at : at + PAIR].T
        x_ref[PAIR:] = own_ref[...].T
    for at, x_ref, own_ref in ((2 * PAIR, qx_ref, q_ref), (2 * PAIR + BLOCK, gx_ref, g_ref)):
        nothing = jnp.zeros((width, BLOCK), BF16)
        x_ref[...] = jnp.concatenate([before_ref[:, at : at + BLOCK], own_ref[...], nothing], axis=1)
    second = second_half(lanes)
    for p in range(pairs):
        s = mm(kx_ref[p * PAIR : (p + 2) * PAIR], by_head(qx_ref[:, p * PAIR : (p + 1) * PAIR]))
        parts = [s[b * BLOCK : (b + 1) * BLOCK] for b in range(4)]
        parts[0] += jnp.where(second, LOW, 0.0)
        if p == 0:
            parts[1] += jnp.where(edge_ref[0] == 1, LOW, 0.0)
        parts[3] += jnp.where(second, 0.0, LOW)
        s = jnp.concatenate(parts, axis=0)
        top = top_of(s)
        s = jnp.exp(s - top)
        exp_ref[p] = s
        top_ref[p] = top
        total_ref[p] = total_of(s)

    @pl.when(edge_ref[1] == 1)
    def _():
        s = mm(kx_ref[tok:], by_head(qx_ref[:, tok:]))
        top = top_of(s)
        s = jnp.exp(s - top)
        exp_ref[pairs, :PAIR] = s
        top_ref[pairs] = top
        total_ref[pairs] = total_of(s)


def global_kernel(
    edge_ref, qx_ref, gx_ref, vt_ref, rows_ref, exp_ref, top_ref, total_ref,
    att_ref, part_ref, ds_ref, factor_ref, delta_ref,
):
    pairs = qx_ref.shape[1] // PAIR - 1
    rows = rows_ref[...]
    values_g = value_rows(rows)

    def pair(p, keys):
        own = slice(p * PAIR, (p + 1) * PAIR)
        near = slice(p * PAIR, p * PAIR + keys)
        g = gx_ref[:, own]
        qm, gm = by_head(qx_ref[:, own]), by_head(g)
        s = global_scores(rows, qm)
        local_top = top_ref[p]
        top = jnp.maximum(local_top, top_of(s))
        s = jnp.exp(s - top)
        factor = jnp.exp(local_top - top)
        inverse = 1.0 / (total_ref[p] * factor + total_of(s))
        factor = factor * inverse
        w = s * inverse
        probs = (exp_ref[p, :keys] * factor).astype(BF16)
        att = mm(vt_ref[:, near], probs) + mm_tn(values_g, w.astype(BF16))
        att = own_head(att).astype(BF16)
        att_ref[:, own] = att
        delta = head_sums(g.astype(F32) * att.astype(F32)) * SCALE
        ds = (w * (mm(values_g, gm) - delta)).astype(BF16)
        ds_ref[p] = ds
        factor_ref[p] = factor
        delta_ref[p] = delta
        part = mm_nt(ds, qm) + mm_nt(pltpu.roll(w, SUM_DEV, 0).astype(BF16), gm)
        return part * (1.0 / SCALE)

    part_ref[...] = sum(pair(p, 2 * PAIR) for p in range(pairs))

    @pl.when(edge_ref[1] == 1)
    def _():
        part_ref[...] += pair(pairs, PAIR)


def gradient_kernel(
    edge_ref, qx_ref, gx_ref, kt_ref, vx_ref, rows_ref, exp_ref, att_ref, ds_ref, factor_ref, delta_ref,
    qg_ref, kg_ref, vg_ref, back_ref,
):
    width, tok = kg_ref.shape
    pairs = qx_ref.shape[1] // PAIR - 1
    rows = rows_ref[...]

    def pair(p, keys):
        own = slice(p * PAIR, (p + 1) * PAIR)
        near = slice(p * PAIR, p * PAIR + keys)
        qm, gm = by_head(qx_ref[:, own]), by_head(gx_ref[:, own])
        w = exp_ref[p, :keys] * factor_ref[p]
        ds = (w * (mm(vx_ref[near], gm) - delta_ref[p])).astype(BF16)
        qg = own_head(mm(kt_ref[:, near], ds) + mm_tn(rows, ds_ref[p])).astype(BF16)
        qg_ref[:, own] = qg
        kg = mm_nt(qm, ds) * (1.0 / SCALE)
        vg = mm_nt(gm, w.astype(BF16)) * (1.0 / SCALE)
        return qg, kg, vg

    grads = [pair(p, 2 * PAIR) for p in range(pairs)]
    edge = jnp.concatenate([att_ref[:, :BLOCK], grads[0][0][:, :BLOCK]], axis=1)
    back_ref[:, 2 * PAIR :] = edge
    for at, i, ref in ((0, 1, kg_ref), (PAIR, 2, vg_ref)):
        back_ref[:, at : at + PAIR] = grads[0][i][:, :PAIR].astype(BF16)
        for p in range(pairs - 1):
            ref[:, p * PAIR : (p + 1) * PAIR] = grads[p][i][:, PAIR:] + grads[p + 1][i][:, :PAIR]
        ref[:, tok - PAIR :] = grads[-1][i][:, PAIR:]

    @pl.when(edge_ref[1] == 1)
    def _():
        _, kg, vg = pair(pairs, PAIR)
        kg_ref[:, tok - PAIR :] += kg
        vg_ref[:, tok - PAIR :] += vg


def owned_kernel(parts_ref, k_ref, v_ref, owned_ref, term_ref):
    owned = jnp.sum(parts_ref[...], axis=0)
    owned_ref[...] = owned
    split = pieces(owned)
    n = 2 * SUM_DEV
    seg = k_ref.shape[1] // SUM_DEV
    total = jnp.zeros((1, k_ref.shape[1]), F32)
    for first, ref in ((0, k_ref), (SUM_DEV, v_ref)):
        met = mm(split, ref[...])
        met = met[:n] + met[n : 2 * n] + met[2 * n :]
        met = jnp.where(segment_mask(first, met.shape[0], met.shape[1], seg), met, 0.0)
        total += jnp.sum(met, axis=0, keepdims=True)
    term = total[:, :seg]
    for j in range(1, SUM_DEV):
        term += total[:, j * seg : (j + 1) * seg]
    term_ref[...] = jnp.broadcast_to(term, term_ref.shape)


def finish_kernel(
    edge_ref, owned_ref, kg_ref, vg_ref, w_ref, back_ref, attx_ref, qgx_ref,
    key_ref, value_ref, att_ref, qg_ref,
):
    tok = kg_ref.shape[1]
    columns = owned_ref[...].T
    w = w_ref[...]
    for first, at, grad_ref, out_ref in ((0, 0, kg_ref, key_ref), (SUM_DEV, PAIR, vg_ref, value_ref)):
        pooled = jnp.concatenate(
            [columns[:, first + j : first + j + 1] * w for j in range(SUM_DEV)], axis=1
        )
        total = grad_ref[...] + pooled
        out_ref[:, : tok - PAIR] = total[:, : tok - PAIR].astype(BF16)
        total = total[:, tok - PAIR :] + back_ref[:, at : at + PAIR].astype(F32)
        out_ref[:, tok - PAIR :] = total.astype(BF16)
    last = edge_ref[1] == 1
    for at, x_ref, out_ref in ((0, attx_ref, att_ref), (BLOCK, qgx_ref, qg_ref)):
        x = x_ref[:, BLOCK : tok + BLOCK]
        out_ref[...] = x
        edge = back_ref[:, 2 * PAIR + at : 2 * PAIR + at + BLOCK]

        @pl.when(jnp.logical_not(last))
        def _():
            out_ref[:, tok - BLOCK :] = edge


def shaped(shape, dtype):
    return jax.ShapeDtypeStruct(shape, dtype)


def call(kernel, outs, count, first=VMEM):
    return pl.pallas_call(
        kernel,
        out_shape=outs,
        in_specs=[first] + [VMEM] * (count - 1),
        out_specs=[VMEM] * len(outs),
        compiler_params=PARAMS,
    )


def local(queries, key_states, value_states, pool_weight, out_grad):
    tok, width = queries.shape
    group_index = lax.axis_index("seq")
    groups = lax.axis_size("seq")
    everyone = groups * lax.axis_size("head")
    n = 2 * SUM_DEV
    seg = pool_weight.shape[0]
    pairs, lanes = tok // PAIR, width // HEAD_DIM * PAIR
    halo = shaped((width, 3 * PAIR), BF16)
    own = shaped((width, tok), BF16)
    grad = shaped((width, tok), F32)
    queries_x = shaped((width, tok + PAIR), BF16)
    keys_x = shaped((tok + PAIR, width), BF16)
    stat = shaped((pairs + 1, 1, lanes), F32)

    arguments = (queries.T, key_states.T, value_states.T, out_grad.T, pool_weight.reshape(1, seg))
    summary, up, q, k, v, g, weight_row = pl.pallas_call(
        pool_kernel,
        out_shape=[shaped((groups, n, width), BF16), halo] + [own] * 4 + [shaped((1, seg), F32)],
        in_specs=[pl.BlockSpec(memory_space=pltpu.HBM)] * 5,
        out_specs=[VMEM] * 7,
        scratch_shapes=[pltpu.SemaphoreType.DMA((5,))],
        compiler_params=PARAMS,
    )(*[pltpu.with_memory_space_constraint(x, pltpu.HBM) for x in arguments])
    before = lax.ppermute(up, "seq", [(i, i + 1) for i in range(groups - 1)])
    order = [[(i + groups // 2) % groups for i in range(groups)]]
    rows = lax.all_to_all(
        summary, "seq", split_axis=0, concat_axis=0, axis_index_groups=order
    )
    rows = rows.reshape(groups * n, width)
    edge = jnp.stack([group_index == 0, group_index == groups - 1]).astype(jnp.int32)
    exps, top, total, qx, gx, kx, vx, kt, vt = call(
        local_kernel,
        [shaped((pairs + 1, 2 * PAIR, lanes), F32), stat, stat]
        + [queries_x, queries_x, keys_x, keys_x, queries_x, queries_x],
        6,
        SMEM,
    )(edge, q, k, v, g, before)

    att_x, part, ds, factor, delta = call(
        global_kernel,
        [queries_x, shaped((groups * n, width), F32)]
        + [shaped((pairs + 1, groups * n, lanes), BF16), stat, stat],
        8,
        SMEM,
    )(edge, qx, gx, vt, rows, exps, top, total)
    parts = lax.all_to_all(
        part.reshape(groups, n, width), "seq", split_axis=0, concat_axis=0, axis_index_groups=order
    )
    qg_x, key_part, value_part, down = call(gradient_kernel, [queries_x, grad, grad, halo], 11, SMEM)(
        edge, qx, gx, kt, vx, rows, exps, att_x, ds, factor, delta
    )
    back = lax.ppermute(down, "seq", [(i + 1, i) for i in range(groups - 1)])
    parts, qg_x = lax.optimization_barrier((parts, qg_x))
    owned, term = call(owned_kernel, [shaped((n, width), F32), shaped((everyone, seg), F32)], 3)(
        parts, k, v
    )
    terms = lax.all_to_all(term, ("seq", "head"), split_axis=0, concat_axis=0)
    key_grad, value_grad, attended, query_grad = call(finish_kernel, [own] * 4, 8, SMEM)(
        edge, owned, key_part, value_part, weight_row, back, att_x, qg_x
    )
    return (attended.T, query_grad.T, key_grad.T, value_grad.T, terms.sum(0))


def solution(mesh):
    return jax.shard_map(
        local,
        mesh=mesh,
        in_specs=(P("seq", "head"), P("seq", "head"), P("seq", "head"), P(), P("seq", "head")),
        out_specs=(P("seq", "head"), P("seq", "head"), P("seq", "head"), P("seq", "head"), P()),
        check_vma=False,
    )
```

```python
import functools

import jax
import jax.numpy as jnp
from jax import lax
from jax.experimental import pallas as pl
from jax.experimental.pallas import tpu as pltpu
from jax.sharding import PartitionSpec as P

HEAD_DIM = 64
BLOCK = 64
SUM_DEV = 4
PAIR = 2 * BLOCK
SCALE = HEAD_DIM ** (-0.5)
LOW = -1e30
VMEM = pl.BlockSpec(memory_space=pltpu.VMEM)
SMEM = pl.BlockSpec(memory_space=pltpu.SMEM)
PARAMS = pltpu.CompilerParams(vmem_limit_bytes=40 * 1024 * 1024)
F32 = jnp.float32
BF16 = jnp.bfloat16


def mm(a, b):
    return lax.dot_general(a, b, (((1,), (0,)), ((), ())), preferred_element_type=F32)


def mm_nt(a, b):
    return lax.dot_general(a, b, (((1,), (1,)), ((), ())), preferred_element_type=F32)


def mm_tn(a, b):
    return lax.dot_general(a, b, (((0,), (0,)), ((), ())), preferred_element_type=F32)


def pieces(x):
    high = x.astype(BF16)
    rest = x - high.astype(F32)
    middle = rest.astype(BF16)
    low = (rest - middle.astype(F32)).astype(BF16)
    return jnp.concatenate([high, middle, low], axis=0)


def segment_mask(first, rows, lanes, seg):
    row = lax.broadcasted_iota(jnp.int32, (rows, lanes), 0)
    lane = lax.broadcasted_iota(jnp.int32, (rows, lanes), 1)
    return row - first == lane // seg


def pool_kernel(*refs):
    sources, (rows_ref, up_ref, *kept), sem = refs[:5], refs[5:12], refs[12]
    q_ref, k_ref, v_ref, g_ref, w_ref = kept
    copies = [
        pltpu.make_async_copy(source, target, sem.at[i])
        for i, (source, target) in enumerate(zip(sources, kept))
    ]
    for i in (4, 1, 2, 0, 3):
        copies[i].start()
    for i in (4, 1, 2):
        copies[i].wait()
    seg = w_ref.shape[1]
    n = 2 * SUM_DEV
    w = jnp.concatenate([w_ref[...]] * SUM_DEV, axis=1)
    w = jnp.broadcast_to(w, (n, w.shape[1]))
    pooled = jnp.zeros((n, k_ref.shape[0]), F32)
    for first, ref in ((0, k_ref), (SUM_DEV, v_ref)):
        weights = jnp.where(segment_mask(first, w.shape[0], w.shape[1], seg), w, 0.0)
        parts = mm_nt(pieces(weights), ref[...])
        pooled += parts[:n] + parts[n : 2 * n] + parts[2 * n :]
    rows_ref[...] = jnp.broadcast_to(pooled.astype(BF16)[None], rows_ref.shape)
    copies[0].wait()
    copies[3].wait()
    tok = k_ref.shape[1]
    up_ref[:, :PAIR] = k_ref[:, tok - PAIR :]
    up_ref[:, PAIR : 2 * PAIR] = v_ref[:, tok - PAIR :]
    up_ref[:, 2 * PAIR :] = jnp.concatenate(
        [q_ref[:, tok - BLOCK :], g_ref[:, tok - BLOCK :]], axis=1
    )


def by_head(x):
    width = x.shape[0]
    x = x * jnp.asarray(SCALE, BF16)
    columns = []
    for h in range(width // HEAD_DIM):
        rows = [x[h * HEAD_DIM : (h + 1) * HEAD_DIM]]
        if h:
            rows.insert(0, jnp.zeros((h * HEAD_DIM, x.shape[1]), BF16))
        if (h + 1) * HEAD_DIM < width:
            rows.append(jnp.zeros((width - (h + 1) * HEAD_DIM, x.shape[1]), BF16))
        columns.append(jnp.concatenate(rows, axis=0))
    return jnp.concatenate(columns, axis=1)


def own_head(x):
    return jnp.concatenate(
        [
            x[h * HEAD_DIM : (h + 1) * HEAD_DIM, h * PAIR : (h + 1) * PAIR]
            for h in range(x.shape[0] // HEAD_DIM)
        ],
        axis=0,
    )


def head_sums(x):
    return jnp.concatenate(
        [
            jnp.sum(x[h * HEAD_DIM : (h + 1) * HEAD_DIM], axis=0, keepdims=True)
            for h in range(x.shape[0] // HEAD_DIM)
        ],
        axis=1,
    )


def top_of(x):
    return jnp.max(x, axis=0, keepdims=True)


def total_of(x):
    return jnp.sum(x, axis=0, keepdims=True)


def second_half(lanes):
    return lax.broadcasted_iota(jnp.int32, (1, lanes), 1) % PAIR >= BLOCK


def global_scores(rows, qm):
    shape = (rows.shape[0], qm.shape[1])
    is_key = lax.broadcasted_iota(jnp.int32, shape, 0) % (2 * SUM_DEV) < SUM_DEV
    return jnp.where(is_key, mm(rows, qm), LOW)


def value_rows(rows):
    return pltpu.roll(rows.astype(F32), rows.shape[0] - SUM_DEV, 0).astype(BF16)


def local_kernel(
    first_ref, q_ref, k_ref, v_ref, g_ref, before_ref,
    exp_ref, top_ref, total_ref, qx_ref, gx_ref, kx_ref, vx_ref, kt_ref, vt_ref,
):
    width, tok = q_ref.shape
    for at, t_ref, x_ref, own_ref in ((0, kt_ref, kx_ref, k_ref), (PAIR, vt_ref, vx_ref, v_ref)):
        t_ref[:, :PAIR] = before_ref[:, at : at + PAIR]
        t_ref[:, PAIR:] = own_ref[...]
        x_ref[:PAIR] = before_ref[:, at : at + PAIR].T
        x_ref[PAIR:] = own_ref[...].T
    for at, x_ref, own_ref in ((2 * PAIR, qx_ref, q_ref), (2 * PAIR + BLOCK, gx_ref, g_ref)):
        x_ref[...] = jnp.concatenate(
            [before_ref[:, at : at + BLOCK], own_ref[:, : tok - BLOCK]], axis=1
        )
    second = second_half(width // HEAD_DIM * PAIR)
    is_first = first_ref[0] == 1
    for p in range(tok // PAIR):
        s = mm(kx_ref[p * PAIR : (p + 2) * PAIR], by_head(qx_ref[:, p * PAIR : (p + 1) * PAIR]))
        parts = [s[b * BLOCK : (b + 1) * BLOCK] for b in range(4)]
        parts[0] += jnp.where(second, LOW, 0.0)
        if p == 0:
            parts[1] += jnp.where(jnp.logical_and(is_first, second), LOW, 0.0)
            parts[2] += jnp.where(jnp.logical_and(is_first, jnp.logical_not(second)), LOW, 0.0)
        parts[3] += jnp.where(second, 0.0, LOW)
        s = jnp.concatenate(parts, axis=0)
        top = top_of(s)
        s = jnp.exp(s - top)
        exp_ref[p] = s
        top_ref[p] = top
        total_ref[p] = total_of(s)


def global_kernel(
    qx_ref, gx_ref, vt_ref, rows_ref, exp_ref, top_ref, total_ref,
    att_ref, part_ref, ds_ref, factor_ref, delta_ref,
):
    rows = rows_ref[...]
    values_g = value_rows(rows)
    values_gt = values_g.T
    part = jnp.zeros(part_ref.shape, F32)
    for p in range(qx_ref.shape[1] // PAIR):
        own = slice(p * PAIR, (p + 1) * PAIR)
        g = gx_ref[:, own]
        qm, gm = by_head(qx_ref[:, own]), by_head(g)
        s = global_scores(rows, qm)
        local_top = top_ref[p]
        top = jnp.maximum(local_top, top_of(s))
        s = jnp.exp(s - top)
        factor = jnp.exp(local_top - top)
        inverse = 1.0 / (total_ref[p] * factor + total_of(s))
        factor = factor * inverse
        w = s * inverse
        probs = (exp_ref[p] * factor).astype(BF16)
        att = mm(vt_ref[:, p * PAIR : (p + 2) * PAIR], probs) + mm(values_gt, w.astype(BF16))
        att = own_head(att).astype(BF16)
        att_ref[:, own] = att
        delta = head_sums(g.astype(F32) * att.astype(F32)) * SCALE
        ds = (w * (mm(values_g, gm) - delta)).astype(BF16)
        part += mm_nt(ds, qm) + mm_nt(pltpu.roll(w, SUM_DEV, 0).astype(BF16), gm)
        ds_ref[p] = ds
        factor_ref[p] = factor
        delta_ref[p] = delta
    part_ref[...] = part * (1.0 / SCALE)


def gradient_kernel(
    qx_ref, gx_ref, kt_ref, vx_ref, rows_ref, exp_ref, att_ref, ds_ref, factor_ref, delta_ref,
    qg_ref, kg_ref, vg_ref, back_ref,
):
    width, tok = kg_ref.shape
    pairs = tok // PAIR
    rows_t = rows_ref[...].T

    def pair(p):
        own = slice(p * PAIR, (p + 1) * PAIR)
        near = slice(p * PAIR, (p + 2) * PAIR)
        qm, gm = by_head(qx_ref[:, own]), by_head(gx_ref[:, own])
        w = exp_ref[p] * factor_ref[p]
        ds = (w * (mm(vx_ref[near], gm) - delta_ref[p])).astype(BF16)
        qg = own_head(mm(kt_ref[:, near], ds) + mm(rows_t, ds_ref[p])).astype(BF16)
        qg_ref[:, own] = qg
        kg = mm_nt(qm, ds) * (1.0 / SCALE)
        vg = mm_nt(gm, w.astype(BF16)) * (1.0 / SCALE)
        return qg, kg, vg

    grads = [pair(p) for p in range(pairs)]
    back_ref[:, 2 * PAIR :] = jnp.concatenate(
        [att_ref[:, :BLOCK], grads[0][0][:, :BLOCK]], axis=1
    )
    for at, i, ref in ((0, 1, kg_ref), (PAIR, 2, vg_ref)):
        back_ref[:, at : at + PAIR] = grads[0][i][:, :PAIR].astype(BF16)
        for p in range(pairs - 1):
            ref[:, p * PAIR : (p + 1) * PAIR] = grads[p][i][:, PAIR:] + grads[p + 1][i][:, :PAIR]
        ref[:, tok - PAIR :] = grads[-1][i][:, PAIR:]


def owned_kernel(parts_ref, k_ref, v_ref, owned_ref, term_ref):
    owned = jnp.sum(parts_ref[...], axis=0)
    owned_ref[...] = owned
    split = pieces(owned)
    n = 2 * SUM_DEV
    seg = k_ref.shape[1] // SUM_DEV
    total = jnp.zeros((1, k_ref.shape[1]), F32)
    for first, ref in ((0, k_ref), (SUM_DEV, v_ref)):
        met = mm(split, ref[...])
        met = met[:n] + met[n : 2 * n] + met[2 * n :]
        met = jnp.where(segment_mask(first, met.shape[0], met.shape[1], seg), met, 0.0)
        total += jnp.sum(met, axis=0, keepdims=True)
    term = total[:, :seg]
    for j in range(1, SUM_DEV):
        term += total[:, j * seg : (j + 1) * seg]
    term_ref[...] = jnp.broadcast_to(term, term_ref.shape)


def finish_kernel(
    owned_ref, kg_ref, vg_ref, w_ref, back_ref, attx_ref, qgx_ref,
    key_ref, value_ref, att_ref, qg_ref,
):
    tok = kg_ref.shape[1]
    columns = owned_ref[...].T
    w = w_ref[...]
    for first, at, grad_ref, out_ref in ((0, 0, kg_ref, key_ref), (SUM_DEV, PAIR, vg_ref, value_ref)):
        pooled = jnp.concatenate(
            [columns[:, first + j : first + j + 1] * w for j in range(SUM_DEV)], axis=1
        )
        total = grad_ref[...] + pooled
        out_ref[:, : tok - PAIR] = total[:, : tok - PAIR].astype(BF16)
        total = total[:, tok - PAIR :] + back_ref[:, at : at + PAIR].astype(F32)
        out_ref[:, tok - PAIR :] = total.astype(BF16)
    for at, x_ref, out_ref in ((0, attx_ref, att_ref), (BLOCK, qgx_ref, qg_ref)):
        edge = back_ref[:, 2 * PAIR + at : 2 * PAIR + at + BLOCK]
        out_ref[...] = jnp.concatenate([x_ref[:, BLOCK:], edge], axis=1)


def shaped(shape, dtype):
    return jax.ShapeDtypeStruct(shape, dtype)


def call(kernel, outs, count, first=VMEM):
    return pl.pallas_call(
        kernel,
        out_shape=outs,
        in_specs=[first] + [VMEM] * (count - 1),
        out_specs=[VMEM] * len(outs),
        compiler_params=PARAMS,
    )


def local(queries, key_states, value_states, pool_weight, out_grad):
    tok, width = queries.shape
    group_index = lax.axis_index("seq")
    groups = lax.axis_size("seq")
    everyone = groups * lax.axis_size("head")
    n = 2 * SUM_DEV
    seg = pool_weight.shape[0]
    pairs, lanes = tok // PAIR, width // HEAD_DIM * PAIR
    halo = shaped((width, 3 * PAIR), BF16)
    own = shaped((width, tok), BF16)
    grad = shaped((width, tok), F32)
    keys = shaped((tok + PAIR, width), BF16)
    keys_t = shaped((width, tok + PAIR), BF16)
    stat = shaped((pairs, 1, lanes), F32)
    up = [(i, (i + 1) % groups) for i in range(groups)]
    down = [(j, i) for i, j in up]
    order = [[(i + groups // 2) % groups for i in range(groups)]]

    def exchange(x):
        x = x.reshape(groups, n, width)
        return lax.all_to_all(x, "seq", split_axis=0, concat_axis=0, axis_index_groups=order)

    arguments = (queries.T, key_states.T, value_states.T, out_grad.T, pool_weight.reshape(1, seg))
    summary, edge, q, k, v, g, weight_row = pl.pallas_call(
        pool_kernel,
        out_shape=[shaped((groups, n, width), BF16), halo] + [own] * 4 + [shaped((1, seg), F32)],
        in_specs=[pl.BlockSpec(memory_space=pltpu.HBM)] * 5,
        out_specs=[VMEM] * 7,
        scratch_shapes=[pltpu.SemaphoreType.DMA((5,))],
        compiler_params=PARAMS,
    )(*[pltpu.with_memory_space_constraint(x, pltpu.HBM) for x in arguments])
    before = lax.ppermute(edge, "seq", up)
    rows = exchange(summary).reshape(groups * n, width)
    is_first = (group_index == 0).astype(jnp.int32).reshape(1)
    exps, top, total, qx, gx, kx, vx, kt, vt = call(
        local_kernel,
        [shaped((pairs, 2 * PAIR, lanes), F32), stat, stat, own, own, keys, keys, keys_t, keys_t],
        6,
        SMEM,
    )(is_first, q, k, v, g, before)

    att_x, part, ds, factor, delta = call(
        global_kernel,
        [own, shaped((groups * n, width), F32), shaped((pairs, groups * n, lanes), BF16), stat, stat],
        7,
    )(qx, gx, vt, rows, exps, top, total)
    parts = exchange(part)
    qg_x, key_part, value_part, edge = call(gradient_kernel, [own, grad, grad, halo], 10)(
        qx, gx, kt, vx, rows, exps, att_x, ds, factor, delta
    )
    back = lax.ppermute(edge, "seq", down)
    parts, qg_x = lax.optimization_barrier((parts, qg_x))
    owned, term = call(owned_kernel, [shaped((n, width), F32), shaped((everyone, seg), F32)], 3)(
        parts, k, v
    )
    terms = lax.all_to_all(term, ("seq", "head"), split_axis=0, concat_axis=0)
    key_grad, value_grad, attended, query_grad = call(finish_kernel, [own] * 4, 7)(
        owned, key_part, value_part, weight_row, back, att_x, qg_x
    )
    return (attended.T, query_grad.T, key_grad.T, value_grad.T, terms.sum(0))


def solution(mesh):
    return jax.shard_map(
        local,
        mesh=mesh,
        in_specs=(P("seq", "head"), P("seq", "head"), P("seq", "head"), P(), P("seq", "head")),
        out_specs=(P("seq", "head"), P("seq", "head"), P("seq", "head"), P("seq", "head"), P()),
        check_vma=False,
    )
```

```python
import functools

import jax
import jax.numpy as jnp
from jax import lax
from jax.experimental import pallas as pl
from jax.experimental.pallas import tpu as pltpu
from jax.sharding import PartitionSpec as P

HEAD_DIM = 64
BLOCK = 64
SUM_DEV = 4
PAIR = 2 * BLOCK
SCALE = HEAD_DIM ** (-0.5)
LOW = -1e30
VMEM = pl.BlockSpec(memory_space=pltpu.VMEM)
SMEM = pl.BlockSpec(memory_space=pltpu.SMEM)
PARAMS = pltpu.CompilerParams(vmem_limit_bytes=40 * 1024 * 1024)
F32 = jnp.float32
BF16 = jnp.bfloat16


def mm(a, b):
    return lax.dot_general(a, b, (((1,), (0,)), ((), ())), preferred_element_type=F32)


def mm_nt(a, b):
    return lax.dot_general(a, b, (((1,), (1,)), ((), ())), preferred_element_type=F32)


def mm_tn(a, b):
    return lax.dot_general(a, b, (((0,), (0,)), ((), ())), preferred_element_type=F32)


def pieces(x):
    high = x.astype(BF16)
    rest = x - high.astype(F32)
    middle = rest.astype(BF16)
    low = (rest - middle.astype(F32)).astype(BF16)
    return jnp.concatenate([high, middle, low], axis=0)


def segment_mask(first, rows, lanes, seg):
    row = lax.broadcasted_iota(jnp.int32, (rows, lanes), 0)
    lane = lax.broadcasted_iota(jnp.int32, (rows, lanes), 1)
    return row - first == lane // seg


def pool_kernel(*refs):
    sources, (rows_ref, up_ref, *kept), sem = refs[:5], refs[5:12], refs[12]
    q_ref, k_ref, v_ref, g_ref, w_ref = kept
    copies = [
        pltpu.make_async_copy(source, target, sem.at[i])
        for i, (source, target) in enumerate(zip(sources, kept))
    ]
    for i in (4, 1, 2, 0, 3):
        copies[i].start()
    for i in (4, 1, 2):
        copies[i].wait()
    seg = w_ref.shape[1]
    n = 2 * SUM_DEV
    w = jnp.concatenate([w_ref[...]] * SUM_DEV, axis=1)
    w = jnp.broadcast_to(w, (n, w.shape[1]))
    pooled = jnp.zeros((n, k_ref.shape[0]), F32)
    for first, ref in ((0, k_ref), (SUM_DEV, v_ref)):
        weights = jnp.where(segment_mask(first, w.shape[0], w.shape[1], seg), w, 0.0)
        parts = mm_nt(pieces(weights), ref[...])
        pooled += parts[:n] + parts[n : 2 * n] + parts[2 * n :]
    rows_ref[...] = jnp.broadcast_to(pooled.astype(BF16)[None], rows_ref.shape)
    copies[0].wait()
    copies[3].wait()
    tok = k_ref.shape[1]
    up_ref[:, :PAIR] = k_ref[:, tok - PAIR :]
    up_ref[:, PAIR : 2 * PAIR] = v_ref[:, tok - PAIR :]
    up_ref[:, 2 * PAIR :] = jnp.concatenate(
        [q_ref[:, tok - BLOCK :], g_ref[:, tok - BLOCK :]], axis=1
    )


def by_head(x):
    width = x.shape[0]
    x = x * jnp.asarray(SCALE, BF16)
    columns = []
    for h in range(width // HEAD_DIM):
        rows = [x[h * HEAD_DIM : (h + 1) * HEAD_DIM]]
        if h:
            rows.insert(0, jnp.zeros((h * HEAD_DIM, x.shape[1]), BF16))
        if (h + 1) * HEAD_DIM < width:
            rows.append(jnp.zeros((width - (h + 1) * HEAD_DIM, x.shape[1]), BF16))
        columns.append(jnp.concatenate(rows, axis=0))
    return jnp.concatenate(columns, axis=1)


def own_head(x):
    return jnp.concatenate(
        [
            x[h * HEAD_DIM : (h + 1) * HEAD_DIM, h * PAIR : (h + 1) * PAIR]
            for h in range(x.shape[0] // HEAD_DIM)
        ],
        axis=0,
    )


def head_sums(x):
    return jnp.concatenate(
        [
            jnp.sum(x[h * HEAD_DIM : (h + 1) * HEAD_DIM], axis=0, keepdims=True)
            for h in range(x.shape[0] // HEAD_DIM)
        ],
        axis=1,
    )


def top_of(x):
    return jnp.max(x, axis=0, keepdims=True)


def total_of(x):
    return jnp.sum(x, axis=0, keepdims=True)


def second_half(lanes):
    return lax.broadcasted_iota(jnp.int32, (1, lanes), 1) % PAIR >= BLOCK


def global_scores(rows, qm):
    shape = (rows.shape[0], qm.shape[1])
    is_key = lax.broadcasted_iota(jnp.int32, shape, 0) % (2 * SUM_DEV) < SUM_DEV
    return jnp.where(is_key, mm(rows, qm), LOW)


def value_rows(rows):
    return pltpu.roll(rows.astype(F32), rows.shape[0] - SUM_DEV, 0).astype(BF16)


def local_kernel(
    first_ref, q_ref, k_ref, v_ref, g_ref, before_ref,
    exp_ref, top_ref, total_ref, qx_ref, gx_ref, kx_ref, vx_ref, kt_ref, vt_ref,
):
    width, tok = q_ref.shape
    for at, t_ref, x_ref, own_ref in ((0, kt_ref, kx_ref, k_ref), (PAIR, vt_ref, vx_ref, v_ref)):
        t_ref[:, :PAIR] = before_ref[:, at : at + PAIR]
        t_ref[:, PAIR:] = own_ref[...]
        x_ref[:PAIR] = before_ref[:, at : at + PAIR].T
        x_ref[PAIR:] = own_ref[...].T
    for at, x_ref, own_ref in ((2 * PAIR, qx_ref, q_ref), (2 * PAIR + BLOCK, gx_ref, g_ref)):
        x_ref[...] = jnp.concatenate(
            [before_ref[:, at : at + BLOCK], own_ref[:, : tok - BLOCK]], axis=1
        )
    second = second_half(width // HEAD_DIM * PAIR)
    is_first = first_ref[0] == 1
    for p in range(tok // PAIR):
        s = mm(kx_ref[p * PAIR : (p + 2) * PAIR], by_head(qx_ref[:, p * PAIR : (p + 1) * PAIR]))
        parts = [s[b * BLOCK : (b + 1) * BLOCK] for b in range(4)]
        parts[0] += jnp.where(second, LOW, 0.0)
        if p == 0:
            parts[1] += jnp.where(jnp.logical_and(is_first, second), LOW, 0.0)
            parts[2] += jnp.where(jnp.logical_and(is_first, jnp.logical_not(second)), LOW, 0.0)
        parts[3] += jnp.where(second, 0.0, LOW)
        s = jnp.concatenate(parts, axis=0)
        top = top_of(s)
        s = jnp.exp(s - top)
        exp_ref[p] = s
        top_ref[p] = top
        total_ref[p] = total_of(s)


def global_kernel(
    qx_ref, gx_ref, vt_ref, rows_ref, exp_ref, top_ref, total_ref,
    att_ref, part_ref, ds_ref, factor_ref, delta_ref,
):
    rows = rows_ref[...]
    values_g = value_rows(rows)
    values_gt = values_g.T
    part_k = jnp.zeros(part_ref.shape, F32)
    part_v = jnp.zeros(part_ref.shape, F32)
    for p in range(qx_ref.shape[1] // PAIR):
        own = slice(p * PAIR, (p + 1) * PAIR)
        g = gx_ref[:, own]
        qm, gm = by_head(qx_ref[:, own]), by_head(g)
        s = global_scores(rows, qm)
        local_top = top_ref[p]
        top = jnp.maximum(local_top, top_of(s))
        s = jnp.exp(s - top)
        factor = jnp.exp(local_top - top)
        inverse = 1.0 / (total_ref[p] * factor + total_of(s))
        factor = factor * inverse
        w = s * inverse
        wb = w.astype(BF16)
        probs = (exp_ref[p] * factor).astype(BF16)
        near = slice(p * PAIR, (p + 2) * PAIR)
        att = []
        for h in range(qx_ref.shape[0] // HEAD_DIM):
            f, c = slice(h * HEAD_DIM, (h + 1) * HEAD_DIM), slice(h * PAIR, (h + 1) * PAIR)
            att.append(mm(vt_ref[f, near], probs[:, c]) + mm(values_gt[f], wb[:, c]))
        att = jnp.concatenate(att, axis=0).astype(BF16)
        att_ref[:, own] = att
        delta = head_sums(g.astype(F32) * att.astype(F32)) * SCALE
        ds = (w * (mm(values_g, gm) - delta)).astype(BF16)
        part_k += mm_nt(ds, qm)
        part_v += mm_nt(wb, gm)
        ds_ref[p] = ds
        factor_ref[p] = factor
        delta_ref[p] = delta
    part_ref[...] = (part_k + pltpu.roll(part_v, SUM_DEV, 0)) * (1.0 / SCALE)


def gradient_kernel(
    qx_ref, gx_ref, kt_ref, vx_ref, rows_ref, exp_ref, att_ref, ds_ref, factor_ref, delta_ref,
    att_out_ref, qg_out_ref, kg_ref, vg_ref, back_ref,
):
    width, tok = kg_ref.shape
    pairs = tok // PAIR
    rows_t = rows_ref[...].T

    def pair(p):
        own = slice(p * PAIR, (p + 1) * PAIR)
        near = slice(p * PAIR, (p + 2) * PAIR)
        qm, gm = by_head(qx_ref[:, own]), by_head(gx_ref[:, own])
        w = exp_ref[p] * factor_ref[p]
        ds = (w * (mm(vx_ref[near], gm) - delta_ref[p])).astype(BF16)
        qg = own_head(mm(kt_ref[:, near], ds) + mm(rows_t, ds_ref[p])).astype(BF16)
        kg = mm_nt(qm, ds) * (1.0 / SCALE)
        vg = mm_nt(gm, w.astype(BF16)) * (1.0 / SCALE)
        return qg, kg, vg

    grads = [pair(p) for p in range(pairs)]
    qg = jnp.concatenate([qg for qg, _, _ in grads], axis=1)
    att = att_ref[...]
    back_ref[:, 2 * PAIR :] = jnp.concatenate([att[:, :BLOCK], qg[:, :BLOCK]], axis=1)
    for x, ref in ((att, att_out_ref), (qg, qg_out_ref)):
        ref[...] = jnp.concatenate([x[:, BLOCK:], x[:, :BLOCK]], axis=1)
    for at, i, ref in ((0, 1, kg_ref), (PAIR, 2, vg_ref)):
        back_ref[:, at : at + PAIR] = grads[0][i][:, :PAIR].astype(BF16)
        for p in range(pairs - 1):
            ref[:, p * PAIR : (p + 1) * PAIR] = grads[p][i][:, PAIR:] + grads[p + 1][i][:, :PAIR]
        ref[:, tok - PAIR :] = grads[-1][i][:, PAIR:]


def owned_kernel(parts_ref, k_ref, v_ref, owned_ref, term_ref):
    owned = jnp.sum(parts_ref[...], axis=0)
    owned_ref[...] = owned
    split = pieces(owned)
    n = 2 * SUM_DEV
    seg = k_ref.shape[1] // SUM_DEV
    total = jnp.zeros((1, k_ref.shape[1]), F32)
    for first, ref in ((0, k_ref), (SUM_DEV, v_ref)):
        met = mm(split, ref[...])
        met = met[:n] + met[n : 2 * n] + met[2 * n :]
        met = jnp.where(segment_mask(first, met.shape[0], met.shape[1], seg), met, 0.0)
        total += jnp.sum(met, axis=0, keepdims=True)
    term = total[:, :seg]
    for j in range(1, SUM_DEV):
        term += total[:, j * seg : (j + 1) * seg]
    term_ref[...] = jnp.broadcast_to(term, term_ref.shape)


def sum_kernel(terms_ref, sum_ref):
    sum_ref[...] = jnp.sum(terms_ref[...], axis=0, keepdims=True)


def outer(rows, weights):
    n = rows.shape[0]
    a, b = pieces(rows), pieces(weights)
    a = [a[i * n : (i + 1) * n] for i in (0, 0, 1, 0, 1, 2)]
    b = [b[i * n : (i + 1) * n] for i in (0, 1, 0, 2, 1, 0)]
    return mm_tn(jnp.concatenate(a, axis=0), jnp.concatenate(b, axis=0))


def finish_kernel(
    owned_ref, kg_ref, vg_ref, w_ref, back_ref, atts_ref, qgs_ref, pool_ref,
    key_out, value_out, att_out, qg_out, pool_out, key_ref, value_ref, att_ref, qg_ref, sem,
):
    copies = []

    def send(ref, out):
        copies.append(pltpu.make_async_copy(ref, out, sem.at[len(copies)]))
        copies[-1].start()

    tok = kg_ref.shape[1]
    low, high = slice(0, tok - PAIR), slice(tok - PAIR, tok)
    send(pool_ref, pool_out)
    for at, x_ref, ref, out in (
        (0, atts_ref, att_ref, att_out),
        (BLOCK, qgs_ref, qg_ref, qg_out),
    ):
        send(x_ref.at[:, low], out.at[:, low])
        edge = back_ref[:, 2 * PAIR + at : 2 * PAIR + at + BLOCK]
        ref[...] = jnp.concatenate([x_ref[:, tok - PAIR : tok - BLOCK], edge], axis=1)
        send(ref, out.at[:, high])
    owned = owned_ref[...]
    w = jnp.concatenate([w_ref[...]] * SUM_DEV, axis=1)
    w = jnp.broadcast_to(w, (owned.shape[0], tok))
    for first, at, grad_ref, ref, out in (
        (0, 0, kg_ref, key_ref, key_out),
        (SUM_DEV, PAIR, vg_ref, value_ref, value_out),
    ):
        weights = jnp.where(segment_mask(first, w.shape[0], tok, w_ref.shape[1]), w, 0.0)
        total = grad_ref[...] + outer(owned, weights)
        ref[:, low] = total[:, low].astype(BF16)
        ref[:, high] = (total[:, high] + back_ref[:, at : at + PAIR].astype(F32)).astype(BF16)
        send(ref, out)
    for copy in copies:
        copy.wait()


def shaped(shape, dtype):
    return jax.ShapeDtypeStruct(shape, dtype)


def call(kernel, outs, count, first=VMEM):
    return pl.pallas_call(
        kernel,
        out_shape=outs,
        in_specs=[first] + [VMEM] * (count - 1),
        out_specs=[VMEM] * len(outs),
        compiler_params=PARAMS,
    )


def local(queries, key_states, value_states, pool_weight, out_grad):
    tok, width = queries.shape
    group_index = lax.axis_index("seq")
    groups = lax.axis_size("seq")
    everyone = groups * lax.axis_size("head")
    n = 2 * SUM_DEV
    seg = pool_weight.shape[0]
    pairs, lanes = tok // PAIR, width // HEAD_DIM * PAIR
    halo = shaped((width, 3 * PAIR), BF16)
    own = shaped((width, tok), BF16)
    grad = shaped((width, tok), F32)
    keys = shaped((tok + PAIR, width), BF16)
    keys_t = shaped((width, tok + PAIR), BF16)
    stat = shaped((pairs, 1, lanes), F32)
    up = [(i, (i + 1) % groups) for i in range(groups)]
    down = [(j, i) for i, j in up]
    quarter = groups // 4
    order = [[part * quarter + i for part in (2, 3, 1, 0) for i in range(quarter)]]

    def exchange(x):
        x = x.reshape(groups, n, width)
        return lax.all_to_all(x, "seq", split_axis=0, concat_axis=0, axis_index_groups=order)

    arguments = (queries.T, key_states.T, value_states.T, out_grad.T, pool_weight.reshape(1, seg))
    summary, edge, q, k, v, g, weight_row = pl.pallas_call(
        pool_kernel,
        out_shape=[shaped((groups, n, width), BF16), halo] + [own] * 4 + [shaped((1, seg), F32)],
        in_specs=[pl.BlockSpec(memory_space=pltpu.HBM)] * 5,
        out_specs=[VMEM] * 7,
        scratch_shapes=[pltpu.SemaphoreType.DMA((5,))],
        compiler_params=PARAMS,
    )(*[pltpu.with_memory_space_constraint(x, pltpu.HBM) for x in arguments])
    before = lax.ppermute(edge, "seq", up)
    rows = exchange(summary).reshape(groups * n, width)
    is_first = (group_index == 0).astype(jnp.int32).reshape(1)
    exps, top, total, qx, gx, kx, vx, kt, vt = call(
        local_kernel,
        [shaped((pairs, 2 * PAIR, lanes), F32), stat, stat, own, own, keys, keys, keys_t, keys_t],
        6,
        SMEM,
    )(is_first, q, k, v, g, before)

    att_x, part, ds, factor, delta = call(
        global_kernel,
        [own, shaped((groups * n, width), F32), shaped((pairs, groups * n, lanes), BF16), stat, stat],
        7,
    )(qx, gx, vt, rows, exps, top, total)
    parts = exchange(part)
    att_own, qg_own, key_part, value_part, edge = call(
        gradient_kernel, [own, own, grad, grad, halo], 10
    )(
        qx, gx, kt, vx, rows, exps, att_x, ds, factor, delta
    )
    back = lax.ppermute(edge, "seq", down)
    parts, qg_own = lax.optimization_barrier((parts, qg_own))
    owned, term = call(owned_kernel, [shaped((n, width), F32), shaped((everyone, seg), F32)], 3)(
        parts, k, v
    )
    terms = lax.all_to_all(term, ("seq", "head"), split_axis=0, concat_axis=0)
    (pool_sum,) = call(sum_kernel, [shaped((1, seg), F32)], 1)(terms)
    key_grad, value_grad, attended, query_grad, pool_grad = pl.pallas_call(
        finish_kernel,
        out_shape=[own] * 4 + [shaped((1, seg), F32)],
        in_specs=[VMEM] * 8,
        out_specs=[pl.BlockSpec(memory_space=pltpu.HBM)] * 5,
        scratch_shapes=[pltpu.VMEM((width, tok), BF16)] * 2
        + [pltpu.VMEM((width, PAIR), BF16)] * 2
        + [pltpu.SemaphoreType.DMA((7,))],
        compiler_params=PARAMS,
    )(owned, key_part, value_part, weight_row, back, att_own, qg_own, pool_sum)
    return (attended.T, query_grad.T, key_grad.T, value_grad.T, pool_grad.reshape(seg))


def solution(mesh):
    return jax.shard_map(
        local,
        mesh=mesh,
        in_specs=(P("seq", "head"), P("seq", "head"), P("seq", "head"), P(), P("seq", "head")),
        out_specs=(P("seq", "head"), P("seq", "head"), P("seq", "head"), P("seq", "head"), P()),
        check_vma=False,
    )
```

```python
import functools

import jax
import jax.numpy as jnp
from jax import lax
from jax.experimental import pallas as pl
from jax.experimental.pallas import tpu as pltpu
from jax.sharding import PartitionSpec as P

HEAD_DIM = 64
BLOCK = 64
SUM_DEV = 4
PAIR = 2 * BLOCK
SCALE = HEAD_DIM ** (-0.5)
LOW = -1e30
VMEM = pl.BlockSpec(memory_space=pltpu.VMEM)
SMEM = pl.BlockSpec(memory_space=pltpu.SMEM)
PARAMS = pltpu.CompilerParams(vmem_limit_bytes=40 * 1024 * 1024)
F32 = jnp.float32
BF16 = jnp.bfloat16


def mm(a, b):
    return lax.dot_general(a, b, (((1,), (0,)), ((), ())), preferred_element_type=F32)


def mm_nt(a, b):
    return lax.dot_general(a, b, (((1,), (1,)), ((), ())), preferred_element_type=F32)


def mm_tn(a, b):
    return lax.dot_general(a, b, (((0,), (0,)), ((), ())), preferred_element_type=F32)


def pieces(x):
    high = x.astype(BF16)
    rest = x - high.astype(F32)
    middle = rest.astype(BF16)
    low = (rest - middle.astype(F32)).astype(BF16)
    return jnp.concatenate([high, middle, low], axis=0)


def segment_mask(first, rows, lanes, seg):
    row = lax.broadcasted_iota(jnp.int32, (rows, lanes), 0)
    lane = lax.broadcasted_iota(jnp.int32, (rows, lanes), 1)
    return row - first == lane // seg


def pool_kernel(*refs):
    sources, (rows_ref, up_ref, *kept), sem = refs[:5], refs[5:12], refs[12]
    q_ref, k_ref, v_ref, g_ref, w_ref = kept
    copies = [
        pltpu.make_async_copy(source, target, sem.at[i])
        for i, (source, target) in enumerate(zip(sources, kept))
    ]
    for i in (4, 1, 2, 0, 3):
        copies[i].start()
    for i in (4, 1, 2):
        copies[i].wait()
    seg = w_ref.shape[1]
    n = 2 * SUM_DEV
    w = jnp.concatenate([w_ref[...]] * SUM_DEV, axis=1)
    w = jnp.broadcast_to(w, (n, w.shape[1]))
    pooled = jnp.zeros((n, k_ref.shape[0]), F32)
    for first, ref in ((0, k_ref), (SUM_DEV, v_ref)):
        weights = jnp.where(segment_mask(first, w.shape[0], w.shape[1], seg), w, 0.0)
        parts = mm_nt(pieces(weights), ref[...])
        pooled += parts[:n] + parts[n : 2 * n] + parts[2 * n :]
    rows_ref[...] = jnp.broadcast_to(pooled.astype(BF16)[None], rows_ref.shape)
    copies[0].wait()
    copies[3].wait()
    tok = k_ref.shape[1]
    up_ref[:, :PAIR] = k_ref[:, tok - PAIR :]
    up_ref[:, PAIR : 2 * PAIR] = v_ref[:, tok - PAIR :]
    up_ref[:, 2 * PAIR :] = jnp.concatenate(
        [q_ref[:, tok - BLOCK :], g_ref[:, tok - BLOCK :]], axis=1
    )


def by_head(x):
    width = x.shape[0]
    x = x * jnp.asarray(SCALE, BF16)
    columns = []
    for h in range(width // HEAD_DIM):
        rows = [x[h * HEAD_DIM : (h + 1) * HEAD_DIM]]
        if h:
            rows.insert(0, jnp.zeros((h * HEAD_DIM, x.shape[1]), BF16))
        if (h + 1) * HEAD_DIM < width:
            rows.append(jnp.zeros((width - (h + 1) * HEAD_DIM, x.shape[1]), BF16))
        columns.append(jnp.concatenate(rows, axis=0))
    return jnp.concatenate(columns, axis=1)


def own_head(x):
    return jnp.concatenate(
        [
            x[h * HEAD_DIM : (h + 1) * HEAD_DIM, h * PAIR : (h + 1) * PAIR]
            for h in range(x.shape[0] // HEAD_DIM)
        ],
        axis=0,
    )


def head_sums(x):
    return jnp.concatenate(
        [
            jnp.sum(x[h * HEAD_DIM : (h + 1) * HEAD_DIM], axis=0, keepdims=True)
            for h in range(x.shape[0] // HEAD_DIM)
        ],
        axis=1,
    )


def top_of(x):
    return jnp.max(x, axis=0, keepdims=True)


def total_of(x):
    return jnp.sum(x, axis=0, keepdims=True)


def second_half(lanes):
    return lax.broadcasted_iota(jnp.int32, (1, lanes), 1) % PAIR >= BLOCK


def global_scores(rows, qm):
    shape = (rows.shape[0], qm.shape[1])
    is_key = lax.broadcasted_iota(jnp.int32, shape, 0) % (2 * SUM_DEV) < SUM_DEV
    return jnp.where(is_key, mm(rows, qm), LOW)


def value_rows(rows):
    return pltpu.roll(rows.astype(F32), rows.shape[0] - SUM_DEV, 0).astype(BF16)


def local_kernel(
    first_ref, q_ref, k_ref, v_ref, g_ref, before_ref,
    exp_ref, top_ref, total_ref, qx_ref, gx_ref, kx_ref, vx_ref, kt_ref, vt_ref,
):
    width, tok = q_ref.shape
    for at, t_ref, x_ref, own_ref in ((0, kt_ref, kx_ref, k_ref), (PAIR, vt_ref, vx_ref, v_ref)):
        t_ref[:, :PAIR] = before_ref[:, at : at + PAIR]
        t_ref[:, PAIR:] = own_ref[...]
        x_ref[:PAIR] = before_ref[:, at : at + PAIR].T
        x_ref[PAIR:] = own_ref[...].T
    for at, x_ref, own_ref in ((2 * PAIR, qx_ref, q_ref), (2 * PAIR + BLOCK, gx_ref, g_ref)):
        x_ref[...] = jnp.concatenate(
            [before_ref[:, at : at + BLOCK], own_ref[:, : tok - BLOCK]], axis=1
        )
    second = second_half(width // HEAD_DIM * PAIR)
    is_first = first_ref[0] == 1
    for p in range(tok // PAIR):
        s = mm(kx_ref[p * PAIR : (p + 2) * PAIR], by_head(qx_ref[:, p * PAIR : (p + 1) * PAIR]))
        parts = [s[b * BLOCK : (b + 1) * BLOCK] for b in range(4)]
        parts[0] += jnp.where(second, LOW, 0.0)
        if p == 0:
            parts[1] += jnp.where(jnp.logical_and(is_first, second), LOW, 0.0)
            parts[2] += jnp.where(jnp.logical_and(is_first, jnp.logical_not(second)), LOW, 0.0)
        parts[3] += jnp.where(second, 0.0, LOW)
        s = jnp.concatenate(parts, axis=0)
        top = top_of(s)
        s = jnp.exp(s - top)
        exp_ref[p] = s
        top_ref[p] = top
        total_ref[p] = total_of(s)


def global_kernel(
    qx_ref, gx_ref, vt_ref, rows_ref, exp_ref, top_ref, total_ref,
    att_ref, part_ref, ds_ref, factor_ref, delta_ref,
):
    rows = rows_ref[...]
    values_g = value_rows(rows)
    values_gt = values_g.T
    part_k = jnp.zeros(part_ref.shape, F32)
    part_v = jnp.zeros(part_ref.shape, F32)
    for p in range(qx_ref.shape[1] // PAIR):
        own = slice(p * PAIR, (p + 1) * PAIR)
        g = gx_ref[:, own]
        qm, gm = by_head(qx_ref[:, own]), by_head(g)
        s = global_scores(rows, qm)
        local_top = top_ref[p]
        top = jnp.maximum(local_top, top_of(s))
        s = jnp.exp(s - top)
        factor = jnp.exp(local_top - top)
        inverse = 1.0 / (total_ref[p] * factor + total_of(s))
        factor = factor * inverse
        w = s * inverse
        wb = w.astype(BF16)
        probs = (exp_ref[p] * factor).astype(BF16)
        near = slice(p * PAIR, (p + 2) * PAIR)
        att = []
        for h in range(qx_ref.shape[0] // HEAD_DIM):
            f, c = slice(h * HEAD_DIM, (h + 1) * HEAD_DIM), slice(h * PAIR, (h + 1) * PAIR)
            att.append(mm(vt_ref[f, near], probs[:, c]) + mm(values_gt[f], wb[:, c]))
        att = jnp.concatenate(att, axis=0).astype(BF16)
        att_ref[:, own] = att
        delta = head_sums(g.astype(F32) * att.astype(F32)) * SCALE
        ds = (w * (mm(values_g, gm) - delta)).astype(BF16)
        part_k += mm_nt(ds, qm)
        part_v += mm_nt(wb, gm)
        ds_ref[p] = ds
        factor_ref[p] = factor
        delta_ref[p] = delta
    part_ref[...] = (part_k + pltpu.roll(part_v, SUM_DEV, 0)) * (1.0 / SCALE)


def gradient_kernel(
    qx_ref, gx_ref, kt_ref, vx_ref, rows_ref, exp_ref, att_ref, ds_ref, factor_ref, delta_ref,
    att_out_ref, qg_out_ref, kg_ref, vg_ref, back_ref,
):
    width, tok = kg_ref.shape
    pairs = tok // PAIR
    rows_t = rows_ref[...].T

    def pair(p):
        own = slice(p * PAIR, (p + 1) * PAIR)
        near = slice(p * PAIR, (p + 2) * PAIR)
        qm, gm = by_head(qx_ref[:, own]), by_head(gx_ref[:, own])
        w = exp_ref[p] * factor_ref[p]
        ds = (w * (mm(vx_ref[near], gm) - delta_ref[p])).astype(BF16)
        qg = own_head(mm(kt_ref[:, near], ds) + mm(rows_t, ds_ref[p])).astype(BF16)
        kg = mm_nt(qm, ds) * (1.0 / SCALE)
        vg = mm_nt(gm, w.astype(BF16)) * (1.0 / SCALE)
        return qg, kg, vg

    grads = [pair(p) for p in range(pairs)]
    qg = jnp.concatenate([qg for qg, _, _ in grads], axis=1)
    att = att_ref[...]
    back_ref[:, 2 * PAIR :] = jnp.concatenate([att[:, :BLOCK], qg[:, :BLOCK]], axis=1)
    for x, ref in ((att, att_out_ref), (qg, qg_out_ref)):
        ref[...] = jnp.concatenate([x[:, BLOCK:], x[:, :BLOCK]], axis=1)
    for at, i, ref in ((0, 1, kg_ref), (PAIR, 2, vg_ref)):
        back_ref[:, at : at + PAIR] = grads[0][i][:, :PAIR].astype(BF16)
        for p in range(pairs - 1):
            ref[:, p * PAIR : (p + 1) * PAIR] = grads[p][i][:, PAIR:] + grads[p + 1][i][:, :PAIR]
        ref[:, tok - PAIR :] = grads[-1][i][:, PAIR:]


def owned_kernel(parts_ref, k_ref, v_ref, owned_ref, term_ref):
    owned = jnp.sum(parts_ref[...], axis=0)
    owned_ref[...] = owned
    split = pieces(owned)
    n = 2 * SUM_DEV
    seg = k_ref.shape[1] // SUM_DEV
    total = jnp.zeros((1, k_ref.shape[1]), F32)
    for first, ref in ((0, k_ref), (SUM_DEV, v_ref)):
        met = mm(split, ref[...])
        met = met[:n] + met[n : 2 * n] + met[2 * n :]
        met = jnp.where(segment_mask(first, met.shape[0], met.shape[1], seg), met, 0.0)
        total += jnp.sum(met, axis=0, keepdims=True)
    term = total[:, :seg]
    for j in range(1, SUM_DEV):
        term += total[:, j * seg : (j + 1) * seg]
    term_ref[...] = jnp.broadcast_to(term, term_ref.shape)


def sum_kernel(terms_ref, sum_ref):
    sum_ref[...] = jnp.sum(terms_ref[...], axis=0, keepdims=True)


def outer(rows, weights):
    n = rows.shape[0]
    a, b = pieces(rows), pieces(weights)
    a = [a[i * n : (i + 1) * n] for i in (0, 0, 1, 0, 1, 2)]
    b = [b[i * n : (i + 1) * n] for i in (0, 1, 0, 2, 1, 0)]
    return mm_tn(jnp.concatenate(a, axis=0), jnp.concatenate(b, axis=0))


def finish_kernel(
    owned_ref, kg_ref, vg_ref, w_ref, back_ref, atts_ref, qgs_ref, pool_ref,
    key_out, value_out, att_out, qg_out, pool_out, key_ref, value_ref, att_ref, qg_ref, sem,
):
    copies = []

    def send(ref, out):
        copies.append(pltpu.make_async_copy(ref, out, sem.at[len(copies)]))
        copies[-1].start()

    tok = kg_ref.shape[1]
    low, high = slice(0, tok - PAIR), slice(tok - PAIR, tok)
    send(pool_ref, pool_out)
    for at, x_ref, ref, out in (
        (0, atts_ref, att_ref, att_out),
        (BLOCK, qgs_ref, qg_ref, qg_out),
    ):
        send(x_ref.at[:, low], out.at[:, low])
        edge = back_ref[:, 2 * PAIR + at : 2 * PAIR + at + BLOCK]
        ref[...] = jnp.concatenate([x_ref[:, tok - PAIR : tok - BLOCK], edge], axis=1)
        send(ref, out.at[:, high])
    owned = owned_ref[...]
    w = jnp.concatenate([w_ref[...]] * SUM_DEV, axis=1)
    w = jnp.broadcast_to(w, (owned.shape[0], tok))
    for first, at, grad_ref, ref, out in (
        (0, 0, kg_ref, key_ref, key_out),
        (SUM_DEV, PAIR, vg_ref, value_ref, value_out),
    ):
        weights = jnp.where(segment_mask(first, w.shape[0], tok, w_ref.shape[1]), w, 0.0)
        total = grad_ref[...] + outer(owned, weights)
        ref[:, low] = total[:, low].astype(BF16)
        ref[:, high] = (total[:, high] + back_ref[:, at : at + PAIR].astype(F32)).astype(BF16)
        send(ref, out)
    for copy in copies:
        copy.wait()


def shaped(shape, dtype):
    return jax.ShapeDtypeStruct(shape, dtype)


def call(kernel, outs, count, first=VMEM):
    return pl.pallas_call(
        kernel,
        out_shape=outs,
        in_specs=[first] + [VMEM] * (count - 1),
        out_specs=[VMEM] * len(outs),
        compiler_params=PARAMS,
    )


def local(queries, key_states, value_states, pool_weight, out_grad):
    tok, width = queries.shape
    group_index = lax.axis_index("seq")
    groups = lax.axis_size("seq")
    everyone = groups * lax.axis_size("head")
    n = 2 * SUM_DEV
    seg = pool_weight.shape[0]
    pairs, lanes = tok // PAIR, width // HEAD_DIM * PAIR
    halo = shaped((width, 3 * PAIR), BF16)
    own = shaped((width, tok), BF16)
    grad = shaped((width, tok), F32)
    keys = shaped((tok + PAIR, width), BF16)
    keys_t = shaped((width, tok + PAIR), BF16)
    stat = shaped((pairs, 1, lanes), F32)
    up = [(i, (i + 1) % groups) for i in range(groups)]
    down = [(j, i) for i, j in up]
    half = groups // 2
    order = [[*range(half, groups), *range(half)[::-1]]]

    def exchange(x):
        x = x.reshape(groups, n, width)
        return lax.all_to_all(x, "seq", split_axis=0, concat_axis=0, axis_index_groups=order)

    arguments = (queries.T, key_states.T, value_states.T, out_grad.T, pool_weight.reshape(1, seg))
    summary, edge, q, k, v, g, weight_row = pl.pallas_call(
        pool_kernel,
        out_shape=[shaped((groups, n, width), BF16), halo] + [own] * 4 + [shaped((1, seg), F32)],
        in_specs=[pl.BlockSpec(memory_space=pltpu.HBM)] * 5,
        out_specs=[VMEM] * 7,
        scratch_shapes=[pltpu.SemaphoreType.DMA((5,))],
        compiler_params=PARAMS,
    )(*[pltpu.with_memory_space_constraint(x, pltpu.HBM) for x in arguments])
    before = lax.ppermute(edge, "seq", up)
    rows = exchange(summary).reshape(groups * n, width)
    is_first = (group_index == 0).astype(jnp.int32).reshape(1)
    exps, top, total, qx, gx, kx, vx, kt, vt = call(
        local_kernel,
        [shaped((pairs, 2 * PAIR, lanes), F32), stat, stat, own, own, keys, keys, keys_t, keys_t],
        6,
        SMEM,
    )(is_first, q, k, v, g, before)

    att_x, part, ds, factor, delta = call(
        global_kernel,
        [own, shaped((groups * n, width), F32), shaped((pairs, groups * n, lanes), BF16), stat, stat],
        7,
    )(qx, gx, vt, rows, exps, top, total)
    parts = exchange(part)
    att_own, qg_own, key_part, value_part, edge = call(
        gradient_kernel, [own, own, grad, grad, halo], 10
    )(
        qx, gx, kt, vx, rows, exps, att_x, ds, factor, delta
    )
    back = lax.ppermute(edge, "seq", down)
    parts, qg_own = lax.optimization_barrier((parts, qg_own))
    owned, term = call(owned_kernel, [shaped((n, width), F32), shaped((everyone, seg), F32)], 3)(
        parts, k, v
    )
    terms = lax.all_to_all(term, ("seq", "head"), split_axis=0, concat_axis=0)
    (pool_sum,) = call(sum_kernel, [shaped((1, seg), F32)], 1)(terms)
    key_grad, value_grad, attended, query_grad, pool_grad = pl.pallas_call(
        finish_kernel,
        out_shape=[own] * 4 + [shaped((1, seg), F32)],
        in_specs=[VMEM] * 8,
        out_specs=[pl.BlockSpec(memory_space=pltpu.HBM)] * 5,
        scratch_shapes=[pltpu.VMEM((width, tok), BF16)] * 2
        + [pltpu.VMEM((width, PAIR), BF16)] * 2
        + [pltpu.SemaphoreType.DMA((7,))],
        compiler_params=PARAMS,
    )(owned, key_part, value_part, weight_row, back, att_own, qg_own, pool_sum)
    return (attended.T, query_grad.T, key_grad.T, value_grad.T, pool_grad.reshape(seg))


def solution(mesh):
    return jax.shard_map(
        local,
        mesh=mesh,
        in_specs=(P("seq", "head"), P("seq", "head"), P("seq", "head"), P(), P("seq", "head")),
        out_specs=(P("seq", "head"), P("seq", "head"), P("seq", "head"), P("seq", "head"), P()),
        check_vma=False,
    )
```

```python
import functools

import jax
import jax.numpy as jnp
from jax import lax
from jax.experimental import pallas as pl
from jax.experimental.pallas import tpu as pltpu
from jax.sharding import PartitionSpec as P

HEAD_DIM = 64
BLOCK = 64
SUM_DEV = 4
PAIR = 2 * BLOCK
SCALE = HEAD_DIM ** (-0.5)
LOW = -1e30
VMEM = pl.BlockSpec(memory_space=pltpu.VMEM)
SMEM = pl.BlockSpec(memory_space=pltpu.SMEM)
PARAMS = pltpu.CompilerParams(vmem_limit_bytes=40 * 1024 * 1024)
F32 = jnp.float32
BF16 = jnp.bfloat16


def mm(a, b):
    return lax.dot_general(a, b, (((1,), (0,)), ((), ())), preferred_element_type=F32)


def mm_nt(a, b):
    return lax.dot_general(a, b, (((1,), (1,)), ((), ())), preferred_element_type=F32)


def mm_tn(a, b):
    return lax.dot_general(a, b, (((0,), (0,)), ((), ())), preferred_element_type=F32)


def pieces(x):
    high = x.astype(BF16)
    rest = x - high.astype(F32)
    middle = rest.astype(BF16)
    low = (rest - middle.astype(F32)).astype(BF16)
    return jnp.concatenate([high, middle, low], axis=0)


def segment_mask(first, rows, lanes, seg):
    row = lax.broadcasted_iota(jnp.int32, (rows, lanes), 0)
    lane = lax.broadcasted_iota(jnp.int32, (rows, lanes), 1)
    return row - first == lane // seg


def pool_kernel(*refs):
    sources, (rows_ref, up_ref, *kept), sem = refs[:5], refs[5:12], refs[12]
    q_ref, k_ref, v_ref, g_ref, w_ref = kept
    copies = [
        pltpu.make_async_copy(source, target, sem.at[i])
        for i, (source, target) in enumerate(zip(sources, kept))
    ]
    for i in (4, 1, 2, 0, 3):
        copies[i].start()
    for i in (4, 1, 2):
        copies[i].wait()
    seg = w_ref.shape[1]
    n = 2 * SUM_DEV
    w = jnp.concatenate([w_ref[...]] * SUM_DEV, axis=1)
    w = jnp.broadcast_to(w, (n, w.shape[1]))
    pooled = jnp.zeros((n, k_ref.shape[0]), F32)
    for first, ref in ((0, k_ref), (SUM_DEV, v_ref)):
        weights = jnp.where(segment_mask(first, w.shape[0], w.shape[1], seg), w, 0.0)
        parts = mm_nt(pieces(weights), ref[...])
        pooled += parts[:n] + parts[n : 2 * n] + parts[2 * n :]
    rows_ref[...] = jnp.broadcast_to(pooled.astype(BF16)[None], rows_ref.shape)
    copies[0].wait()
    copies[3].wait()
    tok = k_ref.shape[1]
    up_ref[:, :PAIR] = k_ref[:, tok - PAIR :]
    up_ref[:, PAIR : 2 * PAIR] = v_ref[:, tok - PAIR :]
    up_ref[:, 2 * PAIR :] = jnp.concatenate(
        [q_ref[:, tok - BLOCK :], g_ref[:, tok - BLOCK :]], axis=1
    )


def by_head(x):
    width = x.shape[0]
    x = x * jnp.asarray(SCALE, BF16)
    columns = []
    for h in range(width // HEAD_DIM):
        rows = [x[h * HEAD_DIM : (h + 1) * HEAD_DIM]]
        if h:
            rows.insert(0, jnp.zeros((h * HEAD_DIM, x.shape[1]), BF16))
        if (h + 1) * HEAD_DIM < width:
            rows.append(jnp.zeros((width - (h + 1) * HEAD_DIM, x.shape[1]), BF16))
        columns.append(jnp.concatenate(rows, axis=0))
    return jnp.concatenate(columns, axis=1)


def own_head(x):
    return jnp.concatenate(
        [
            x[h * HEAD_DIM : (h + 1) * HEAD_DIM, h * PAIR : (h + 1) * PAIR]
            for h in range(x.shape[0] // HEAD_DIM)
        ],
        axis=0,
    )


def head_sums(x):
    return jnp.concatenate(
        [
            jnp.sum(x[h * HEAD_DIM : (h + 1) * HEAD_DIM], axis=0, keepdims=True)
            for h in range(x.shape[0] // HEAD_DIM)
        ],
        axis=1,
    )


def top_of(x):
    return jnp.max(x, axis=0, keepdims=True)


def total_of(x):
    return jnp.sum(x, axis=0, keepdims=True)


def second_half(lanes):
    return lax.broadcasted_iota(jnp.int32, (1, lanes), 1) % PAIR >= BLOCK


def global_scores(rows, qm):
    shape = (rows.shape[0], qm.shape[1])
    is_key = lax.broadcasted_iota(jnp.int32, shape, 0) % (2 * SUM_DEV) < SUM_DEV
    return jnp.where(is_key, mm(rows, qm), LOW)


def value_rows(rows):
    return pltpu.roll(rows.astype(F32), rows.shape[0] - SUM_DEV, 0).astype(BF16)


def local_kernel(
    first_ref, q_ref, k_ref, v_ref, g_ref, before_ref,
    exp_ref, top_ref, total_ref, qx_ref, gx_ref, kx_ref, vx_ref, kt_ref, vt_ref,
):
    width, tok = q_ref.shape
    for at, t_ref, x_ref, own_ref in ((0, kt_ref, kx_ref, k_ref), (PAIR, vt_ref, vx_ref, v_ref)):
        t_ref[:, :PAIR] = before_ref[:, at : at + PAIR]
        t_ref[:, PAIR:] = own_ref[...]
        x_ref[:PAIR] = before_ref[:, at : at + PAIR].T
        x_ref[PAIR:] = own_ref[...].T
    for at, x_ref, own_ref in ((2 * PAIR, qx_ref, q_ref), (2 * PAIR + BLOCK, gx_ref, g_ref)):
        x_ref[...] = jnp.concatenate(
            [before_ref[:, at : at + BLOCK], own_ref[:, : tok - BLOCK]], axis=1
        )
    second = second_half(width // HEAD_DIM * PAIR)
    is_first = first_ref[0] == 1
    for p in range(tok // PAIR):
        s = mm(kx_ref[p * PAIR : (p + 2) * PAIR], by_head(qx_ref[:, p * PAIR : (p + 1) * PAIR]))
        parts = [s[b * BLOCK : (b + 1) * BLOCK] for b in range(4)]
        parts[0] += jnp.where(second, LOW, 0.0)
        if p == 0:
            parts[1] += jnp.where(jnp.logical_and(is_first, second), LOW, 0.0)
            parts[2] += jnp.where(jnp.logical_and(is_first, jnp.logical_not(second)), LOW, 0.0)
        parts[3] += jnp.where(second, 0.0, LOW)
        s = jnp.concatenate(parts, axis=0)
        top = top_of(s)
        s = jnp.exp(s - top)
        exp_ref[p] = s
        top_ref[p] = top
        total_ref[p] = total_of(s)


def global_kernel(
    qx_ref, gx_ref, vt_ref, rows_ref, exp_ref, top_ref, total_ref,
    att_ref, part_ref, ds_ref, factor_ref, delta_ref,
):
    rows = rows_ref[...]
    width = qx_ref.shape[0]
    pairs = range(qx_ref.shape[1] // PAIR)
    own = [slice(p * PAIR, (p + 1) * PAIR) for p in pairs]
    qm = [by_head(qx_ref[:, own[p]]) for p in pairs]
    s = global_scores(rows, jnp.concatenate(qm, axis=1))
    lanes = qm[0].shape[1]
    s = [s[:, p * lanes : (p + 1) * lanes] for p in pairs]
    values_g = value_rows(rows)
    values_gt = values_g.T
    gm = [by_head(gx_ref[:, own[p]]) for p in pairs]
    top = [jnp.maximum(top_ref[p], top_of(s[p])) for p in pairs]
    s = [jnp.exp(s[p] - top[p]) for p in pairs]
    factor = [jnp.exp(top_ref[p] - top[p]) for p in pairs]
    inverse = [1.0 / (total_ref[p] * factor[p] + total_of(s[p])) for p in pairs]
    factor = [factor[p] * inverse[p] for p in pairs]
    w = [s[p] * inverse[p] for p in pairs]
    wb = [w[p].astype(BF16) for p in pairs]
    probs = [(exp_ref[p] * factor[p]).astype(BF16) for p in pairs]
    heads = range(width // HEAD_DIM)
    f = [slice(h * HEAD_DIM, (h + 1) * HEAD_DIM) for h in heads]
    c = [slice(h * PAIR, (h + 1) * PAIR) for h in heads]
    att = [
        jnp.concatenate(
            [
                mm(vt_ref[f[h], p * PAIR : (p + 2) * PAIR], probs[p][:, c[h]])
                + mm(values_gt[f[h]], wb[p][:, c[h]])
                for h in heads
            ],
            axis=0,
        ).astype(BF16)
        for p in pairs
    ]
    dprob = mm(values_g, jnp.concatenate(gm, axis=1))
    dprob = [dprob[:, p * lanes : (p + 1) * lanes] for p in pairs]
    part_v = mm_nt(jnp.concatenate(wb, axis=1), jnp.concatenate(gm, axis=1))
    delta = [
        head_sums(gx_ref[:, own[p]].astype(F32) * att[p].astype(F32)) * SCALE for p in pairs
    ]
    ds = [(w[p] * (dprob[p] - delta[p])).astype(BF16) for p in pairs]
    part_k = mm_nt(jnp.concatenate(ds, axis=1), jnp.concatenate(qm, axis=1))
    part_ref[...] = (part_k + pltpu.roll(part_v, SUM_DEV, 0)) * (1.0 / SCALE)
    for p in pairs:
        att_ref[:, own[p]] = att[p]
        ds_ref[p] = ds[p]
        factor_ref[p] = factor[p]
        delta_ref[p] = delta[p]


def gradient_kernel(
    qx_ref, gx_ref, kt_ref, vx_ref, rows_ref, exp_ref, att_ref, ds_ref, factor_ref, delta_ref,
    att_out_ref, qg_out_ref, kg_ref, vg_ref, back_ref,
):
    width, tok = kg_ref.shape
    pairs = tok // PAIR
    rows_t = rows_ref[...].T

    def pair(p):
        own = slice(p * PAIR, (p + 1) * PAIR)
        near = slice(p * PAIR, (p + 2) * PAIR)
        qm, gm = by_head(qx_ref[:, own]), by_head(gx_ref[:, own])
        w = exp_ref[p] * factor_ref[p]
        ds = (w * (mm(vx_ref[near], gm) - delta_ref[p])).astype(BF16)
        qg = own_head(mm(kt_ref[:, near], ds) + mm(rows_t, ds_ref[p])).astype(BF16)
        kg = mm_nt(qm, ds) * (1.0 / SCALE)
        vg = mm_nt(gm, w.astype(BF16)) * (1.0 / SCALE)
        return qg, kg, vg

    grads = [pair(p) for p in range(pairs)]
    qg = jnp.concatenate([qg for qg, _, _ in grads], axis=1)
    att = att_ref[...]
    back_ref[:, 2 * PAIR :] = jnp.concatenate([att[:, :BLOCK], qg[:, :BLOCK]], axis=1)
    for x, ref in ((att, att_out_ref), (qg, qg_out_ref)):
        ref[...] = jnp.concatenate([x[:, BLOCK:], x[:, :BLOCK]], axis=1)
    for at, i, ref in ((0, 1, kg_ref), (PAIR, 2, vg_ref)):
        back_ref[:, at : at + PAIR] = grads[0][i][:, :PAIR].astype(BF16)
        for p in range(pairs - 1):
            ref[:, p * PAIR : (p + 1) * PAIR] = grads[p][i][:, PAIR:] + grads[p + 1][i][:, :PAIR]
        ref[:, tok - PAIR :] = grads[-1][i][:, PAIR:]


def owned_kernel(parts_ref, k_ref, v_ref, owned_ref, term_ref):
    owned = jnp.sum(parts_ref[...], axis=0)
    owned_ref[...] = owned
    split = pieces(owned)
    n = 2 * SUM_DEV
    seg = k_ref.shape[1] // SUM_DEV
    total = jnp.zeros((1, k_ref.shape[1]), F32)
    for first, ref in ((0, k_ref), (SUM_DEV, v_ref)):
        met = mm(split, ref[...])
        met = met[:n] + met[n : 2 * n] + met[2 * n :]
        met = jnp.where(segment_mask(first, met.shape[0], met.shape[1], seg), met, 0.0)
        total += jnp.sum(met, axis=0, keepdims=True)
    term = total[:, :seg]
    for j in range(1, SUM_DEV):
        term += total[:, j * seg : (j + 1) * seg]
    term_ref[...] = jnp.broadcast_to(term, term_ref.shape)


def sum_kernel(terms_ref, sum_ref):
    sum_ref[...] = jnp.sum(terms_ref[...], axis=0, keepdims=True)


def outer(rows, weights):
    n = rows.shape[0]
    a, b = pieces(rows), pieces(weights)
    a = [a[i * n : (i + 1) * n] for i in (0, 0, 1, 0, 1, 2)]
    b = [b[i * n : (i + 1) * n] for i in (0, 1, 0, 2, 1, 0)]
    return mm_tn(jnp.concatenate(a, axis=0), jnp.concatenate(b, axis=0))


def finish_kernel(
    owned_ref, kg_ref, vg_ref, w_ref, back_ref, atts_ref, qgs_ref, pool_ref,
    key_out, value_out, att_out, qg_out, pool_out, key_ref, value_ref, att_ref, qg_ref, sem,
):
    copies = []

    def send(ref, out):
        copies.append(pltpu.make_async_copy(ref, out, sem.at[len(copies)]))
        copies[-1].start()

    tok = kg_ref.shape[1]
    low, high = slice(0, tok - PAIR), slice(tok - PAIR, tok)
    send(pool_ref, pool_out)
    for at, x_ref, ref, out in (
        (0, atts_ref, att_ref, att_out),
        (BLOCK, qgs_ref, qg_ref, qg_out),
    ):
        send(x_ref.at[:, low], out.at[:, low])
        edge = back_ref[:, 2 * PAIR + at : 2 * PAIR + at + BLOCK]
        ref[...] = jnp.concatenate([x_ref[:, tok - PAIR : tok - BLOCK], edge], axis=1)
        send(ref, out.at[:, high])
    owned = owned_ref[...]
    w = jnp.concatenate([w_ref[...]] * SUM_DEV, axis=1)
    w = jnp.broadcast_to(w, (owned.shape[0], tok))
    for first, at, grad_ref, ref, out in (
        (0, 0, kg_ref, key_ref, key_out),
        (SUM_DEV, PAIR, vg_ref, value_ref, value_out),
    ):
        weights = jnp.where(segment_mask(first, w.shape[0], tok, w_ref.shape[1]), w, 0.0)
        total = grad_ref[...] + outer(owned, weights)
        ref[:, low] = total[:, low].astype(BF16)
        ref[:, high] = (total[:, high] + back_ref[:, at : at + PAIR].astype(F32)).astype(BF16)
        send(ref, out)
    for copy in copies:
        copy.wait()


def shaped(shape, dtype):
    return jax.ShapeDtypeStruct(shape, dtype)


def call(kernel, outs, count, first=VMEM):
    return pl.pallas_call(
        kernel,
        out_shape=outs,
        in_specs=[first] + [VMEM] * (count - 1),
        out_specs=[VMEM] * len(outs),
        compiler_params=PARAMS,
    )


def local(queries, key_states, value_states, pool_weight, out_grad):
    tok, width = queries.shape
    group_index = lax.axis_index("seq")
    groups = lax.axis_size("seq")
    everyone = groups * lax.axis_size("head")
    n = 2 * SUM_DEV
    seg = pool_weight.shape[0]
    pairs, lanes = tok // PAIR, width // HEAD_DIM * PAIR
    halo = shaped((width, 3 * PAIR), BF16)
    own = shaped((width, tok), BF16)
    grad = shaped((width, tok), F32)
    keys = shaped((tok + PAIR, width), BF16)
    keys_t = shaped((width, tok + PAIR), BF16)
    stat = shaped((pairs, 1, lanes), F32)
    up = [(i, (i + 1) % groups) for i in range(groups)]
    down = [(j, i) for i, j in up]
    half = groups // 2
    order = [[*range(half, groups), *range(half)[::-1]]]

    def exchange(x):
        x = x.reshape(groups, n, width)
        return lax.all_to_all(x, "seq", split_axis=0, concat_axis=0, axis_index_groups=order)

    arguments = (queries.T, key_states.T, value_states.T, out_grad.T, pool_weight.reshape(1, seg))
    summary, edge, q, k, v, g, weight_row = pl.pallas_call(
        pool_kernel,
        out_shape=[shaped((groups, n, width), BF16), halo] + [own] * 4 + [shaped((1, seg), F32)],
        in_specs=[pl.BlockSpec(memory_space=pltpu.HBM)] * 5,
        out_specs=[VMEM] * 7,
        scratch_shapes=[pltpu.SemaphoreType.DMA((5,))],
        compiler_params=PARAMS,
    )(*[pltpu.with_memory_space_constraint(x, pltpu.HBM) for x in arguments])
    before = lax.ppermute(edge, "seq", up)
    rows = exchange(summary).reshape(groups * n, width)
    is_first = (group_index == 0).astype(jnp.int32).reshape(1)
    exps, top, total, qx, gx, kx, vx, kt, vt = call(
        local_kernel,
        [shaped((pairs, 2 * PAIR, lanes), F32), stat, stat, own, own, keys, keys, keys_t, keys_t],
        6,
        SMEM,
    )(is_first, q, k, v, g, before)

    att_x, part, ds, factor, delta = call(
        global_kernel,
        [own, shaped((groups * n, width), F32), shaped((pairs, groups * n, lanes), BF16), stat, stat],
        7,
    )(qx, gx, vt, rows, exps, top, total)
    parts = exchange(part)
    att_own, qg_own, key_part, value_part, edge = call(
        gradient_kernel, [own, own, grad, grad, halo], 10
    )(
        qx, gx, kt, vx, rows, exps, att_x, ds, factor, delta
    )
    back = lax.ppermute(edge, "seq", down)
    parts, qg_own = lax.optimization_barrier((parts, qg_own))
    owned, term = call(owned_kernel, [shaped((n, width), F32), shaped((everyone, seg), F32)], 3)(
        parts, k, v
    )
    terms = lax.all_to_all(term, ("seq", "head"), split_axis=0, concat_axis=0)
    (pool_sum,) = call(sum_kernel, [shaped((1, seg), F32)], 1)(terms)
    key_grad, value_grad, attended, query_grad, pool_grad = pl.pallas_call(
        finish_kernel,
        out_shape=[own] * 4 + [shaped((1, seg), F32)],
        in_specs=[VMEM] * 8,
        out_specs=[pl.BlockSpec(memory_space=pltpu.HBM)] * 5,
        scratch_shapes=[pltpu.VMEM((width, tok), BF16)] * 2
        + [pltpu.VMEM((width, PAIR), BF16)] * 2
        + [pltpu.SemaphoreType.DMA((7,))],
        compiler_params=PARAMS,
    )(owned, key_part, value_part, weight_row, back, att_own, qg_own, pool_sum)
    return (attended.T, query_grad.T, key_grad.T, value_grad.T, pool_grad.reshape(seg))


def solution(mesh):
    return jax.shard_map(
        local,
        mesh=mesh,
        in_specs=(P("seq", "head"), P("seq", "head"), P("seq", "head"), P(), P("seq", "head")),
        out_specs=(P("seq", "head"), P("seq", "head"), P("seq", "head"), P("seq", "head"), P()),
        check_vma=False,
    )
```

```python
import functools

import jax
import jax.numpy as jnp
from jax import lax
from jax.experimental import pallas as pl
from jax.experimental.pallas import tpu as pltpu
from jax.sharding import PartitionSpec as P

HEAD_DIM = 64
BLOCK = 64
SUM_DEV = 4
PAIR = 2 * BLOCK
SCALE = HEAD_DIM ** (-0.5)
LOW = -1e30
VMEM = pl.BlockSpec(memory_space=pltpu.VMEM)
SMEM = pl.BlockSpec(memory_space=pltpu.SMEM)
PARAMS = pltpu.CompilerParams(vmem_limit_bytes=40 * 1024 * 1024)
F32 = jnp.float32
BF16 = jnp.bfloat16


def mm(a, b):
    return lax.dot_general(a, b, (((1,), (0,)), ((), ())), preferred_element_type=F32)


def mm_nt(a, b):
    return lax.dot_general(a, b, (((1,), (1,)), ((), ())), preferred_element_type=F32)


def mm_tn(a, b):
    return lax.dot_general(a, b, (((0,), (0,)), ((), ())), preferred_element_type=F32)


def pieces(x):
    high = x.astype(BF16)
    rest = x - high.astype(F32)
    middle = rest.astype(BF16)
    low = (rest - middle.astype(F32)).astype(BF16)
    return jnp.concatenate([high, middle, low], axis=0)


def segment_mask(first, rows, lanes, seg):
    row = lax.broadcasted_iota(jnp.int32, (rows, lanes), 0)
    lane = lax.broadcasted_iota(jnp.int32, (rows, lanes), 1)
    return row - first == lane // seg


def pool_kernel(*refs):
    sources, (rows_ref, up_ref, *kept), sem = refs[:5], refs[5:12], refs[12]
    q_ref, k_ref, v_ref, g_ref, w_ref = kept
    copies = [
        pltpu.make_async_copy(source, target, sem.at[i])
        for i, (source, target) in enumerate(zip(sources, kept))
    ]
    for i in (4, 1, 2, 0, 3):
        copies[i].start()
    for i in (4, 1, 2):
        copies[i].wait()
    seg = w_ref.shape[1]
    n = 2 * SUM_DEV
    w = jnp.concatenate([w_ref[...]] * SUM_DEV, axis=1)
    w = jnp.broadcast_to(w, (n, w.shape[1]))
    pooled = jnp.zeros((n, k_ref.shape[0]), F32)
    for first, ref in ((0, k_ref), (SUM_DEV, v_ref)):
        weights = jnp.where(segment_mask(first, w.shape[0], w.shape[1], seg), w, 0.0)
        parts = mm_nt(pieces(weights), ref[...])
        pooled += parts[:n] + parts[n : 2 * n] + parts[2 * n :]
    rows_ref[...] = jnp.broadcast_to(pooled.astype(BF16)[None], rows_ref.shape)
    copies[0].wait()
    copies[3].wait()
    tok = k_ref.shape[1]
    up_ref[:, :PAIR] = k_ref[:, tok - PAIR :]
    up_ref[:, PAIR : 2 * PAIR] = v_ref[:, tok - PAIR :]
    up_ref[:, 2 * PAIR :] = jnp.concatenate(
        [q_ref[:, tok - BLOCK :], g_ref[:, tok - BLOCK :]], axis=1
    )


def by_head(x):
    width = x.shape[0]
    x = x * jnp.asarray(SCALE, BF16)
    columns = []
    for h in range(width // HEAD_DIM):
        rows = [x[h * HEAD_DIM : (h + 1) * HEAD_DIM]]
        if h:
            rows.insert(0, jnp.zeros((h * HEAD_DIM, x.shape[1]), BF16))
        if (h + 1) * HEAD_DIM < width:
            rows.append(jnp.zeros((width - (h + 1) * HEAD_DIM, x.shape[1]), BF16))
        columns.append(jnp.concatenate(rows, axis=0))
    return jnp.concatenate(columns, axis=1)


def own_head(x):
    return jnp.concatenate(
        [
            x[h * HEAD_DIM : (h + 1) * HEAD_DIM, h * PAIR : (h + 1) * PAIR]
            for h in range(x.shape[0] // HEAD_DIM)
        ],
        axis=0,
    )


def head_sums(x):
    return jnp.concatenate(
        [
            jnp.sum(x[h * HEAD_DIM : (h + 1) * HEAD_DIM], axis=0, keepdims=True)
            for h in range(x.shape[0] // HEAD_DIM)
        ],
        axis=1,
    )


def top_of(x):
    return jnp.max(x, axis=0, keepdims=True)


def total_of(x):
    return jnp.sum(x, axis=0, keepdims=True)


def second_half(lanes):
    return lax.broadcasted_iota(jnp.int32, (1, lanes), 1) % PAIR >= BLOCK


def global_scores(rows, qm):
    shape = (rows.shape[0], qm.shape[1])
    is_key = lax.broadcasted_iota(jnp.int32, shape, 0) % (2 * SUM_DEV) < SUM_DEV
    return jnp.where(is_key, mm(rows, qm), LOW)


def value_rows(rows):
    return pltpu.roll(rows.astype(F32), rows.shape[0] - SUM_DEV, 0).astype(BF16)


def local_kernel(
    first_ref, q_ref, k_ref, v_ref, g_ref, before_ref,
    exp_ref, top_ref, total_ref, qx_ref, gx_ref, kx_ref, vx_ref, kt_ref, vt_ref,
):
    width, tok = q_ref.shape
    for at, t_ref, x_ref, own_ref in ((0, kt_ref, kx_ref, k_ref), (PAIR, vt_ref, vx_ref, v_ref)):
        t_ref[:, :PAIR] = before_ref[:, at : at + PAIR]
        t_ref[:, PAIR:] = own_ref[...]
        x_ref[:PAIR] = before_ref[:, at : at + PAIR].T
        x_ref[PAIR:] = own_ref[...].T
    for at, x_ref, own_ref in ((2 * PAIR, qx_ref, q_ref), (2 * PAIR + BLOCK, gx_ref, g_ref)):
        x_ref[...] = jnp.concatenate(
            [before_ref[:, at : at + BLOCK], own_ref[:, : tok - BLOCK]], axis=1
        )
    second = second_half(width // HEAD_DIM * PAIR)
    is_first = first_ref[0] == 1
    for p in range(tok // PAIR):
        s = mm(kx_ref[p * PAIR : (p + 2) * PAIR], by_head(qx_ref[:, p * PAIR : (p + 1) * PAIR]))
        parts = [s[b * BLOCK : (b + 1) * BLOCK] for b in range(4)]
        parts[0] += jnp.where(second, LOW, 0.0)
        if p == 0:
            parts[1] += jnp.where(jnp.logical_and(is_first, second), LOW, 0.0)
            parts[2] += jnp.where(jnp.logical_and(is_first, jnp.logical_not(second)), LOW, 0.0)
        parts[3] += jnp.where(second, 0.0, LOW)
        s = jnp.concatenate(parts, axis=0)
        top = top_of(s)
        s = jnp.exp(s - top)
        exp_ref[p] = s
        top_ref[p] = top
        total_ref[p] = total_of(s)


def global_kernel(
    qx_ref, gx_ref, vt_ref, rows_ref, exp_ref, top_ref, total_ref,
    att_ref, part_ref, ds_ref, factor_ref, delta_ref,
):
    rows = rows_ref[...]
    width = qx_ref.shape[0]
    pairs = range(qx_ref.shape[1] // PAIR)
    own = [slice(p * PAIR, (p + 1) * PAIR) for p in pairs]
    qm = [by_head(qx_ref[:, own[p]]) for p in pairs]
    s = global_scores(rows, jnp.concatenate(qm, axis=1))
    lanes = qm[0].shape[1]
    s = [s[:, p * lanes : (p + 1) * lanes] for p in pairs]
    values_g = value_rows(rows)
    values_gt = values_g.T
    gm = [by_head(gx_ref[:, own[p]]) for p in pairs]
    top = [jnp.maximum(top_ref[p], top_of(s[p])) for p in pairs]
    s = [jnp.exp(s[p] - top[p]) for p in pairs]
    factor = [jnp.exp(top_ref[p] - top[p]) for p in pairs]
    inverse = [1.0 / (total_ref[p] * factor[p] + total_of(s[p])) for p in pairs]
    factor = [factor[p] * inverse[p] for p in pairs]
    w = [s[p] * inverse[p] for p in pairs]
    wb = [w[p].astype(BF16) for p in pairs]
    probs = [(exp_ref[p] * factor[p]).astype(BF16) for p in pairs]
    heads = range(width // HEAD_DIM)
    f = [slice(h * HEAD_DIM, (h + 1) * HEAD_DIM) for h in heads]
    c = [slice(h * PAIR, (h + 1) * PAIR) for h in heads]
    att = [
        jnp.concatenate(
            [
                mm(vt_ref[f[h], p * PAIR : (p + 2) * PAIR], probs[p][:, c[h]])
                + mm(values_gt[f[h]], wb[p][:, c[h]])
                for h in heads
            ],
            axis=0,
        ).astype(BF16)
        for p in pairs
    ]
    dprob = mm(values_g, jnp.concatenate(gm, axis=1))
    dprob = [dprob[:, p * lanes : (p + 1) * lanes] for p in pairs]
    part_v = mm_nt(jnp.concatenate(wb, axis=1), jnp.concatenate(gm, axis=1))
    delta = [
        head_sums(gx_ref[:, own[p]].astype(F32) * att[p].astype(F32)) * SCALE for p in pairs
    ]
    ds = [(w[p] * (dprob[p] - delta[p])).astype(BF16) for p in pairs]
    part_k = mm_nt(jnp.concatenate(ds, axis=1), jnp.concatenate(qm, axis=1))
    part_ref[...] = (part_k + pltpu.roll(part_v, SUM_DEV, 0)) * (1.0 / SCALE)
    for p in pairs:
        att_ref[:, own[p]] = att[p]
        ds_ref[p] = ds[p]
        factor_ref[p] = factor[p]
        delta_ref[p] = delta[p]


def gradient_kernel(
    qx_ref, gx_ref, kt_ref, vx_ref, rows_ref, exp_ref, att_ref, ds_ref, factor_ref, delta_ref,
    att_out_ref, qg_out_ref, kg_ref, vg_ref, back_ref,
):
    width, tok = kg_ref.shape
    pairs = tok // PAIR
    rows_t = rows_ref[...].T

    def pair(p):
        own = slice(p * PAIR, (p + 1) * PAIR)
        near = slice(p * PAIR, (p + 2) * PAIR)
        qm, gm = by_head(qx_ref[:, own]), by_head(gx_ref[:, own])
        w = exp_ref[p] * factor_ref[p]
        ds = (w * (mm(vx_ref[near], gm) - delta_ref[p])).astype(BF16)
        qg = own_head(mm(kt_ref[:, near], ds) + mm(rows_t, ds_ref[p])).astype(BF16)
        kg = mm_nt(qm, ds) * (1.0 / SCALE)
        vg = mm_nt(gm, w.astype(BF16)) * (1.0 / SCALE)
        return qg, kg, vg

    grads = [pair(p) for p in range(pairs)]
    qg = jnp.concatenate([qg for qg, _, _ in grads], axis=1)
    att = att_ref[...]
    back_ref[:, 2 * PAIR :] = jnp.concatenate([att[:, :BLOCK], qg[:, :BLOCK]], axis=1)
    for x, ref in ((att, att_out_ref), (qg, qg_out_ref)):
        ref[...] = jnp.concatenate([x[:, BLOCK:], x[:, :BLOCK]], axis=1)
    for at, i, ref in ((0, 1, kg_ref), (PAIR, 2, vg_ref)):
        back_ref[:, at : at + PAIR] = grads[0][i][:, :PAIR].astype(BF16)
        for p in range(pairs - 1):
            ref[:, p * PAIR : (p + 1) * PAIR] = grads[p][i][:, PAIR:] + grads[p + 1][i][:, :PAIR]
        ref[:, tok - PAIR :] = grads[-1][i][:, PAIR:]


def outer(rows, weights):
    n = rows.shape[0]
    a, b = pieces(rows), pieces(weights)
    a = [a[i * n : (i + 1) * n] for i in (0, 0, 1, 0, 1, 2)]
    b = [b[i * n : (i + 1) * n] for i in (0, 1, 0, 2, 1, 0)]
    return mm_tn(jnp.concatenate(a, axis=0), jnp.concatenate(b, axis=0))


def owned_kernel(parts_ref, k_ref, v_ref, w_ref, term_ref, kp_ref, vp_ref):
    owned = jnp.sum(parts_ref[...], axis=0)
    split = pieces(owned)
    n = 2 * SUM_DEV
    seg = k_ref.shape[1] // SUM_DEV
    total = jnp.zeros((1, k_ref.shape[1]), F32)
    for first, ref in ((0, k_ref), (SUM_DEV, v_ref)):
        met = mm(split, ref[...])
        met = met[:n] + met[n : 2 * n] + met[2 * n :]
        met = jnp.where(segment_mask(first, met.shape[0], met.shape[1], seg), met, 0.0)
        total += jnp.sum(met, axis=0, keepdims=True)
    term = total[:, :seg]
    for j in range(1, SUM_DEV):
        term += total[:, j * seg : (j + 1) * seg]
    term_ref[...] = jnp.broadcast_to(term, term_ref.shape)
    tok = k_ref.shape[1]
    w = jnp.concatenate([w_ref[...]] * SUM_DEV, axis=1)
    w = jnp.broadcast_to(w, (n, tok))
    for first, ref in ((0, kp_ref), (SUM_DEV, vp_ref)):
        ref[...] = outer(owned, jnp.where(segment_mask(first, n, tok, seg), w, 0.0))


def sum_kernel(terms_ref, sum_ref):
    sum_ref[...] = jnp.sum(terms_ref[...], axis=0, keepdims=True)


def finish_kernel(
    kp_ref, vp_ref, kg_ref, vg_ref, back_ref, atts_ref, qgs_ref, pool_ref,
    key_out, value_out, att_out, qg_out, pool_out, key_ref, value_ref, att_ref, qg_ref, sem,
):
    copies = []

    def send(ref, out):
        copies.append(pltpu.make_async_copy(ref, out, sem.at[len(copies)]))
        copies[-1].start()

    tok = kg_ref.shape[1]
    low, high = slice(0, tok - PAIR), slice(tok - PAIR, tok)
    send(pool_ref, pool_out)
    for at, x_ref, ref, out in (
        (0, atts_ref, att_ref, att_out),
        (BLOCK, qgs_ref, qg_ref, qg_out),
    ):
        send(x_ref.at[:, low], out.at[:, low])
        edge = back_ref[:, 2 * PAIR + at : 2 * PAIR + at + BLOCK]
        ref[...] = jnp.concatenate([x_ref[:, tok - PAIR : tok - BLOCK], edge], axis=1)
        send(ref, out.at[:, high])
    for at, pooled_ref, grad_ref, ref, out in (
        (0, kp_ref, kg_ref, key_ref, key_out),
        (PAIR, vp_ref, vg_ref, value_ref, value_out),
    ):
        total = grad_ref[...] + pooled_ref[...]
        ref[:, low] = total[:, low].astype(BF16)
        ref[:, high] = (total[:, high] + back_ref[:, at : at + PAIR].astype(F32)).astype(BF16)
        send(ref, out)
    for copy in copies:
        copy.wait()


def shaped(shape, dtype):
    return jax.ShapeDtypeStruct(shape, dtype)


def call(kernel, outs, count, first=VMEM):
    return pl.pallas_call(
        kernel,
        out_shape=outs,
        in_specs=[first] + [VMEM] * (count - 1),
        out_specs=[VMEM] * len(outs),
        compiler_params=PARAMS,
    )


def local(queries, key_states, value_states, pool_weight, out_grad):
    tok, width = queries.shape
    group_index = lax.axis_index("seq")
    groups = lax.axis_size("seq")
    everyone = groups * lax.axis_size("head")
    n = 2 * SUM_DEV
    seg = pool_weight.shape[0]
    pairs, lanes = tok // PAIR, width // HEAD_DIM * PAIR
    halo = shaped((width, 3 * PAIR), BF16)
    own = shaped((width, tok), BF16)
    grad = shaped((width, tok), F32)
    keys = shaped((tok + PAIR, width), BF16)
    keys_t = shaped((width, tok + PAIR), BF16)
    stat = shaped((pairs, 1, lanes), F32)
    up = [(i, (i + 1) % groups) for i in range(groups)]
    down = [(j, i) for i, j in up]
    half = groups // 2
    order = [[*range(half, groups), *range(half)[::-1]]]

    def exchange(x):
        x = x.reshape(groups, n, width)
        return lax.all_to_all(x, "seq", split_axis=0, concat_axis=0, axis_index_groups=order)

    arguments = (queries.T, key_states.T, value_states.T, out_grad.T, pool_weight.reshape(1, seg))
    summary, edge, q, k, v, g, weight_row = pl.pallas_call(
        pool_kernel,
        out_shape=[shaped((groups, n, width), BF16), halo] + [own] * 4 + [shaped((1, seg), F32)],
        in_specs=[pl.BlockSpec(memory_space=pltpu.HBM)] * 5,
        out_specs=[VMEM] * 7,
        scratch_shapes=[pltpu.SemaphoreType.DMA((5,))],
        compiler_params=PARAMS,
    )(*[pltpu.with_memory_space_constraint(x, pltpu.HBM) for x in arguments])
    before = lax.ppermute(edge, "seq", up)
    rows = exchange(summary).reshape(groups * n, width)
    is_first = (group_index == 0).astype(jnp.int32).reshape(1)
    exps, top, total, qx, gx, kx, vx, kt, vt = call(
        local_kernel,
        [shaped((pairs, 2 * PAIR, lanes), F32), stat, stat, own, own, keys, keys, keys_t, keys_t],
        6,
        SMEM,
    )(is_first, q, k, v, g, before)

    att_x, part, ds, factor, delta = call(
        global_kernel,
        [own, shaped((groups * n, width), F32), shaped((pairs, groups * n, lanes), BF16), stat, stat],
        7,
    )(qx, gx, vt, rows, exps, top, total)
    parts = exchange(part)
    att_own, qg_own, key_part, value_part, edge = call(
        gradient_kernel, [own, own, grad, grad, halo], 10
    )(
        qx, gx, kt, vx, rows, exps, att_x, ds, factor, delta
    )
    back = lax.ppermute(edge, "seq", down)
    parts, qg_own = lax.optimization_barrier((parts, qg_own))
    term, key_pooled, value_pooled = call(
        owned_kernel, [shaped((everyone, seg), F32), grad, grad], 4
    )(parts, k, v, weight_row)
    terms = lax.all_to_all(term, ("seq", "head"), split_axis=0, concat_axis=0)
    (pool_sum,) = call(sum_kernel, [shaped((1, seg), F32)], 1)(terms)
    key_grad, value_grad, attended, query_grad, pool_grad = pl.pallas_call(
        finish_kernel,
        out_shape=[own] * 4 + [shaped((1, seg), F32)],
        in_specs=[VMEM] * 8,
        out_specs=[pl.BlockSpec(memory_space=pltpu.HBM)] * 5,
        scratch_shapes=[pltpu.VMEM((width, tok), BF16)] * 2
        + [pltpu.VMEM((width, PAIR), BF16)] * 2
        + [pltpu.SemaphoreType.DMA((7,))],
        compiler_params=PARAMS,
    )(key_pooled, value_pooled, key_part, value_part, back, att_own, qg_own, pool_sum)
    return (attended.T, query_grad.T, key_grad.T, value_grad.T, pool_grad.reshape(seg))


def solution(mesh):
    return jax.shard_map(
        local,
        mesh=mesh,
        in_specs=(P("seq", "head"), P("seq", "head"), P("seq", "head"), P(), P("seq", "head")),
        out_specs=(P("seq", "head"), P("seq", "head"), P("seq", "head"), P("seq", "head"), P()),
        check_vma=False,
    )
```

```python
import functools

import jax
import jax.numpy as jnp
from jax import lax
from jax.experimental import pallas as pl
from jax.experimental.pallas import tpu as pltpu
from jax.sharding import PartitionSpec as P

HEAD_DIM = 64
BLOCK = 64
SUM_DEV = 4
PAIR = 2 * BLOCK
SCALE = HEAD_DIM ** (-0.5)
LOW = -1e30
VMEM = pl.BlockSpec(memory_space=pltpu.VMEM)
PARAMS = pltpu.CompilerParams(vmem_limit_bytes=40 * 1024 * 1024)
F32 = jnp.float32
BF16 = jnp.bfloat16


def mm(a, b):
    return lax.dot_general(a, b, (((1,), (0,)), ((), ())), preferred_element_type=F32)


def mm_nt(a, b):
    return lax.dot_general(a, b, (((1,), (1,)), ((), ())), preferred_element_type=F32)


def mm_tn(a, b):
    return lax.dot_general(a, b, (((0,), (0,)), ((), ())), preferred_element_type=F32)


def pieces(x):
    high = x.astype(BF16)
    rest = x - high.astype(F32)
    middle = rest.astype(BF16)
    low = (rest - middle.astype(F32)).astype(BF16)
    return jnp.concatenate([high, middle, low], axis=0)


def segment_mask(first, rows, lanes, seg):
    row = lax.broadcasted_iota(jnp.int32, (rows, lanes), 0)
    lane = lax.broadcasted_iota(jnp.int32, (rows, lanes), 1)
    return row - first == lane // seg


def pool_kernel(*refs):
    sources, (rows_ref, up_ref, *kept), sem = refs[:5], refs[5:12], refs[12]
    q_ref, k_ref, v_ref, g_ref, w_ref = kept
    copies = [
        pltpu.make_async_copy(source, target, sem.at[i])
        for i, (source, target) in enumerate(zip(sources, kept))
    ]
    for i in (4, 1, 2, 0, 3):
        copies[i].start()
    for i in (4, 1, 2):
        copies[i].wait()
    seg = w_ref.shape[1]
    n = 2 * SUM_DEV
    w = jnp.concatenate([w_ref[...]] * SUM_DEV, axis=1)
    w = jnp.broadcast_to(w, (n, w.shape[1]))
    pooled = jnp.zeros((n, k_ref.shape[0]), F32)
    for first, ref in ((0, k_ref), (SUM_DEV, v_ref)):
        weights = jnp.where(segment_mask(first, w.shape[0], w.shape[1], seg), w, 0.0)
        parts = mm_nt(pieces(weights), ref[...])
        pooled += parts[:n] + parts[n : 2 * n] + parts[2 * n :]
    rows_ref[...] = jnp.broadcast_to(pooled.astype(BF16)[None], rows_ref.shape)
    copies[0].wait()
    copies[3].wait()
    tok = k_ref.shape[1]
    up_ref[:, :PAIR] = k_ref[:, tok - PAIR :]
    up_ref[:, PAIR : 2 * PAIR] = v_ref[:, tok - PAIR :]
    up_ref[:, 2 * PAIR :] = jnp.concatenate(
        [q_ref[:, tok - BLOCK :], g_ref[:, tok - BLOCK :]], axis=1
    )


def by_head(x):
    width = x.shape[0]
    x = x * jnp.asarray(SCALE, BF16)
    columns = []
    for h in range(width // HEAD_DIM):
        rows = [x[h * HEAD_DIM : (h + 1) * HEAD_DIM]]
        if h:
            rows.insert(0, jnp.zeros((h * HEAD_DIM, x.shape[1]), BF16))
        if (h + 1) * HEAD_DIM < width:
            rows.append(jnp.zeros((width - (h + 1) * HEAD_DIM, x.shape[1]), BF16))
        columns.append(jnp.concatenate(rows, axis=0))
    return jnp.concatenate(columns, axis=1)


def own_head(x):
    return jnp.concatenate(
        [
            x[h * HEAD_DIM : (h + 1) * HEAD_DIM, h * PAIR : (h + 1) * PAIR]
            for h in range(x.shape[0] // HEAD_DIM)
        ],
        axis=0,
    )


def head_sums(x):
    return jnp.concatenate(
        [
            jnp.sum(x[h * HEAD_DIM : (h + 1) * HEAD_DIM], axis=0, keepdims=True)
            for h in range(x.shape[0] // HEAD_DIM)
        ],
        axis=1,
    )


def top_of(x):
    return jnp.max(x, axis=0, keepdims=True)


def total_of(x):
    return jnp.sum(x, axis=0, keepdims=True)


def second_half(lanes):
    return lax.broadcasted_iota(jnp.int32, (1, lanes), 1) % PAIR >= BLOCK


def global_scores(rows, qm):
    shape = (rows.shape[0], qm.shape[1])
    is_key = lax.broadcasted_iota(jnp.int32, shape, 0) % (2 * SUM_DEV) < SUM_DEV
    return jnp.where(is_key, mm(rows, qm), LOW)


def value_rows(rows):
    return pltpu.roll(rows.astype(F32), rows.shape[0] - SUM_DEV, 0).astype(BF16)


def rows_kernel(rows_ref, values_ref, values_t_ref, keys_t_ref):
    rows = rows_ref[...]
    values = value_rows(rows)
    values_ref[...] = values
    values_t_ref[...] = values.T
    keys_t_ref[...] = rows.T


def attention_kernel(
    q_ref, k_ref, v_ref, g_ref, before_ref, rows_ref, values_ref, values_t_ref,
    weight_ref, qx_ref, gx_ref, vx_ref, kt_ref, att_ref, part_ref, ds_ref, delta_ref,
    kx_ref, vt_ref,
):
    width, tok = q_ref.shape
    for at, t_ref, x_ref, own_ref in ((0, kt_ref, kx_ref, k_ref), (PAIR, vt_ref, vx_ref, v_ref)):
        t_ref[:, :PAIR] = before_ref[:, at : at + PAIR]
        t_ref[:, PAIR:] = own_ref[...]
        x_ref[:PAIR] = before_ref[:, at : at + PAIR].T
        x_ref[PAIR:] = own_ref[...].T
    for at, x_ref, own_ref in ((2 * PAIR, qx_ref, q_ref), (2 * PAIR + BLOCK, gx_ref, g_ref)):
        x_ref[...] = jnp.concatenate(
            [before_ref[:, at : at + BLOCK], own_ref[:, : tok - BLOCK]], axis=1
        )
    second = second_half(width // HEAD_DIM * PAIR)
    is_first = lax.axis_index("seq") == 0
    pairs = range(tok // PAIR)
    own = [slice(p * PAIR, (p + 1) * PAIR) for p in pairs]
    qm = [by_head(qx_ref[:, own[p]]) for p in pairs]
    local = []
    for p in pairs:
        s = mm(kx_ref[p * PAIR : (p + 2) * PAIR], qm[p])
        parts = [s[b * BLOCK : (b + 1) * BLOCK] for b in range(4)]
        parts[0] += jnp.where(second, LOW, 0.0)
        if p == 0:
            parts[1] += jnp.where(jnp.logical_and(is_first, second), LOW, 0.0)
            parts[2] += jnp.where(jnp.logical_and(is_first, jnp.logical_not(second)), LOW, 0.0)
        parts[3] += jnp.where(second, 0.0, LOW)
        local.append(jnp.concatenate(parts, axis=0))
    rows = rows_ref[...]
    s = global_scores(rows, jnp.concatenate(qm, axis=1))
    lanes = qm[0].shape[1]
    s = [s[:, p * lanes : (p + 1) * lanes] for p in pairs]
    values_g = values_ref[...]
    values_gt = values_t_ref[...]
    gm = [by_head(gx_ref[:, own[p]]) for p in pairs]
    top = [jnp.maximum(top_of(local[p]), top_of(s[p])) for p in pairs]
    local = [jnp.exp(local[p] - top[p]) for p in pairs]
    s = [jnp.exp(s[p] - top[p]) for p in pairs]
    inverse = [1.0 / (total_of(local[p]) + total_of(s[p])) for p in pairs]
    local = [local[p] * inverse[p] for p in pairs]
    w = [s[p] * inverse[p] for p in pairs]
    wb = [w[p].astype(BF16) for p in pairs]
    probs = [local[p].astype(BF16) for p in pairs]
    heads = range(width // HEAD_DIM)
    f = [slice(h * HEAD_DIM, (h + 1) * HEAD_DIM) for h in heads]
    c = [slice(h * PAIR, (h + 1) * PAIR) for h in heads]
    att = [
        jnp.concatenate(
            [
                mm(vt_ref[f[h], p * PAIR : (p + 2) * PAIR], probs[p][:, c[h]])
                + mm(values_gt[f[h]], wb[p][:, c[h]])
                for h in heads
            ],
            axis=0,
        ).astype(BF16)
        for p in pairs
    ]
    dprob = mm(values_g, jnp.concatenate(gm, axis=1))
    dprob = [dprob[:, p * lanes : (p + 1) * lanes] for p in pairs]
    part_v = mm_nt(jnp.concatenate(wb, axis=1), jnp.concatenate(gm, axis=1))
    delta = [
        head_sums(gx_ref[:, own[p]].astype(F32) * att[p].astype(F32)) * SCALE for p in pairs
    ]
    ds = [(w[p] * (dprob[p] - delta[p])).astype(BF16) for p in pairs]
    part_k = mm_nt(jnp.concatenate(ds, axis=1), jnp.concatenate(qm, axis=1))
    part_ref[...] = (part_k + pltpu.roll(part_v, SUM_DEV, 0)) * (1.0 / SCALE)
    for p in pairs:
        att_ref[:, own[p]] = att[p]
        ds_ref[p] = ds[p]
        weight_ref[p] = local[p]
        delta_ref[p] = delta[p]


def gradient_kernel(
    qx_ref, gx_ref, kt_ref, vx_ref, keys_gt_ref, weight_ref, att_ref, ds_ref, delta_ref,
    att_out_ref, qg_out_ref, kg_ref, vg_ref, back_ref,
):
    width, tok = kg_ref.shape
    pairs = tok // PAIR
    rows_t = keys_gt_ref[...]

    def pair(p):
        own = slice(p * PAIR, (p + 1) * PAIR)
        near = slice(p * PAIR, (p + 2) * PAIR)
        qm, gm = by_head(qx_ref[:, own]), by_head(gx_ref[:, own])
        w = weight_ref[p]
        ds = (w * (mm(vx_ref[near], gm) - delta_ref[p])).astype(BF16)
        qg = own_head(mm(kt_ref[:, near], ds) + mm(rows_t, ds_ref[p])).astype(BF16)
        kg = mm_nt(qm, ds) * (1.0 / SCALE)
        vg = mm_nt(gm, w.astype(BF16)) * (1.0 / SCALE)
        return qg, kg, vg

    grads = [pair(p) for p in range(pairs)]
    qg = jnp.concatenate([qg for qg, _, _ in grads], axis=1)
    att = att_ref[...]
    back_ref[:, 2 * PAIR :] = jnp.concatenate([att[:, :BLOCK], qg[:, :BLOCK]], axis=1)
    for x, ref in ((att, att_out_ref), (qg, qg_out_ref)):
        ref[...] = jnp.concatenate([x[:, BLOCK:], x[:, :BLOCK]], axis=1)
    for at, i, ref in ((0, 1, kg_ref), (PAIR, 2, vg_ref)):
        back_ref[:, at : at + PAIR] = grads[0][i][:, :PAIR].astype(BF16)
        for p in range(pairs - 1):
            ref[:, p * PAIR : (p + 1) * PAIR] = grads[p][i][:, PAIR:] + grads[p + 1][i][:, :PAIR]
        ref[:, tok - PAIR :] = grads[-1][i][:, PAIR:]


def outer(rows, weights):
    n = rows.shape[0]
    a, b = pieces(rows), pieces(weights)
    a = [a[i * n : (i + 1) * n] for i in (0, 0, 1, 0, 1, 2)]
    b = [b[i * n : (i + 1) * n] for i in (0, 1, 0, 2, 1, 0)]
    return mm_tn(jnp.concatenate(a, axis=0), jnp.concatenate(b, axis=0))


def owned_kernel(parts_ref, k_ref, v_ref, w_ref, term_ref, kp_ref, vp_ref):
    owned = jnp.sum(parts_ref[...], axis=0)
    split = pieces(owned)
    n = 2 * SUM_DEV
    seg = k_ref.shape[1] // SUM_DEV
    total = jnp.zeros((1, k_ref.shape[1]), F32)
    for first, ref in ((0, k_ref), (SUM_DEV, v_ref)):
        met = mm(split, ref[...])
        met = met[:n] + met[n : 2 * n] + met[2 * n :]
        met = jnp.where(segment_mask(first, met.shape[0], met.shape[1], seg), met, 0.0)
        total += jnp.sum(met, axis=0, keepdims=True)
    term = total[:, :seg]
    for j in range(1, SUM_DEV):
        term += total[:, j * seg : (j + 1) * seg]
    term_ref[...] = jnp.broadcast_to(term, term_ref.shape)
    tok = k_ref.shape[1]
    w = jnp.concatenate([w_ref[...]] * SUM_DEV, axis=1)
    w = jnp.broadcast_to(w, (n, tok))
    for first, ref in ((0, kp_ref), (SUM_DEV, vp_ref)):
        ref[...] = outer(owned, jnp.where(segment_mask(first, n, tok, seg), w, 0.0))


def sum_kernel(terms_ref, sum_ref):
    sum_ref[...] = jnp.sum(terms_ref[...], axis=0, keepdims=True)


def finish_kernel(
    kp_ref, vp_ref, kg_ref, vg_ref, back_ref, atts_ref, qgs_ref, pool_ref,
    key_out, value_out, att_out, qg_out, pool_out, key_ref, value_ref, att_ref, qg_ref, sem,
):
    copies = []

    def send(ref, out):
        copies.append(pltpu.make_async_copy(ref, out, sem.at[len(copies)]))
        copies[-1].start()

    tok = kg_ref.shape[1]
    low, high = slice(0, tok - PAIR), slice(tok - PAIR, tok)
    send(pool_ref, pool_out)
    for at, x_ref, ref, out in (
        (0, atts_ref, att_ref, att_out),
        (BLOCK, qgs_ref, qg_ref, qg_out),
    ):
        send(x_ref.at[:, low], out.at[:, low])
        edge = back_ref[:, 2 * PAIR + at : 2 * PAIR + at + BLOCK]
        ref[...] = jnp.concatenate([x_ref[:, tok - PAIR : tok - BLOCK], edge], axis=1)
        send(ref, out.at[:, high])
    for at, pooled_ref, grad_ref, ref, out in (
        (0, kp_ref, kg_ref, key_ref, key_out),
        (PAIR, vp_ref, vg_ref, value_ref, value_out),
    ):
        total = grad_ref[...] + pooled_ref[...]
        ref[:, low] = total[:, low].astype(BF16)
        ref[:, high] = (total[:, high] + back_ref[:, at : at + PAIR].astype(F32)).astype(BF16)
        send(ref, out)
    for copy in copies:
        copy.wait()


def shaped(shape, dtype):
    return jax.ShapeDtypeStruct(shape, dtype)


def call(kernel, outs, count, scratch=()):
    return pl.pallas_call(
        kernel,
        out_shape=outs,
        in_specs=[VMEM] * count,
        out_specs=[VMEM] * len(outs),
        scratch_shapes=list(scratch),
        compiler_params=PARAMS,
    )


def local(queries, key_states, value_states, pool_weight, out_grad):
    tok, width = queries.shape
    groups = lax.axis_size("seq")
    everyone = groups * lax.axis_size("head")
    n = 2 * SUM_DEV
    seg = pool_weight.shape[0]
    pairs, lanes = tok // PAIR, width // HEAD_DIM * PAIR
    halo = shaped((width, 3 * PAIR), BF16)
    own = shaped((width, tok), BF16)
    grad = shaped((width, tok), F32)
    keys = shaped((tok + PAIR, width), BF16)
    keys_t = shaped((width, tok + PAIR), BF16)
    stat = shaped((pairs, 1, lanes), F32)
    up = [(i, (i + 1) % groups) for i in range(groups)]
    down = [(j, i) for i, j in up]
    half = groups // 2
    order = [[*range(half, groups), *range(half)[::-1]]]

    def exchange(x):
        x = x.reshape(groups, n, width)
        return lax.all_to_all(x, "seq", split_axis=0, concat_axis=0, axis_index_groups=order)

    arguments = (queries.T, key_states.T, value_states.T, out_grad.T, pool_weight.reshape(1, seg))
    summary, edge, q, k, v, g, weight_row = pl.pallas_call(
        pool_kernel,
        out_shape=[shaped((groups, n, width), BF16), halo] + [own] * 4 + [shaped((1, seg), F32)],
        in_specs=[pl.BlockSpec(memory_space=pltpu.HBM)] * 5,
        out_specs=[VMEM] * 7,
        scratch_shapes=[pltpu.SemaphoreType.DMA((5,))],
        compiler_params=PARAMS,
    )(*[pltpu.with_memory_space_constraint(x, pltpu.HBM) for x in arguments])
    before = lax.ppermute(edge, "seq", up)
    rows = exchange(summary).reshape(groups * n, width)
    values_g, values_gt, keys_gt = call(
        rows_kernel,
        [shaped((groups * n, width), BF16)] + [shaped((width, groups * n), BF16)] * 2,
        1,
    )(rows)
    keys_gt, before = lax.optimization_barrier((keys_gt, before))
    w, qx, gx, vx, kt, att_x, part, ds, delta = call(
        attention_kernel,
        [shaped((pairs, 2 * PAIR, lanes), F32), own, own, keys, keys_t, own]
        + [shaped((groups * n, width), F32), shaped((pairs, groups * n, lanes), BF16), stat],
        8,
        [pltpu.VMEM(keys.shape, BF16), pltpu.VMEM(keys_t.shape, BF16)],
    )(q, k, v, g, before, rows, values_g, values_gt)
    parts = exchange(part)
    att_own, qg_own, key_part, value_part, edge = call(
        gradient_kernel, [own, own, grad, grad, halo], 9
    )(
        qx, gx, kt, vx, keys_gt, w, att_x, ds, delta
    )
    back = lax.ppermute(edge, "seq", down)
    parts, qg_own = lax.optimization_barrier((parts, qg_own))
    term, key_pooled, value_pooled = call(
        owned_kernel, [shaped((everyone, seg), F32), grad, grad], 4
    )(parts, k, v, weight_row)
    terms = lax.all_to_all(term, ("seq", "head"), split_axis=0, concat_axis=0)
    (pool_sum,) = call(sum_kernel, [shaped((1, seg), F32)], 1)(terms)
    key_grad, value_grad, attended, query_grad, pool_grad = pl.pallas_call(
        finish_kernel,
        out_shape=[own] * 4 + [shaped((1, seg), F32)],
        in_specs=[VMEM] * 8,
        out_specs=[pl.BlockSpec(memory_space=pltpu.HBM)] * 5,
        scratch_shapes=[pltpu.VMEM((width, tok), BF16)] * 2
        + [pltpu.VMEM((width, PAIR), BF16)] * 2
        + [pltpu.SemaphoreType.DMA((7,))],
        compiler_params=PARAMS,
    )(key_pooled, value_pooled, key_part, value_part, back, att_own, qg_own, pool_sum)
    return (attended.T, query_grad.T, key_grad.T, value_grad.T, pool_grad.reshape(seg))


def solution(mesh):
    return jax.shard_map(
        local,
        mesh=mesh,
        in_specs=(P("seq", "head"), P("seq", "head"), P("seq", "head"), P(), P("seq", "head")),
        out_specs=(P("seq", "head"), P("seq", "head"), P("seq", "head"), P("seq", "head"), P()),
        check_vma=False,
    )
```

```python
import functools

import jax
import jax.numpy as jnp
from jax import lax
from jax.experimental import pallas as pl
from jax.experimental.pallas import tpu as pltpu
from jax.sharding import PartitionSpec as P

HEAD_DIM = 64
BLOCK = 64
SUM_DEV = 4
PAIR = 2 * BLOCK
SCALE = HEAD_DIM ** (-0.5)
LOW = -1e30
VMEM = pl.BlockSpec(memory_space=pltpu.VMEM)
PARAMS = pltpu.CompilerParams(vmem_limit_bytes=40 * 1024 * 1024)
F32 = jnp.float32
BF16 = jnp.bfloat16


def mm(a, b):
    return lax.dot_general(a, b, (((1,), (0,)), ((), ())), preferred_element_type=F32)


def mm_nt(a, b):
    return lax.dot_general(a, b, (((1,), (1,)), ((), ())), preferred_element_type=F32)


def mm_tn(a, b):
    return lax.dot_general(a, b, (((0,), (0,)), ((), ())), preferred_element_type=F32)


def pieces(x):
    high = x.astype(BF16)
    rest = x - high.astype(F32)
    middle = rest.astype(BF16)
    low = (rest - middle.astype(F32)).astype(BF16)
    return jnp.concatenate([high, middle, low], axis=0)


def segment_mask(first, rows, lanes, seg):
    row = lax.broadcasted_iota(jnp.int32, (rows, lanes), 0)
    lane = lax.broadcasted_iota(jnp.int32, (rows, lanes), 1)
    return row - first == lane // seg


def pool_kernel(*refs):
    sources, (rows_ref, up_ref, *kept), sem = refs[:5], refs[5:12], refs[12]
    q_ref, k_ref, v_ref, g_ref, w_ref = kept
    copies = [
        pltpu.make_async_copy(source, target, sem.at[i])
        for i, (source, target) in enumerate(zip(sources, kept))
    ]
    for i in (4, 1, 2, 0, 3):
        copies[i].start()
    for i in (4, 1, 2):
        copies[i].wait()
    seg = w_ref.shape[1]
    n = 2 * SUM_DEV
    w = jnp.concatenate([w_ref[...]] * SUM_DEV, axis=1)
    w = jnp.broadcast_to(w, (n, w.shape[1]))
    pooled = jnp.zeros((n, k_ref.shape[0]), F32)
    for first, ref in ((0, k_ref), (SUM_DEV, v_ref)):
        weights = jnp.where(segment_mask(first, w.shape[0], w.shape[1], seg), w, 0.0)
        parts = mm_nt(pieces(weights), ref[...])
        pooled += parts[:n] + parts[n : 2 * n] + parts[2 * n :]
    rows_ref[...] = jnp.broadcast_to(pooled.astype(BF16)[None], rows_ref.shape)
    copies[0].wait()
    copies[3].wait()
    tok = k_ref.shape[1]
    up_ref[:, :PAIR] = k_ref[:, tok - PAIR :]
    up_ref[:, PAIR : 2 * PAIR] = v_ref[:, tok - PAIR :]
    up_ref[:, 2 * PAIR :] = jnp.concatenate(
        [q_ref[:, tok - BLOCK :], g_ref[:, tok - BLOCK :]], axis=1
    )


def by_head(x):
    width = x.shape[0]
    x = x * jnp.asarray(SCALE, BF16)
    columns = []
    for h in range(width // HEAD_DIM):
        rows = [x[h * HEAD_DIM : (h + 1) * HEAD_DIM]]
        if h:
            rows.insert(0, jnp.zeros((h * HEAD_DIM, x.shape[1]), BF16))
        if (h + 1) * HEAD_DIM < width:
            rows.append(jnp.zeros((width - (h + 1) * HEAD_DIM, x.shape[1]), BF16))
        columns.append(jnp.concatenate(rows, axis=0))
    return jnp.concatenate(columns, axis=1)


def own_head(x):
    return jnp.concatenate(
        [
            x[h * HEAD_DIM : (h + 1) * HEAD_DIM, h * PAIR : (h + 1) * PAIR]
            for h in range(x.shape[0] // HEAD_DIM)
        ],
        axis=0,
    )


def head_sums(x):
    return jnp.concatenate(
        [
            jnp.sum(x[h * HEAD_DIM : (h + 1) * HEAD_DIM], axis=0, keepdims=True)
            for h in range(x.shape[0] // HEAD_DIM)
        ],
        axis=1,
    )


def top_of(x):
    return jnp.max(x, axis=0, keepdims=True)


def total_of(x):
    return jnp.sum(x, axis=0, keepdims=True)


def second_half(lanes):
    return lax.broadcasted_iota(jnp.int32, (1, lanes), 1) % PAIR >= BLOCK


def global_scores(rows, qm):
    shape = (rows.shape[0], qm.shape[1])
    is_key = lax.broadcasted_iota(jnp.int32, shape, 0) % (2 * SUM_DEV) < SUM_DEV
    return jnp.where(is_key, mm(rows, qm), LOW)


def value_rows(rows):
    return pltpu.roll(rows.astype(F32), rows.shape[0] - SUM_DEV, 0).astype(BF16)


def rows_kernel(rows_ref, values_ref, values_t_ref, keys_t_ref):
    rows = rows_ref[...]
    values = value_rows(rows)
    values_ref[...] = values
    values_t_ref[...] = values.T
    keys_t_ref[...] = rows.T


def attention_kernel(
    q_ref, k_ref, v_ref, g_ref, before_ref, rows_ref, values_ref, values_t_ref,
    weight_ref, qx_ref, gx_ref, vx_ref, kt_ref, att_ref, part_ref, ds_ref, delta_ref,
    kx_ref, vt_ref,
):
    width, tok = q_ref.shape
    for at, x_ref, own_ref in ((2 * PAIR, qx_ref, q_ref), (2 * PAIR + BLOCK, gx_ref, g_ref)):
        x_ref[...] = jnp.concatenate(
            [before_ref[:, at : at + BLOCK], own_ref[:, : tok - BLOCK]], axis=1
        )
    pairs = range(tok // PAIR)
    own = [slice(p * PAIR, (p + 1) * PAIR) for p in pairs]
    qm = [by_head(qx_ref[:, own[p]]) for p in pairs]
    rows = rows_ref[...]
    s = global_scores(rows, jnp.concatenate(qm, axis=1))
    lanes = qm[0].shape[1]
    s = [s[:, p * lanes : (p + 1) * lanes] for p in pairs]
    values_g = values_ref[...]
    values_gt = values_t_ref[...]
    gm = [by_head(gx_ref[:, own[p]]) for p in pairs]
    for at, t_ref, x_ref, own_ref in ((0, kt_ref, kx_ref, k_ref), (PAIR, vt_ref, vx_ref, v_ref)):
        t_ref[:, :PAIR] = before_ref[:, at : at + PAIR]
        t_ref[:, PAIR:] = own_ref[...]
        x_ref[:PAIR] = before_ref[:, at : at + PAIR].T
        x_ref[PAIR:] = own_ref[...].T
    second = second_half(width // HEAD_DIM * PAIR)
    is_first = lax.axis_index("seq") == 0
    local = []
    for p in pairs:
        scores = mm(kx_ref[p * PAIR : (p + 2) * PAIR], qm[p])
        parts = [scores[b * BLOCK : (b + 1) * BLOCK] for b in range(4)]
        parts[0] += jnp.where(second, LOW, 0.0)
        if p == 0:
            parts[1] += jnp.where(jnp.logical_and(is_first, second), LOW, 0.0)
            parts[2] += jnp.where(jnp.logical_and(is_first, jnp.logical_not(second)), LOW, 0.0)
        parts[3] += jnp.where(second, 0.0, LOW)
        local.append(jnp.concatenate(parts, axis=0))
    top = [jnp.maximum(top_of(local[p]), top_of(s[p])) for p in pairs]
    local = [jnp.exp(local[p] - top[p]) for p in pairs]
    s = [jnp.exp(s[p] - top[p]) for p in pairs]
    inverse = [1.0 / (total_of(local[p]) + total_of(s[p])) for p in pairs]
    local = [local[p] * inverse[p] for p in pairs]
    w = [s[p] * inverse[p] for p in pairs]
    wb = [w[p].astype(BF16) for p in pairs]
    probs = [local[p].astype(BF16) for p in pairs]
    heads = range(width // HEAD_DIM)
    f = [slice(h * HEAD_DIM, (h + 1) * HEAD_DIM) for h in heads]
    c = [slice(h * PAIR, (h + 1) * PAIR) for h in heads]
    att = [
        jnp.concatenate(
            [
                mm(vt_ref[f[h], p * PAIR : (p + 2) * PAIR], probs[p][:, c[h]])
                + mm(values_gt[f[h]], wb[p][:, c[h]])
                for h in heads
            ],
            axis=0,
        ).astype(BF16)
        for p in pairs
    ]
    dprob = mm(values_g, jnp.concatenate(gm, axis=1))
    dprob = [dprob[:, p * lanes : (p + 1) * lanes] for p in pairs]
    part_v = mm_nt(jnp.concatenate(wb, axis=1), jnp.concatenate(gm, axis=1))
    delta = [
        head_sums(gx_ref[:, own[p]].astype(F32) * att[p].astype(F32)) * SCALE for p in pairs
    ]
    ds = [(w[p] * (dprob[p] - delta[p])).astype(BF16) for p in pairs]
    part_k = mm_nt(jnp.concatenate(ds, axis=1), jnp.concatenate(qm, axis=1))
    part_ref[...] = (part_k + pltpu.roll(part_v, SUM_DEV, 0)) * (1.0 / SCALE)
    for p in pairs:
        att_ref[:, own[p]] = att[p]
        ds_ref[p] = ds[p]
        weight_ref[p] = local[p]
        delta_ref[p] = delta[p]


def gradient_kernel(
    qx_ref, gx_ref, kt_ref, vx_ref, keys_gt_ref, weight_ref, att_ref, ds_ref, delta_ref,
    att_out_ref, qg_out_ref, kg_ref, vg_ref, back_ref,
):
    width, tok = kg_ref.shape
    pairs = tok // PAIR
    rows_t = keys_gt_ref[...]

    def pair(p):
        own = slice(p * PAIR, (p + 1) * PAIR)
        near = slice(p * PAIR, (p + 2) * PAIR)
        qm, gm = by_head(qx_ref[:, own]), by_head(gx_ref[:, own])
        w = weight_ref[p]
        ds = (w * (mm(vx_ref[near], gm) - delta_ref[p])).astype(BF16)
        qg = own_head(mm(kt_ref[:, near], ds) + mm(rows_t, ds_ref[p])).astype(BF16)
        kg = mm_nt(qm, ds) * (1.0 / SCALE)
        vg = mm_nt(gm, w.astype(BF16)) * (1.0 / SCALE)
        return qg, kg, vg

    grads = [pair(p) for p in range(pairs)]
    qg = jnp.concatenate([qg for qg, _, _ in grads], axis=1)
    att = att_ref[...]
    back_ref[:, 2 * PAIR :] = jnp.concatenate([att[:, :BLOCK], qg[:, :BLOCK]], axis=1)
    for x, ref in ((att, att_out_ref), (qg, qg_out_ref)):
        ref[...] = jnp.concatenate([x[:, BLOCK:], x[:, :BLOCK]], axis=1)
    for at, i, ref in ((0, 1, kg_ref), (PAIR, 2, vg_ref)):
        back_ref[:, at : at + PAIR] = grads[0][i][:, :PAIR].astype(BF16)
        for p in range(pairs - 1):
            ref[:, p * PAIR : (p + 1) * PAIR] = grads[p][i][:, PAIR:] + grads[p + 1][i][:, :PAIR]
        ref[:, tok - PAIR :] = grads[-1][i][:, PAIR:]


def outer(rows, weights):
    n = rows.shape[0]
    a, b = pieces(rows), pieces(weights)
    a = [a[i * n : (i + 1) * n] for i in (0, 0, 1, 0, 1, 2)]
    b = [b[i * n : (i + 1) * n] for i in (0, 1, 0, 2, 1, 0)]
    return mm_tn(jnp.concatenate(a, axis=0), jnp.concatenate(b, axis=0))


def owned_kernel(parts_ref, k_ref, v_ref, w_ref, term_ref, kp_ref, vp_ref):
    owned = jnp.sum(parts_ref[...], axis=0)
    split = pieces(owned)
    n = 2 * SUM_DEV
    seg = k_ref.shape[1] // SUM_DEV
    total = jnp.zeros((1, k_ref.shape[1]), F32)
    for first, ref in ((0, k_ref), (SUM_DEV, v_ref)):
        met = mm(split, ref[...])
        met = met[:n] + met[n : 2 * n] + met[2 * n :]
        met = jnp.where(segment_mask(first, met.shape[0], met.shape[1], seg), met, 0.0)
        total += jnp.sum(met, axis=0, keepdims=True)
    term = total[:, :seg]
    for j in range(1, SUM_DEV):
        term += total[:, j * seg : (j + 1) * seg]
    term_ref[...] = jnp.broadcast_to(term, term_ref.shape)
    tok = k_ref.shape[1]
    w = jnp.concatenate([w_ref[...]] * SUM_DEV, axis=1)
    w = jnp.broadcast_to(w, (n, tok))
    for first, ref in ((0, kp_ref), (SUM_DEV, vp_ref)):
        ref[...] = outer(owned, jnp.where(segment_mask(first, n, tok, seg), w, 0.0))


def sum_kernel(terms_ref, sum_ref):
    sum_ref[...] = jnp.sum(terms_ref[...], axis=0, keepdims=True)


def finish_kernel(
    kp_ref, vp_ref, kg_ref, vg_ref, back_ref, atts_ref, qgs_ref, pool_ref,
    key_out, value_out, att_out, qg_out, pool_out, key_ref, value_ref, att_ref, qg_ref, sem,
):
    copies = []

    def send(ref, out):
        copies.append(pltpu.make_async_copy(ref, out, sem.at[len(copies)]))
        copies[-1].start()

    tok = kg_ref.shape[1]
    low, high = slice(0, tok - PAIR), slice(tok - PAIR, tok)
    send(pool_ref, pool_out)
    for at, x_ref, ref, out in (
        (0, atts_ref, att_ref, att_out),
        (BLOCK, qgs_ref, qg_ref, qg_out),
    ):
        send(x_ref.at[:, low], out.at[:, low])
        edge = back_ref[:, 2 * PAIR + at : 2 * PAIR + at + BLOCK]
        ref[...] = jnp.concatenate([x_ref[:, tok - PAIR : tok - BLOCK], edge], axis=1)
        send(ref, out.at[:, high])
    for at, pooled_ref, grad_ref, ref, out in (
        (0, kp_ref, kg_ref, key_ref, key_out),
        (PAIR, vp_ref, vg_ref, value_ref, value_out),
    ):
        total = grad_ref[...] + pooled_ref[...]
        ref[:, low] = total[:, low].astype(BF16)
        ref[:, high] = (total[:, high] + back_ref[:, at : at + PAIR].astype(F32)).astype(BF16)
        send(ref, out)
    for copy in copies:
        copy.wait()


def shaped(shape, dtype):
    return jax.ShapeDtypeStruct(shape, dtype)


def call(kernel, outs, count, scratch=()):
    return pl.pallas_call(
        kernel,
        out_shape=outs,
        in_specs=[VMEM] * count,
        out_specs=[VMEM] * len(outs),
        scratch_shapes=list(scratch),
        compiler_params=PARAMS,
    )


def local(queries, key_states, value_states, pool_weight, out_grad):
    tok, width = queries.shape
    groups = lax.axis_size("seq")
    everyone = groups * lax.axis_size("head")
    n = 2 * SUM_DEV
    seg = pool_weight.shape[0]
    pairs, lanes = tok // PAIR, width // HEAD_DIM * PAIR
    halo = shaped((width, 3 * PAIR), BF16)
    own = shaped((width, tok), BF16)
    grad = shaped((width, tok), F32)
    keys = shaped((tok + PAIR, width), BF16)
    keys_t = shaped((width, tok + PAIR), BF16)
    stat = shaped((pairs, 1, lanes), F32)
    up = [(i, (i + 1) % groups) for i in range(groups)]
    down = [(j, i) for i, j in up]
    half = groups // 2
    order = [[*range(half, groups), *range(half)[::-1]]]

    def exchange(x):
        x = x.reshape(groups, n, width)
        return lax.all_to_all(x, "seq", split_axis=0, concat_axis=0, axis_index_groups=order)

    arguments = (queries.T, key_states.T, value_states.T, out_grad.T, pool_weight.reshape(1, seg))
    summary, edge, q, k, v, g, weight_row = pl.pallas_call(
        pool_kernel,
        out_shape=[shaped((groups, n, width), BF16), halo] + [own] * 4 + [shaped((1, seg), F32)],
        in_specs=[pl.BlockSpec(memory_space=pltpu.HBM)] * 5,
        out_specs=[VMEM] * 7,
        scratch_shapes=[pltpu.SemaphoreType.DMA((5,))],
        compiler_params=PARAMS,
    )(*[pltpu.with_memory_space_constraint(x, pltpu.HBM) for x in arguments])
    before = lax.ppermute(edge, "seq", up)
    rows = exchange(summary).reshape(groups * n, width)
    values_g, values_gt, keys_gt = call(
        rows_kernel,
        [shaped((groups * n, width), BF16)] + [shaped((width, groups * n), BF16)] * 2,
        1,
    )(rows)
    keys_gt, before = lax.optimization_barrier((keys_gt, before))
    w, qx, gx, vx, kt, att_x, part, ds, delta = call(
        attention_kernel,
        [shaped((pairs, 2 * PAIR, lanes), F32), own, own, keys, keys_t, own]
        + [shaped((groups * n, width), F32), shaped((pairs, groups * n, lanes), BF16), stat],
        8,
        [pltpu.VMEM(keys.shape, BF16), pltpu.VMEM(keys_t.shape, BF16)],
    )(q, k, v, g, before, rows, values_g, values_gt)
    parts = exchange(part)
    att_own, qg_own, key_part, value_part, edge = call(
        gradient_kernel, [own, own, grad, grad, halo], 9
    )(
        qx, gx, kt, vx, keys_gt, w, att_x, ds, delta
    )
    back = lax.ppermute(edge, "seq", down)
    parts, qg_own = lax.optimization_barrier((parts, qg_own))
    term, key_pooled, value_pooled = call(
        owned_kernel, [shaped((everyone, seg), F32), grad, grad], 4
    )(parts, k, v, weight_row)
    terms = lax.all_to_all(term, ("seq", "head"), split_axis=0, concat_axis=0)
    (pool_sum,) = call(sum_kernel, [shaped((1, seg), F32)], 1)(terms)
    key_grad, value_grad, attended, query_grad, pool_grad = pl.pallas_call(
        finish_kernel,
        out_shape=[own] * 4 + [shaped((1, seg), F32)],
        in_specs=[VMEM] * 8,
        out_specs=[pl.BlockSpec(memory_space=pltpu.HBM)] * 5,
        scratch_shapes=[pltpu.VMEM((width, tok), BF16)] * 2
        + [pltpu.VMEM((width, PAIR), BF16)] * 2
        + [pltpu.SemaphoreType.DMA((7,))],
        compiler_params=PARAMS,
    )(key_pooled, value_pooled, key_part, value_part, back, att_own, qg_own, pool_sum)
    return (attended.T, query_grad.T, key_grad.T, value_grad.T, pool_grad.reshape(seg))


def solution(mesh):
    return jax.shard_map(
        local,
        mesh=mesh,
        in_specs=(P("seq", "head"), P("seq", "head"), P("seq", "head"), P(), P("seq", "head")),
        out_specs=(P("seq", "head"), P("seq", "head"), P("seq", "head"), P("seq", "head"), P()),
        check_vma=False,
    )
```

```python
import functools

import jax
import jax.numpy as jnp
from jax import lax
from jax.experimental import pallas as pl
from jax.experimental.pallas import tpu as pltpu
from jax.sharding import PartitionSpec as P

HEAD_DIM = 64
BLOCK = 64
SUM_DEV = 4
PAIR = 2 * BLOCK
SCALE = HEAD_DIM ** (-0.5)
LOW = -1e30
VMEM = pl.BlockSpec(memory_space=pltpu.VMEM)
PARAMS = pltpu.CompilerParams(vmem_limit_bytes=40 * 1024 * 1024)
F32 = jnp.float32
BF16 = jnp.bfloat16


def mm(a, b):
    return lax.dot_general(a, b, (((1,), (0,)), ((), ())), preferred_element_type=F32)


def mm_nt(a, b):
    return lax.dot_general(a, b, (((1,), (1,)), ((), ())), preferred_element_type=F32)


def mm_tn(a, b):
    return lax.dot_general(a, b, (((0,), (0,)), ((), ())), preferred_element_type=F32)


def pieces(x):
    high = x.astype(BF16)
    rest = x - high.astype(F32)
    middle = rest.astype(BF16)
    low = (rest - middle.astype(F32)).astype(BF16)
    return jnp.concatenate([high, middle, low], axis=0)


def segment_mask(first, rows, lanes, seg):
    row = lax.broadcasted_iota(jnp.int32, (rows, lanes), 0)
    lane = lax.broadcasted_iota(jnp.int32, (rows, lanes), 1)
    return row - first == lane // seg


def pool_kernel(*refs):
    sources, (rows_ref, up_ref, *kept), sem = refs[:5], refs[5:12], refs[12]
    q_ref, k_ref, v_ref, g_ref, w_ref = kept
    copies = [
        pltpu.make_async_copy(source, target, sem.at[i])
        for i, (source, target) in enumerate(zip(sources, kept))
    ]
    for i in (4, 1, 2, 0, 3):
        copies[i].start()
    copies[4].wait()
    seg = w_ref.shape[1]
    n = 2 * SUM_DEV
    w = jnp.concatenate([w_ref[...]] * SUM_DEV, axis=1)
    w = jnp.broadcast_to(w, (n, w.shape[1]))
    weights = [
        pieces(jnp.where(segment_mask(first, n, w.shape[1], seg), w, 0.0)) for first in (0, SUM_DEV)
    ]
    copies[1].wait()
    copies[2].wait()
    pooled = mm_nt(weights[0], k_ref[...]) + mm_nt(weights[1], v_ref[...])
    pooled = pooled[:n] + pooled[n : 2 * n] + pooled[2 * n :]
    rows_ref[...] = jnp.broadcast_to(pooled.astype(BF16)[None], rows_ref.shape)
    copies[0].wait()
    copies[3].wait()
    tok = k_ref.shape[1]
    up_ref[:, :PAIR] = k_ref[:, tok - PAIR :]
    up_ref[:, PAIR : 2 * PAIR] = v_ref[:, tok - PAIR :]
    up_ref[:, 2 * PAIR :] = jnp.concatenate(
        [q_ref[:, tok - BLOCK :], g_ref[:, tok - BLOCK :]], axis=1
    )


def by_head(x):
    width = x.shape[0]
    x = x * jnp.asarray(SCALE, BF16)
    columns = []
    for h in range(width // HEAD_DIM):
        rows = [x[h * HEAD_DIM : (h + 1) * HEAD_DIM]]
        if h:
            rows.insert(0, jnp.zeros((h * HEAD_DIM, x.shape[1]), BF16))
        if (h + 1) * HEAD_DIM < width:
            rows.append(jnp.zeros((width - (h + 1) * HEAD_DIM, x.shape[1]), BF16))
        columns.append(jnp.concatenate(rows, axis=0))
    return jnp.concatenate(columns, axis=1)


def own_head(x):
    return jnp.concatenate(
        [
            x[h * HEAD_DIM : (h + 1) * HEAD_DIM, h * PAIR : (h + 1) * PAIR]
            for h in range(x.shape[0] // HEAD_DIM)
        ],
        axis=0,
    )


def head_sums(x):
    return jnp.concatenate(
        [
            jnp.sum(x[h * HEAD_DIM : (h + 1) * HEAD_DIM], axis=0, keepdims=True)
            for h in range(x.shape[0] // HEAD_DIM)
        ],
        axis=1,
    )


def top_of(x):
    return jnp.max(x, axis=0, keepdims=True)


def total_of(x):
    return jnp.sum(x, axis=0, keepdims=True)


def second_half(lanes):
    return lax.broadcasted_iota(jnp.int32, (1, lanes), 1) % PAIR >= BLOCK


def global_scores(rows, qm):
    shape = (rows.shape[0], qm.shape[1])
    is_key = lax.broadcasted_iota(jnp.int32, shape, 0) % (2 * SUM_DEV) < SUM_DEV
    return jnp.where(is_key, mm(rows, qm), LOW)


def value_rows(rows):
    return pltpu.roll(rows.astype(F32), rows.shape[0] - SUM_DEV, 0).astype(BF16)


def rows_kernel(rows_ref, values_ref, values_t_ref, keys_t_ref):
    rows = rows_ref[...]
    values = value_rows(rows)
    values_ref[...] = values
    values_t_ref[...] = values.T
    keys_t_ref[...] = rows.T


def attention_kernel(
    q_ref, k_ref, v_ref, g_ref, before_ref, rows_ref, values_ref, values_t_ref,
    weight_ref, qx_ref, gx_ref, vx_ref, kt_ref, att_ref, part_ref, ds_ref, delta_ref,
    kx_ref, vt_ref,
):
    width, tok = q_ref.shape
    for at, x_ref, own_ref in ((2 * PAIR, qx_ref, q_ref), (2 * PAIR + BLOCK, gx_ref, g_ref)):
        x_ref[...] = jnp.concatenate(
            [before_ref[:, at : at + BLOCK], own_ref[:, : tok - BLOCK]], axis=1
        )
    pairs = range(tok // PAIR)
    own = [slice(p * PAIR, (p + 1) * PAIR) for p in pairs]
    qm = [by_head(qx_ref[:, own[p]]) for p in pairs]
    rows = rows_ref[...]
    s = global_scores(rows, jnp.concatenate(qm, axis=1))
    lanes = qm[0].shape[1]
    s = [s[:, p * lanes : (p + 1) * lanes] for p in pairs]
    values_g = values_ref[...]
    values_gt = values_t_ref[...]
    gm = [by_head(gx_ref[:, own[p]]) for p in pairs]
    for at, t_ref, x_ref, own_ref in ((0, kt_ref, kx_ref, k_ref), (PAIR, vt_ref, vx_ref, v_ref)):
        t_ref[:, :PAIR] = before_ref[:, at : at + PAIR]
        t_ref[:, PAIR:] = own_ref[...]
        x_ref[:PAIR] = before_ref[:, at : at + PAIR].T
        x_ref[PAIR:] = own_ref[...].T
    second = second_half(width // HEAD_DIM * PAIR)
    is_first = lax.axis_index("seq") == 0
    local = []
    for p in pairs:
        scores = mm(kx_ref[p * PAIR : (p + 2) * PAIR], qm[p])
        parts = [scores[b * BLOCK : (b + 1) * BLOCK] for b in range(4)]
        parts[0] += jnp.where(second, LOW, 0.0)
        if p == 0:
            parts[1] += jnp.where(jnp.logical_and(is_first, second), LOW, 0.0)
            parts[2] += jnp.where(jnp.logical_and(is_first, jnp.logical_not(second)), LOW, 0.0)
        parts[3] += jnp.where(second, 0.0, LOW)
        local.append(jnp.concatenate(parts, axis=0))
    top = [jnp.maximum(top_of(local[p]), top_of(s[p])) for p in pairs]
    local = [jnp.exp(local[p] - top[p]) for p in pairs]
    s = [jnp.exp(s[p] - top[p]) for p in pairs]
    inverse = [1.0 / (total_of(local[p]) + total_of(s[p])) for p in pairs]
    local = [local[p] * inverse[p] for p in pairs]
    w = [s[p] * inverse[p] for p in pairs]
    wb = [w[p].astype(BF16) for p in pairs]
    probs = [local[p].astype(BF16) for p in pairs]
    heads = range(width // HEAD_DIM)
    f = [slice(h * HEAD_DIM, (h + 1) * HEAD_DIM) for h in heads]
    c = [slice(h * PAIR, (h + 1) * PAIR) for h in heads]
    att = [
        jnp.concatenate(
            [
                mm(vt_ref[f[h], p * PAIR : (p + 2) * PAIR], probs[p][:, c[h]])
                + mm(values_gt[f[h]], wb[p][:, c[h]])
                for h in heads
            ],
            axis=0,
        ).astype(BF16)
        for p in pairs
    ]
    dprob = mm(values_g, jnp.concatenate(gm, axis=1))
    dprob = [dprob[:, p * lanes : (p + 1) * lanes] for p in pairs]
    part_v = mm_nt(jnp.concatenate(wb, axis=1), jnp.concatenate(gm, axis=1))
    delta = [
        head_sums(gx_ref[:, own[p]].astype(F32) * att[p].astype(F32)) * SCALE for p in pairs
    ]
    ds = [(w[p] * (dprob[p] - delta[p])).astype(BF16) for p in pairs]
    part_k = mm_nt(jnp.concatenate(ds, axis=1), jnp.concatenate(qm, axis=1))
    part_ref[...] = (part_k + pltpu.roll(part_v, SUM_DEV, 0)) * (1.0 / SCALE)
    for p in pairs:
        att_ref[:, own[p]] = att[p]
        ds_ref[p] = ds[p]
        weight_ref[p] = local[p]
        delta_ref[p] = delta[p]


def gradient_kernel(
    qx_ref, gx_ref, kt_ref, vx_ref, keys_gt_ref, weight_ref, att_ref, ds_ref, delta_ref,
    att_out_ref, qg_out_ref, kg_ref, vg_ref, back_ref,
):
    width, tok = kg_ref.shape
    pairs = tok // PAIR
    rows_t = keys_gt_ref[...]

    def pair(p):
        own = slice(p * PAIR, (p + 1) * PAIR)
        near = slice(p * PAIR, (p + 2) * PAIR)
        qm, gm = by_head(qx_ref[:, own]), by_head(gx_ref[:, own])
        w = weight_ref[p]
        ds = (w * (mm(vx_ref[near], gm) - delta_ref[p])).astype(BF16)
        qg = own_head(mm(kt_ref[:, near], ds) + mm(rows_t, ds_ref[p])).astype(BF16)
        kg = mm_nt(qm, ds) * (1.0 / SCALE)
        vg = mm_nt(gm, w.astype(BF16)) * (1.0 / SCALE)
        return qg, kg, vg

    grads = [pair(p) for p in range(pairs)]
    qg = jnp.concatenate([qg for qg, _, _ in grads], axis=1)
    att = att_ref[...]
    back_ref[:, 2 * PAIR :] = jnp.concatenate([att[:, :BLOCK], qg[:, :BLOCK]], axis=1)
    for x, ref in ((att, att_out_ref), (qg, qg_out_ref)):
        ref[...] = jnp.concatenate([x[:, BLOCK:], x[:, :BLOCK]], axis=1)
    for at, i, ref in ((0, 1, kg_ref), (PAIR, 2, vg_ref)):
        back_ref[:, at : at + PAIR] = grads[0][i][:, :PAIR].astype(BF16)
        for p in range(pairs - 1):
            ref[:, p * PAIR : (p + 1) * PAIR] = grads[p][i][:, PAIR:] + grads[p + 1][i][:, :PAIR]
        ref[:, tok - PAIR :] = grads[-1][i][:, PAIR:]


def outer(rows, weights):
    n = rows.shape[0]
    a, b = pieces(rows), pieces(weights)
    a = [a[i * n : (i + 1) * n] for i in (0, 0, 1, 0, 1, 2)]
    b = [b[i * n : (i + 1) * n] for i in (0, 1, 0, 2, 1, 0)]
    return mm_tn(jnp.concatenate(a, axis=0), jnp.concatenate(b, axis=0))


def owned_kernel(parts_ref, k_ref, v_ref, w_ref, term_ref, kp_ref, vp_ref):
    owned = jnp.sum(parts_ref[...], axis=0)
    split = pieces(owned)
    n = 2 * SUM_DEV
    seg = k_ref.shape[1] // SUM_DEV
    total = jnp.zeros((1, k_ref.shape[1]), F32)
    for first, ref in ((0, k_ref), (SUM_DEV, v_ref)):
        met = mm(split, ref[...])
        met = met[:n] + met[n : 2 * n] + met[2 * n :]
        met = jnp.where(segment_mask(first, met.shape[0], met.shape[1], seg), met, 0.0)
        total += jnp.sum(met, axis=0, keepdims=True)
    term = total[:, :seg]
    for j in range(1, SUM_DEV):
        term += total[:, j * seg : (j + 1) * seg]
    term_ref[...] = jnp.broadcast_to(term, term_ref.shape)
    tok = k_ref.shape[1]
    w = jnp.concatenate([w_ref[...]] * SUM_DEV, axis=1)
    w = jnp.broadcast_to(w, (n, tok))
    for first, ref in ((0, kp_ref), (SUM_DEV, vp_ref)):
        ref[...] = outer(owned, jnp.where(segment_mask(first, n, tok, seg), w, 0.0))


def sum_kernel(terms_ref, sum_ref):
    sum_ref[...] = jnp.sum(terms_ref[...], axis=0, keepdims=True)


def finish_kernel(
    kp_ref, vp_ref, kg_ref, vg_ref, back_ref, atts_ref, qgs_ref, pool_ref,
    key_out, value_out, att_out, qg_out, pool_out, key_ref, value_ref, att_ref, qg_ref, sem,
):
    copies = []

    def send(ref, out):
        copies.append(pltpu.make_async_copy(ref, out, sem.at[len(copies)]))
        copies[-1].start()

    tok = kg_ref.shape[1]
    low, high = slice(0, tok - PAIR), slice(tok - PAIR, tok)
    send(pool_ref, pool_out)
    for at, x_ref, ref, out in (
        (0, atts_ref, att_ref, att_out),
        (BLOCK, qgs_ref, qg_ref, qg_out),
    ):
        send(x_ref.at[:, low], out.at[:, low])
        edge = back_ref[:, 2 * PAIR + at : 2 * PAIR + at + BLOCK]
        ref[...] = jnp.concatenate([x_ref[:, tok - PAIR : tok - BLOCK], edge], axis=1)
        send(ref, out.at[:, high])
    for at, pooled_ref, grad_ref, ref, out in (
        (0, kp_ref, kg_ref, key_ref, key_out),
        (PAIR, vp_ref, vg_ref, value_ref, value_out),
    ):
        total = grad_ref[...] + pooled_ref[...]
        ref[:, low] = total[:, low].astype(BF16)
        ref[:, high] = (total[:, high] + back_ref[:, at : at + PAIR].astype(F32)).astype(BF16)
        send(ref, out)
    for copy in copies:
        copy.wait()


def shaped(shape, dtype):
    return jax.ShapeDtypeStruct(shape, dtype)


def call(kernel, outs, count, scratch=()):
    return pl.pallas_call(
        kernel,
        out_shape=outs,
        in_specs=[VMEM] * count,
        out_specs=[VMEM] * len(outs),
        scratch_shapes=list(scratch),
        compiler_params=PARAMS,
    )


def local(queries, key_states, value_states, pool_weight, out_grad):
    tok, width = queries.shape
    groups = lax.axis_size("seq")
    everyone = groups * lax.axis_size("head")
    n = 2 * SUM_DEV
    seg = pool_weight.shape[0]
    pairs, lanes = tok // PAIR, width // HEAD_DIM * PAIR
    halo = shaped((width, 3 * PAIR), BF16)
    own = shaped((width, tok), BF16)
    grad = shaped((width, tok), F32)
    keys = shaped((tok + PAIR, width), BF16)
    keys_t = shaped((width, tok + PAIR), BF16)
    stat = shaped((pairs, 1, lanes), F32)
    up = [(i, (i + 1) % groups) for i in range(groups)]
    down = [(j, i) for i, j in up]
    half = groups // 2
    order = [[*range(half, groups), *range(half)[::-1]]]

    def exchange(x):
        x = x.reshape(groups, n, width)
        return lax.all_to_all(x, "seq", split_axis=0, concat_axis=0, axis_index_groups=order)

    arguments = (queries.T, key_states.T, value_states.T, out_grad.T, pool_weight.reshape(1, seg))
    summary, edge, q, k, v, g, weight_row = pl.pallas_call(
        pool_kernel,
        out_shape=[shaped((groups, n, width), BF16), halo] + [own] * 4 + [shaped((1, seg), F32)],
        in_specs=[pl.BlockSpec(memory_space=pltpu.HBM)] * 5,
        out_specs=[VMEM] * 7,
        scratch_shapes=[pltpu.SemaphoreType.DMA((5,))],
        compiler_params=PARAMS,
    )(*[pltpu.with_memory_space_constraint(x, pltpu.HBM) for x in arguments])
    before = lax.ppermute(edge, "seq", up)
    rows = exchange(summary).reshape(groups * n, width)
    values_g, values_gt, keys_gt = call(
        rows_kernel,
        [shaped((groups * n, width), BF16)] + [shaped((width, groups * n), BF16)] * 2,
        1,
    )(rows)
    keys_gt, before = lax.optimization_barrier((keys_gt, before))
    w, qx, gx, vx, kt, att_x, part, ds, delta = call(
        attention_kernel,
        [shaped((pairs, 2 * PAIR, lanes), F32), own, own, keys, keys_t, own]
        + [shaped((groups * n, width), F32), shaped((pairs, groups * n, lanes), BF16), stat],
        8,
        [pltpu.VMEM(keys.shape, BF16), pltpu.VMEM(keys_t.shape, BF16)],
    )(q, k, v, g, before, rows, values_g, values_gt)
    parts = exchange(part)
    att_own, qg_own, key_part, value_part, edge = call(
        gradient_kernel, [own, own, grad, grad, halo], 9
    )(
        qx, gx, kt, vx, keys_gt, w, att_x, ds, delta
    )
    back = lax.ppermute(edge, "seq", down)
    parts, qg_own = lax.optimization_barrier((parts, qg_own))
    term, key_pooled, value_pooled = call(
        owned_kernel, [shaped((everyone, seg), F32), grad, grad], 4
    )(parts, k, v, weight_row)
    terms = lax.all_to_all(term, ("seq", "head"), split_axis=0, concat_axis=0)
    (pool_sum,) = call(sum_kernel, [shaped((1, seg), F32)], 1)(terms)
    key_grad, value_grad, attended, query_grad, pool_grad = pl.pallas_call(
        finish_kernel,
        out_shape=[own] * 4 + [shaped((1, seg), F32)],
        in_specs=[VMEM] * 8,
        out_specs=[pl.BlockSpec(memory_space=pltpu.HBM)] * 5,
        scratch_shapes=[pltpu.VMEM((width, tok), BF16)] * 2
        + [pltpu.VMEM((width, PAIR), BF16)] * 2
        + [pltpu.SemaphoreType.DMA((7,))],
        compiler_params=PARAMS,
    )(key_pooled, value_pooled, key_part, value_part, back, att_own, qg_own, pool_sum)
    return (attended.T, query_grad.T, key_grad.T, value_grad.T, pool_grad.reshape(seg))


def solution(mesh):
    return jax.shard_map(
        local,
        mesh=mesh,
        in_specs=(P("seq", "head"), P("seq", "head"), P("seq", "head"), P(), P("seq", "head")),
        out_specs=(P("seq", "head"), P("seq", "head"), P("seq", "head"), P("seq", "head"), P()),
        check_vma=False,
    )
```
